32 devices in a mesh: ctx: 8 (over y, x, core), head: 4 (over z).
Axes of the slice: x: 2, y: 2, z: 4, core: 2. Of those that a mesh axis runs over, the one named last changes fastest.
Arguments:
- queries: float32 [4096, 8192], P('ctx', 'head'), as said below
- keys: float32 [4096, 8192], P('ctx', 'head')
- values: float32 [4096, 8192], P('ctx', 'head')
- head_gain: float32 [2, 64], P(None, 'head'), may hold values from 0.3 to 3
Outputs:
- mixed: float32 [4096, 8192], P('ctx', 'head')
The draws below stay inside these ranges and needn't reach their ends.
Inputs may be any that keep to these rules, and one draw needn't show every extreme that they name: queries, keys and values are finite real numbers.
All inputs are finite; a program needn't handle non-finite values.
Results may differ from the reference program's by a relative error of at most 0.0003.
Values sent between devices are 32-bit elements; how exact they have to be, the bound alone decides.
No kernel may reach another device: no remote copies, remote signals or barrier semaphores. Data moves between devices by JAX's collectives and lax.ppermute only.
A program may use at most 128 MiB of HBM per device.

```python
import math
import jax
import jax.numpy as jnp
from jax import lax

HEADS = 64
HD = 128
WINDOW = 128
TOKENS = 4096


def paired_draw(key):
    columns = HEADS * HD
    query_part = jnp.clip(jax.random.normal(jax.random.fold_in(key, 101), (TOKENS, columns), jnp.float32), -6.0, 6.0)
    key_part = jnp.clip(jax.random.normal(jax.random.fold_in(key, 102), (TOKENS, columns), jnp.float32), -6.0, 6.0)
    return (query_part, key_part)


def draw_queries(key, part):
    return paired_draw(key)[0]


def draw_keys(key, part):
    return paired_draw(key)[1]


def draw_values(key, part):
    columns = HEADS * HD
    base_values = jnp.clip(jax.random.normal(jax.random.fold_in(key, 201), (TOKENS, columns), jnp.float32), -6.0, 6.0)
    return base_values


def shard_levels(rng, dims, shards, smallest, high):
    loudness = 1.0
    for position, parts in shards:
        draws = jax.random.uniform(jax.random.fold_in(jax.random.fold_in(rng, 6), position), (parts,), jnp.float32, smallest / len(shards), high / len(shards))
        loudness = loudness * jnp.repeat(jnp.exp(draws), dims[position] // parts).reshape((-1,) + (1,) * (len(dims) - 1 - position))
    return loudness


def setup_inputs(seed: int = 0) -> dict:
    key_of = jax.random.split(jax.random.key(seed), 5)
    return {
        "queries": draw_queries(jax.random.fold_in(key_of[4], 71), 0),
        "keys": draw_keys(jax.random.fold_in(key_of[4], 71), 0),
        "values": draw_values(jax.random.fold_in(key_of[4], 71), 0),
        "head_gain": jnp.clip(jnp.exp(math.log(3.0) - 2.3025851 * jax.random.uniform(key_of[3], (2, HEADS), jnp.float32) ** shard_levels(key_of[3], (2, HEADS), ((1, 4),), -0.2, 0.2)), 0.3, 3.0),
    }


def reference(queries, keys, values, head_gain):
    factor = 1.0 / math.sqrt(HD)
    nblocks = TOKENS // WINDOW
    highest = lax.Precision.HIGHEST

    def blocked(matrix):
        return matrix.reshape(nblocks, WINDOW, HEADS, HD).transpose(0, 2, 1, 3)
    query_blocks = blocked(queries)
    key_blocks = blocked(keys)
    value_blocks = blocked(values)
    empty_block = jnp.zeros((1, HEADS, WINDOW, HD), jnp.float32)
    key_before = jnp.concatenate([empty_block, key_blocks[:-1]], axis=0)
    value_before = jnp.concatenate([empty_block, value_blocks[:-1]], axis=0)
    offsets = jnp.arange(WINDOW)
    causal = offsets[:, None] >= offsets[None, :]

    def advance(state, inputs):
        number, query_now, key_now, value_now, key_prev, value_prev = inputs
        key_both = jnp.concatenate([key_prev, key_now], axis=1)
        value_both = jnp.concatenate([value_prev, value_now], axis=1)
        scores = jnp.einsum('hqd,hkd->hqk', query_now, key_both, precision=highest) * factor
        query_pos = number * WINDOW + offsets
        key_pos = (number - 1) * WINDOW + jnp.arange(2 * WINDOW)
        spacing = query_pos[:, None] - key_pos[None, :]
        allowed = (spacing >= 0) & (spacing < WINDOW) & (key_pos >= 0)[None, :]
        scores = jnp.where(allowed[None], scores, -jnp.inf)
        biggest = lax.optimization_barrier(jnp.max(scores, axis=-1, keepdims=True))
        weights = jnp.exp(scores - biggest)
        window_out = jnp.einsum('hqk,hkd->hqd', weights, value_both, precision=highest) / lax.optimization_barrier(jnp.sum(weights, axis=-1, keepdims=True))
        inner_dot = jnp.einsum('hqd,hkd->hqk', query_now, key_now, precision=highest)
        inner_dot = jnp.where(causal[None], inner_dot, 0.0)
        linear_out = jnp.einsum('hqk,hkd->hqd', inner_dot, value_now, precision=highest)
        linear_out = linear_out + jnp.einsum('hqd,hde->hqe', query_now, state, precision=highest)
        state = state + jnp.einsum('hkd,hke->hde', key_now, value_now, precision=highest)
        return (state, (window_out, linear_out))
    start_state = jnp.zeros((HEADS, HD, HD), jnp.float32)
    numbers = jnp.arange(nblocks).astype(jnp.int32)
    final_state, outputs = lax.scan(advance, start_state, (numbers, query_blocks, key_blocks, value_blocks, key_before, value_before))
    window_all = outputs[0].transpose(0, 2, 1, 3).reshape(TOKENS, HEADS, HD)
    linear_all = outputs[1].transpose(0, 2, 1, 3).reshape(TOKENS, HEADS, HD)
    branch_a = window_all * head_gain[0][None, :, None]
    branch_b = linear_all * head_gain[1][None, :, None]
    norm_a = jnp.sqrt(lax.optimization_barrier(jnp.mean(branch_a * branch_a, axis=(1, 2))) + 1e-06)
    norm_b = jnp.sqrt(lax.optimization_barrier(jnp.mean(branch_b * branch_b, axis=(1, 2))) + 1e-06)
    mixed = branch_a / norm_a[:, None, None] + branch_b / norm_b[:, None, None]
    return mixed.reshape(TOKENS, HEADS * HD)
```

```python
import functools
import math

import jax
import jax.numpy as jnp
from jax import lax
from jax.experimental import pallas as pl
from jax.experimental.pallas import tpu as pltpu
from jax.sharding import PartitionSpec as P

HEADS = 64
HD = 128
WINDOW = 128
EPS = 1e-06
F32 = jnp.float32
BF16 = jnp.bfloat16
EXP2_SCALE = math.log2(math.e) / math.sqrt(HD)
VMEM_BYTES = 24 * 1024 * 1024


def halves(x):
    high = x.astype(BF16)
    low = (x - high.astype(F32)).astype(BF16)
    return high, low


def dot(a, b):
    return lax.dot_general(a, b, (((1,), (0,)), ((), ())), preferred_element_type=F32)


def dot_rows(a, b):
    return lax.dot_general(a, b, (((1,), (1,)), ((), ())), preferred_element_type=F32)


def dot_columns(a, b):
    return lax.dot_general(a, b, (((0,), (0,)), ((), ())), preferred_element_type=F32)


def side(a, b):
    return jnp.concatenate([a, b], axis=1)


def stack(a, b):
    return jnp.concatenate([a, b], axis=0)


def product(a_high, a_low, b_high, b_low):
    return dot(a_high, b_high) + dot(a_high, b_low) + dot(a_low, b_high)


def outer_state(k_high, k_low, v_high, v_low):
    grid = dot_columns(side(k_high, k_low), side(v_high, v_low))
    return grid[:HD, :HD] + (grid[:HD, HD:] + grid[HD:, :HD]) + grid[HD:, HD:]


def pair_scores(q_high, q_low, k_high, k_low):
    return dot_rows(side(q_high, q_low), side(k_high, k_high)) + dot_rows(q_high, k_low)


def lower_mask():
    rows = lax.broadcasted_iota(jnp.int32, (WINDOW, WINDOW), 0)
    columns = lax.broadcasted_iota(jnp.int32, (WINDOW, WINDOW), 1)
    return rows >= columns


def window_tile(scores, lower, values, gain):
    biggest = jnp.max(scores, axis=1, keepdims=True)
    weights = jnp.exp2((scores - biggest) * EXP2_SCALE)
    total = jnp.sum(weights, axis=1, keepdims=True)
    wide = side(jnp.where(lower, 0.0, weights), jnp.where(lower, weights, 0.0))
    out = product(*halves(wide), *values)
    return out * (gain / total)


def row_sums(square):
    ones = jnp.ones((8, HD), BF16)
    high, low = halves(square)
    return dot_rows(ones, high) + dot_rows(ones, low)


def totals_kernel(k_ref, v_ref, keep_ref, send_ref, tail_k_ref, tail_v_ref):
    core = lax.axis_index("ctx") % 2
    states = []
    for j in range(2):
        columns = slice(j * HD, (j + 1) * HD)
        states.append(outer_state(*halves(k_ref[:, columns]), *halves(v_ref[:, columns])))
    keep_ref[0] = jnp.where(core == 0, states[0], states[1])
    send_ref[0] = jnp.where(core == 0, states[1], states[0])
    rows = k_ref.shape[0]
    tail_k_ref[...] = k_ref[rows - WINDOW :, :]
    tail_v_ref[...] = v_ref[rows - WINDOW :, :]


def local_kernel(gain_ref, q_ref, k_ref, v_ref, a_ref, b_ref, sum_ref, square_ref):
    step = pl.program_id(0)
    lower = lower_mask()
    tiles = q_ref.shape[0] // WINDOW

    @pl.when(step == 0)
    def _():
        square_ref[...] = jnp.zeros_like(square_ref)

    for j in range(2):
        columns = slice(j * HD, (j + 1) * HD)
        gain_a = gain_ref[0, 2 * step + j]
        gain_b = gain_ref[1, 2 * step + j]
        state = None
        k_before = v_before = None
        for n in range(tiles):
            rows = slice(n * WINDOW, (n + 1) * WINDOW)
            q_high, q_low = halves(q_ref[rows, columns])
            k_now = halves(k_ref[rows, columns])
            v_now = halves(v_ref[rows, columns])
            if n == 0:
                now = pair_scores(q_high, q_low, *k_now)
                inner = jnp.where(lower, now, 0.0)
                b = product(*halves(inner), *v_now)
                a_ref[rows, columns] = jnp.zeros((WINDOW, HD), F32)
            else:
                both = pair_scores(
                    q_high, q_low, stack(k_before[0], k_now[0]), stack(k_before[1], k_now[1])
                )
                before, now = both[:, :WINDOW], both[:, WINDOW:]
                values = stack(v_before[0], v_now[0]), stack(v_before[1], v_now[1])
                a = window_tile(jnp.where(lower, now, before), lower, values, gain_a)
                a_ref[rows, columns] = a
                square_ref[rows, :] += a * a
                inner_high, inner_low = halves(jnp.where(lower, now, 0.0))
                state_high, state_low = halves(state)
                b = product(
                    side(inner_high, q_high),
                    side(inner_low, q_low),
                    stack(v_now[0], state_high),
                    stack(v_now[1], state_low),
                )
            b_ref[rows, columns] = b * gain_b
            if n < tiles - 1:
                added = outer_state(*k_now, *v_now)
                state = added if state is None else state + added
            k_before, v_before = k_now, v_now

    @pl.when(step == pl.num_programs(0) - 1)
    def _():
        sum_ref[...] = row_sums(square_ref[...])


def earlier_kernel(gain_ref, q_ref, b_ref, mine_ref, other_ref, sum_a_ref, out_ref, sums_ref, square_ref):
    step = pl.program_id(0)
    core = lax.axis_index("ctx") % 2

    @pl.when(step == 0)
    def _():
        square_ref[...] = jnp.zeros_like(square_ref)

    for j in range(2):
        columns = slice(j * HD, (j + 1) * HD)
        state = jnp.where(core == j, mine_ref[0], other_ref[0])
        gain_b = gain_ref[1, 2 * step + j]
        q_high, q_low = halves(q_ref[:, columns])
        b = b_ref[:, columns] + gain_b * product(q_high, q_low, *halves(state))
        out_ref[:, columns] = b
        square_ref[...] += b * b

    @pl.when(step == pl.num_programs(0) - 1)
    def _():
        row = lax.broadcasted_iota(jnp.int32, sums_ref.shape, 0)
        sums_ref[...] = jnp.where(row == 0, sum_a_ref[...], row_sums(square_ref[...]))


def first_tile_kernel(gain_ref, q_ref, k_ref, v_ref, tail_k_ref, tail_v_ref, a_ref, sum_ref, square_ref):
    step = pl.program_id(0)
    lower = lower_mask()
    reachable = jnp.logical_or(lower, lax.axis_index("ctx") > 0)

    @pl.when(step == 0)
    def _():
        square_ref[...] = jnp.zeros_like(square_ref)

    for j in range(2):
        columns = slice(j * HD, (j + 1) * HD)
        gain_a = gain_ref[0, 2 * step + j]
        q_high, q_low = halves(q_ref[:, columns])
        k_both = halves(stack(tail_k_ref[:, columns], k_ref[:, columns]))
        v_both = halves(stack(tail_v_ref[:, columns], v_ref[:, columns]))
        both = pair_scores(q_high, q_low, *k_both)
        scores = jnp.where(lower, both[:, WINDOW:], both[:, :WINDOW])
        scores = jnp.where(reachable, scores, -jnp.inf)
        a = window_tile(scores, lower, v_both, gain_a)
        a_ref[:, columns] = a
        square_ref[...] += a * a

    @pl.when(step == pl.num_programs(0) - 1)
    def _():
        sum_ref[...] = row_sums(square_ref[...])


def inverse_norm(total):
    return 1.0 / jnp.sqrt(total / (HEADS * HD) + EPS)


def scale_kernel(parts, *refs):
    sums, (a_ref, b_ref, out_ref) = refs[:parts], refs[-3:]
    total = sums[0][...]
    for part in sums[1:parts]:
        total = total + part[...]
    columns = inverse_norm(total).T
    out_ref[...] = a_ref[...] * columns[:, 0:1] + b_ref[...] * columns[:, 1:2]


def first_scale_kernel(parts, *refs):
    sums_b, sums_a = refs[:parts], refs[parts : 2 * parts]
    a_ref, b_ref, _, out_ref = refs[-4:]
    total_a, total_b = sums_a[0][...], sums_b[0][...]
    for part_a, part_b in zip(sums_a[1:], sums_b[1:]):
        total_a, total_b = total_a + part_a[...], total_b + part_b[...]
    inverse_a = inverse_norm(total_a).T[:, 0:1]
    inverse_b = inverse_norm(total_b).T[:, 1:2]
    out_ref[...] = a_ref[...] * inverse_a + b_ref[...] * inverse_b


def swap(block, axis, bit):
    return lax.ppermute(block, axis, [(i, i ^ bit) for i in range(lax.axis_size(axis))])


def everyone(block, axis):
    count = lax.axis_size(axis)
    return [block] + [
        lax.ppermute(block, axis, [(i, (i + s) % count) for i in range(count)]) for s in range(1, count)
    ]


def earlier_states(keep, send):
    count = lax.axis_size("ctx")
    index = lax.axis_index("ctx")
    devices = range(count)
    core = index % 2
    beside = swap(send, "ctx", 1)
    chip = keep + beside
    if count == 8:
        x = (index >> 1) % 2
        route = [(i, i ^ 2) for i in devices if i % 2 == 0]
        route += [(i, i + 4) for i in devices if i % 2 == 1 and i < 4]
        first = lax.ppermute(chip, "ctx", route)
        message = first + jnp.where((core == 0) | (x == 0), chip, 0.0)
        route = [(i, i + 4) for i in devices if i % 2 == 0 and i < 4]
        route += [(i, i ^ 2) for i in devices if i % 2 == 1 and i != 3]
        second = lax.ppermute(message, "ctx", route)
        earlier = jnp.where((core == 1) | (x == 1), first, 0.0) + second
    else:
        earlier = jnp.zeros_like(chip)
        running = chip
        bit = 2
        while bit < count:
            partner = swap(running, "ctx", bit)
            earlier = earlier + jnp.where((index & bit) != 0, partner, 0.0)
            running = running + partner
            bit *= 2
    mine = earlier + jnp.where(core == 1, beside, 0.0)
    other = swap(earlier + jnp.where(core == 0, keep, 0.0), "ctx", 1)
    return mine, other


def shards(queries, keys, values, head_gain):
    rows, width = queries.shape
    heads = head_gain.shape[1]
    steps = heads // 2
    parts = lax.axis_size("head")
    smem = pl.BlockSpec(memory_space=pltpu.SMEM)
    whole = pl.BlockSpec((rows, 2 * HD), lambda i: (0, i))
    top = pl.BlockSpec((WINDOW, 2 * HD), lambda i: (0, i))
    state = pl.BlockSpec((1, HD, HD), lambda i: (i, 0, 0))
    sums_block = pl.BlockSpec((8, rows), lambda i: (0, 0))
    first_sums_block = pl.BlockSpec((8, WINDOW), lambda i: (0, 0))

    def array(*shape):
        return jax.ShapeDtypeStruct(shape, F32)

    def call(kernel, name, flops, moved, **kwargs):
        return pl.pallas_call(
            kernel,
            name=name,
            compiler_params=pltpu.CompilerParams(vmem_limit_bytes=VMEM_BYTES),
            cost_estimate=pl.CostEstimate(flops=flops, bytes_accessed=moved, transcendentals=0),
            **kwargs,
        )

    size = rows * width * 4
    unit = 2 * rows * width * HD
    keep, send, tail_k, tail_v = call(
        totals_kernel,
        "totals",
        4 * unit,
        2 * size,
        grid=(steps,),
        in_specs=[whole, whole],
        out_specs=[state, state, top, top],
        out_shape=[
            array(steps, HD, HD),
            array(steps, HD, HD),
            array(WINDOW, width),
            array(WINDOW, width),
        ],
    )(keys, values)

    route = [(i, i + 1) for i in range(lax.axis_size("ctx") - 1)]
    mine, other = earlier_states(keep, send)
    before_k = lax.ppermute(tail_k, "ctx", route)
    before_v = lax.ppermute(tail_v, "ctx", route)

    window, linear, sum_a = call(
        local_kernel,
        "local",
        24 * unit,
        5 * size,
        grid=(steps,),
        in_specs=[smem, whole, whole, whole],
        out_specs=[whole, whole, sums_block],
        out_shape=[array(rows, width), array(rows, width), array(8, rows)],
        scratch_shapes=[pltpu.VMEM((rows, HD), F32)],
    )(head_gain, queries, keys, values)

    linear, sums = call(
        earlier_kernel,
        "earlier",
        3 * unit,
        3 * size,
        grid=(steps,),
        in_specs=[smem, whole, whole, state, state, sums_block],
        out_specs=[whole, sums_block],
        out_shape=[array(rows, width), array(8, rows)],
        scratch_shapes=[pltpu.VMEM((rows, HD), F32)],
    )(head_gain, queries, linear, mine, other, sum_a)
    all_sums = everyone(sums, "head")

    first_a, first_sum = call(
        first_tile_kernel,
        "first_tile",
        2 * unit,
        size,
        grid=(steps,),
        in_specs=[smem, top, top, top, top, top],
        out_specs=[top, first_sums_block],
        out_shape=[array(WINDOW, width), array(8, WINDOW)],
        scratch_shapes=[pltpu.VMEM((WINDOW, HD), F32)],
    )(head_gain, queries, keys, values, before_k, before_v)
    all_first = everyone(first_sum, "head")

    row_block = pl.BlockSpec((WINDOW, width), lambda i: (i + 1, 0))
    first_block = pl.BlockSpec((WINDOW, width), lambda i: (0, 0))
    out = call(
        functools.partial(scale_kernel, parts),
        "scale",
        unit // 64,
        2 * size,
        grid=(rows // WINDOW - 1,),
        in_specs=[pl.BlockSpec((8, WINDOW), lambda i: (0, i + 1))] * parts + [row_block, row_block],
        out_specs=row_block,
        out_shape=array(rows, width),
    )(*all_sums, window, linear)
    return call(
        functools.partial(first_scale_kernel, parts),
        "first_scale",
        unit // 256,
        size // 2,
        grid=(1,),
        in_specs=[first_sums_block] * (2 * parts)
        + [first_block, first_block, pl.BlockSpec(memory_space=pl.ANY)],
        out_specs=first_block,
        out_shape=array(rows, width),
        input_output_aliases={2 * parts + 2: 0},
    )(*all_sums, *all_first, first_a, linear, out)


def solution(mesh):
    in_specs = (P("ctx", "head"), P("ctx", "head"), P("ctx", "head"), P(None, "head"))
    out_specs = P("ctx", "head")
    return jax.shard_map(shards, mesh=mesh, in_specs=in_specs, out_specs=out_specs, check_vma=False)
```

```python
import functools
import math

import jax
import jax.numpy as jnp
from jax import lax
from jax.experimental import pallas as pl
from jax.experimental.pallas import tpu as pltpu
from jax.sharding import PartitionSpec as P

HEADS = 64
HD = 128
WINDOW = 128
EPS = 1e-06
F32 = jnp.float32
BF16 = jnp.bfloat16
EXP2_SCALE = math.log2(math.e) / math.sqrt(HD)
VMEM_BYTES = 24 * 1024 * 1024


def halves(x):
    high = x.astype(BF16)
    low = (x - high.astype(F32)).astype(BF16)
    return high, low


def dot(a, b):
    return lax.dot_general(a, b, (((1,), (0,)), ((), ())), preferred_element_type=F32)


def dot_rows(a, b):
    return lax.dot_general(a, b, (((1,), (1,)), ((), ())), preferred_element_type=F32)


def dot_columns(a, b):
    return lax.dot_general(a, b, (((0,), (0,)), ((), ())), preferred_element_type=F32)


def side(a, b):
    return jnp.concatenate([a, b], axis=1)


def stack(a, b):
    return jnp.concatenate([a, b], axis=0)


def outer_state(k_high, k_low, v_high, v_low):
    grid = dot_columns(side(k_high, k_low), side(v_high, v_low))
    return grid[:HD, :HD] + (grid[:HD, HD:] + grid[HD:, :HD]) + grid[HD:, HD:]


def lower_mask():
    rows = lax.broadcasted_iota(jnp.int32, (WINDOW, WINDOW), 0)
    columns = lax.broadcasted_iota(jnp.int32, (WINDOW, WINDOW), 1)
    return rows >= columns


def row_sums(square):
    ones = jnp.ones((8, HD), BF16)
    high, low = halves(square)
    return dot_rows(ones, high) + dot_rows(ones, low)


def wide_keys(k_high, k_low):
    return stack(side(k_high, k_high), side(k_low, jnp.zeros_like(k_low)))


def wide_state(state):
    high, low = halves(state)
    return stack(side(high, low), side(high, jnp.zeros_like(high)))


def folded(wide):
    half = wide.shape[1] // 2
    return wide[:, :half] + wide[:, half:]


def totals_kernel(k_ref, v_ref, keep_ref, send_ref, half_ref, tail_k_ref, tail_v_ref):
    core = lax.axis_index("ctx") % 2
    rows = k_ref.shape[0]
    middle = rows // 2
    states = []
    for j in range(2):
        columns = slice(j * HD, (j + 1) * HD)
        k_high, k_low = halves(k_ref[:, columns])
        v_high, v_low = halves(v_ref[:, columns])
        first = outer_state(k_high[:middle], k_low[:middle], v_high[:middle], v_low[:middle])
        second = outer_state(k_high[middle:], k_low[middle:], v_high[middle:], v_low[middle:])
        half_ref[j] = first
        states.append(first + second)
    keep_ref[0] = jnp.where(core == 0, states[0], states[1])
    send_ref[0] = jnp.where(core == 0, states[1], states[0])
    tail_k_ref[...] = k_ref[rows - WINDOW :, :]
    tail_v_ref[...] = v_ref[rows - WINDOW :, :]


def weights_of(scores):
    biggest = jnp.max(scores, axis=1, keepdims=True)
    weights = jnp.exp2((scores - biggest) * EXP2_SCALE)
    return weights, jnp.sum(weights, axis=1, keepdims=True)


def masked_pair(weights, below, above):
    high, low = halves(weights)
    return side(high * above, high * below), side(low * above, low * below)


def local_kernel(gain_ref, q_ref, k_ref, v_ref, a_ref, b_ref, qq_ref, sum_ref, square_ref):
    step = pl.program_id(0)
    lower = lower_mask()
    below = jnp.where(lower, 1.0, 0.0).astype(BF16)
    above = jnp.where(lower, 0.0, 1.0).astype(BF16)
    rows = q_ref.shape[0]
    tiles = rows // WINDOW

    @pl.when(step == 0)
    def _():
        square_ref[...] = jnp.zeros_like(square_ref)

    def tile(n):
        return slice(n * WINDOW, (n + 1) * WINDOW)

    scores = []
    for j in range(2):
        columns = slice(j * HD, (j + 1) * HD)
        qq = side(*halves(q_ref[:, columns]))
        qq_ref[:, 2 * j * HD : 2 * (j + 1) * HD] = qq
        k_high, k_low = halves(k_ref[:, columns])
        now, before = [], [None]
        for n in range(tiles):
            keys = wide_keys(k_high[tile(n)], k_low[tile(n)])
            found = folded(dot_rows(qq[n * WINDOW : min((n + 2) * WINDOW, rows)], keys))
            now.append(found[:WINDOW])
            before.append(found[WINDOW:])
        scores.append((now, before))
    for j in range(2):
        columns = slice(j * HD, (j + 1) * HD)
        v_high, v_low = halves(v_ref[:, columns])
        vv = side(v_high, v_low)
        now, before = scores[j]
        gain_a = gain_ref[0, 2 * step + j]
        for n in range(tiles):
            inner_high, inner_low = halves(jnp.where(lower, now[n], 0.0))
            if n == 0:
                wide = dot(stack(inner_high, inner_low), vv[tile(0)])
                b_ref[tile(0), columns] = folded(wide[:WINDOW]) + wide[WINDOW:, :HD]
                a_ref[tile(0), columns] = jnp.zeros((WINDOW, HD), F32)
                continue
            weights, total = weights_of(jnp.where(lower, now[n], before[n]))
            pair_high, pair_low = masked_pair(weights, below, above)
            if n % 2:
                before_high, before_low = halves(before[n])
            else:
                before_high = before_low = jnp.zeros((WINDOW, HD), BF16)
            left = jnp.concatenate(
                [pair_high, pair_low, side(before_high, inner_high), side(before_low, inner_low)], axis=0
            )
            wide = dot(left, vv[(n - 1) * WINDOW : (n + 1) * WINDOW])
            a = (folded(wide[tile(0)]) + wide[tile(1), :HD]) * (gain_a / total)
            a_ref[tile(n), columns] = a
            square_ref[tile(n), :] += a * a
            b_ref[tile(n), columns] = folded(wide[tile(2)]) + wide[tile(3), :HD]

    @pl.when(step == pl.num_programs(0) - 1)
    def _():
        sum_ref[...] = row_sums(square_ref[...])


def message_kernel(first_ref, chip_ref, _, __, out_ref):
    index = lax.axis_index("ctx")
    added = (index % 2 == 0) | ((index >> 1) % 2 == 0)
    out_ref[...] = first_ref[...] + jnp.where(added, chip_ref[...], 0.0)


def prefix_kernel(first_ref, second_ref, keep_ref, beside_ref, mine_ref, other_ref):
    index = lax.axis_index("ctx")
    core = index % 2
    held = (core == 1) | ((index >> 1) % 2 == 1)
    earlier = jnp.where(held, first_ref[...], 0.0) + second_ref[...]
    mine_ref[...] = earlier + jnp.where(core == 1, beside_ref[...], 0.0)
    other_ref[...] = earlier + jnp.where(core == 0, keep_ref[...], 0.0)


def earlier_kernel(
    gain_ref, qq_ref, b_ref, half_ref, mine_ref, other_ref, sum_a_ref, out_ref, sums_ref, square_ref
):
    step = pl.program_id(0)
    core = lax.axis_index("ctx") % 2
    rows = qq_ref.shape[0]
    middle = rows // 2

    @pl.when(step == 0)
    def _():
        square_ref[...] = jnp.zeros_like(square_ref)

    for j in range(2):
        columns = slice(j * HD, (j + 1) * HD)
        state = jnp.where(core == j, mine_ref[0], other_ref[0])
        gain_b = gain_ref[1, 2 * step + j]
        for part, held in ((slice(0, middle), state), (slice(middle, rows), state + half_ref[j])):
            qq = qq_ref[part, 2 * j * HD : 2 * (j + 1) * HD]
            b = gain_b * (b_ref[part, columns] + folded(dot(qq, wide_state(held))))
            out_ref[part, columns] = b
            square_ref[part, :] += b * b

    @pl.when(step == pl.num_programs(0) - 1)
    def _():
        row = lax.broadcasted_iota(jnp.int32, sums_ref.shape, 0)
        sums_ref[...] = jnp.where(row == 0, sum_a_ref[...], row_sums(square_ref[...]))


def first_tile_kernel(gain_ref, q_ref, k_ref, v_ref, tail_k_ref, tail_v_ref, a_ref, sum_ref, square_ref):
    step = pl.program_id(0)
    count = q_ref.shape[1] // HD
    lower = lower_mask()
    below = jnp.where(lower, 1.0, 0.0).astype(BF16)
    above = jnp.where(lower, 0.0, 1.0).astype(BF16)
    reachable = jnp.logical_or(lower, lax.axis_index("ctx") > 0)

    @pl.when(step == 0)
    def _():
        square_ref[...] = jnp.zeros_like(square_ref)

    scores = []
    for j in range(count):
        columns = slice(j * HD, (j + 1) * HD)
        qq = side(*halves(q_ref[:, columns]))
        now = folded(dot_rows(qq, wide_keys(*halves(k_ref[:, columns]))))
        before = folded(dot_rows(qq, wide_keys(*halves(tail_k_ref[:, columns]))))
        scores.append(jnp.where(reachable, jnp.where(lower, now, before), -jnp.inf))
    for j in range(count):
        columns = slice(j * HD, (j + 1) * HD)
        gain_a = gain_ref[0, count * step + j]
        weights, total = weights_of(scores[j])
        pair_high, pair_low = masked_pair(weights, below, above)
        vv = side(*halves(stack(tail_v_ref[:, columns], v_ref[:, columns])))
        wide = dot(stack(pair_high, pair_low), vv)
        a = (folded(wide[:WINDOW]) + wide[WINDOW:, :HD]) * (gain_a / total)
        a_ref[:, columns] = a
        square_ref[...] += a * a

    @pl.when(step == pl.num_programs(0) - 1)
    def _():
        sum_ref[...] = row_sums(square_ref[...])


def inverse_norm(total):
    return 1.0 / jnp.sqrt(total / (HEADS * HD) + EPS)


def scale_kernel(parts, *refs):
    sums, (a_ref, b_ref, out_ref) = refs[:parts], refs[-3:]
    total = sums[0][...]
    for part in sums[1:parts]:
        total = total + part[...]
    columns = inverse_norm(total).T
    out_ref[...] = a_ref[...] * columns[:, 0:1] + b_ref[...] * columns[:, 1:2]


def first_scale_kernel(parts, *refs):
    sums_b, sums_a = refs[:parts], refs[parts : 2 * parts]
    a_ref, b_ref, _, out_ref = refs[-4:]
    total_a, total_b = sums_a[0][...], sums_b[0][...]
    for part_a, part_b in zip(sums_a[1:], sums_b[1:]):
        total_a, total_b = total_a + part_a[...], total_b + part_b[...]
    inverse_a = inverse_norm(total_a).T[:, 0:1]
    inverse_b = inverse_norm(total_b).T[:, 1:2]
    out_ref[...] = a_ref[...] * inverse_a + b_ref[...] * inverse_b


def swap(block, axis, bit):
    return lax.ppermute(block, axis, [(i, i ^ bit) for i in range(lax.axis_size(axis))])


def everyone(block, axis):
    count = lax.axis_size(axis)
    return [block] + [
        lax.ppermute(block, axis, [(i, (i + s) % count) for i in range(count)]) for s in range(1, count)
    ]


def chip_totals(keep, send):
    beside = swap(send, "ctx", 1)
    return beside, keep + beside


def first_phase(chip):
    route = [(i, i ^ 2) for i in range(8) if i % 2 == 0]
    route += [(i, i + 4) for i in range(8) if i % 2 == 1 and i < 4]
    return lax.ppermute(chip, "ctx", route)


def second_phase(message):
    route = [(i, i + 4) for i in range(8) if i % 2 == 0 and i < 4]
    route += [(i, i ^ 2) for i in range(8) if i % 2 == 1 and i != 3]
    return lax.ppermute(message, "ctx", route)


def doubled_prefix(chip):
    index = lax.axis_index("ctx")
    earlier = jnp.zeros_like(chip)
    running = chip
    bit = 2
    while bit < lax.axis_size("ctx"):
        partner = swap(running, "ctx", bit)
        earlier = earlier + jnp.where((index & bit) != 0, partner, 0.0)
        running = running + partner
        bit *= 2
    return earlier


def shards(queries, keys, values, head_gain):
    rows, width = queries.shape
    heads = head_gain.shape[1]
    steps = heads // 2
    parts = lax.axis_size("head")
    queries, keys, values = (
        pltpu.with_memory_space_constraint(x, pltpu.HBM) for x in (queries, keys, values)
    )
    smem = pl.BlockSpec(memory_space=pltpu.SMEM)
    anywhere = pl.BlockSpec(memory_space=pl.ANY)
    whole = pl.BlockSpec((rows, 2 * HD), lambda i: (0, i))
    top = pl.BlockSpec((WINDOW, 2 * HD), lambda i: (0, i))
    top_four = pl.BlockSpec((WINDOW, 4 * HD), lambda i: (0, i))
    doubled = pl.BlockSpec((rows, 4 * HD), lambda i: (0, i))
    state = pl.BlockSpec((1, HD, HD), lambda i: (i, 0, 0))
    state_pair = pl.BlockSpec((2, HD, HD), lambda i: (i, 0, 0))
    sums_block = pl.BlockSpec((8, rows), lambda i: (0, 0))
    first_sums_block = pl.BlockSpec((8, WINDOW), lambda i: (0, 0))

    def array(*shape):
        return jax.ShapeDtypeStruct(shape, F32)

    def call(kernel, name, flops, moved, **kwargs):
        return pl.pallas_call(
            kernel,
            name=name,
            compiler_params=pltpu.CompilerParams(vmem_limit_bytes=VMEM_BYTES),
            cost_estimate=pl.CostEstimate(flops=flops, bytes_accessed=moved, transcendentals=0),
            **kwargs,
        )

    size = rows * width * 4
    unit = 2 * rows * width * HD
    packed = array(steps, HD, HD)
    keep, send, half, tail_k, tail_v = call(
        totals_kernel,
        "totals",
        4 * unit,
        2 * size,
        grid=(steps,),
        in_specs=[whole, whole],
        out_specs=[state, state, state_pair, top, top],
        out_shape=[packed, packed, array(heads, HD, HD), array(WINDOW, width), array(WINDOW, width)],
    )(keys, values)

    route = [(i, i + 1) for i in range(lax.axis_size("ctx") - 1)]
    before_k = lax.ppermute(tail_k, "ctx", route)
    before_v = lax.ppermute(tail_v, "ctx", route)
    beside, chip = chip_totals(keep, send)

    window, linear, qq, sum_a = call(
        local_kernel,
        "local",
        24 * unit,
        5 * size,
        grid=(steps,),
        in_specs=[smem, whole, whole, whole],
        out_specs=[whole, whole, doubled, sums_block],
        out_shape=[
            array(rows, width),
            array(rows, width),
            jax.ShapeDtypeStruct((rows, 2 * width), BF16),
            array(8, rows),
        ],
        scratch_shapes=[pltpu.VMEM((rows, HD), F32)],
    )(head_gain, queries, keys, values)

    if lax.axis_size("ctx") == 8:
        first = first_phase(chip)
        message = call(
            message_kernel,
            "message",
            0,
            size // 4,
            in_specs=[pl.BlockSpec(), pl.BlockSpec(), anywhere, anywhere],
            out_shape=packed,
        )(first, chip, sum_a, before_k)
        second = second_phase(message)
        mine, other = call(
            prefix_kernel, "prefix", 0, size // 2, out_shape=[packed, packed]
        )(first, second, keep, beside)
    else:
        earlier = doubled_prefix(chip)
        core = lax.axis_index("ctx") % 2
        mine = earlier + jnp.where(core == 1, beside, 0.0)
        other = earlier + jnp.where(core == 0, keep, 0.0)
    other = swap(other, "ctx", 1)

    linear, sums = call(
        earlier_kernel,
        "earlier",
        3 * unit,
        3 * size,
        grid=(steps,),
        in_specs=[smem, doubled, whole, state_pair, state, state, sums_block],
        out_specs=[whole, sums_block],
        out_shape=[array(rows, width), array(8, rows)],
        scratch_shapes=[pltpu.VMEM((rows, HD), F32)],
    )(head_gain, qq, linear, half, mine, other, sum_a)
    all_sums = everyone(sums, "head")

    first_a, first_sum = call(
        first_tile_kernel,
        "first_tile",
        2 * unit,
        size,
        grid=(heads // 4,),
        in_specs=[smem] + [top_four] * 5,
        out_specs=[top_four, first_sums_block],
        out_shape=[array(WINDOW, width), array(8, WINDOW)],
        scratch_shapes=[pltpu.VMEM((WINDOW, HD), F32)],
    )(head_gain, queries, keys, values, before_k, before_v)
    all_first = everyone(first_sum, "head")

    row_block = pl.BlockSpec((WINDOW, width), lambda i: (i + 1, 0))
    first_block = pl.BlockSpec((WINDOW, width), lambda i: (0, 0))
    out = call(
        functools.partial(scale_kernel, parts),
        "scale",
        unit // 64,
        2 * size,
        grid=(rows // WINDOW - 1,),
        in_specs=[pl.BlockSpec((8, WINDOW), lambda i: (0, i + 1))] * parts + [row_block, row_block],
        out_specs=row_block,
        out_shape=array(rows, width),
    )(*all_sums, window, linear)
    return call(
        functools.partial(first_scale_kernel, parts),
        "first_scale",
        unit // 256,
        size // 2,
        grid=(1,),
        in_specs=[first_sums_block] * (2 * parts) + [first_block, first_block, anywhere],
        out_specs=first_block,
        out_shape=array(rows, width),
        input_output_aliases={2 * parts + 2: 0},
    )(*all_sums, *all_first, first_a, linear, out)


def solution(mesh):
    in_specs = (P("ctx", "head"), P("ctx", "head"), P("ctx", "head"), P(None, "head"))
    out_specs = P("ctx", "head")
    return jax.shard_map(shards, mesh=mesh, in_specs=in_specs, out_specs=out_specs, check_vma=False)
```

```python
import functools
import math

import jax
import jax.numpy as jnp
from jax import lax
from jax.experimental import pallas as pl
from jax.experimental.pallas import tpu as pltpu
from jax.sharding import PartitionSpec as P

HEADS = 64
HD = 128
WINDOW = 128
EPS = 1e-06
F32 = jnp.float32
BF16 = jnp.bfloat16
EXP2_SCALE = math.log2(math.e) / math.sqrt(HD)
VMEM_BYTES = 24 * 1024 * 1024


def halves(x):
    high = x.astype(BF16)
    low = (x - high.astype(F32)).astype(BF16)
    return high, low


def dot(a, b):
    return lax.dot_general(a, b, (((1,), (0,)), ((), ())), preferred_element_type=F32)


def dot_rows(a, b):
    return lax.dot_general(a, b, (((1,), (1,)), ((), ())), preferred_element_type=F32)


def dot_columns(a, b):
    return lax.dot_general(a, b, (((0,), (0,)), ((), ())), preferred_element_type=F32)


def side(a, b):
    return jnp.concatenate([a, b], axis=1)


def stack(a, b):
    return jnp.concatenate([a, b], axis=0)


def outer_state(k_high, k_low, v_high, v_low):
    grid = dot_columns(side(k_high, k_low), side(v_high, v_low))
    return grid[:HD, :HD] + (grid[:HD, HD:] + grid[HD:, :HD]) + grid[HD:, HD:]


def lower_mask():
    rows = lax.broadcasted_iota(jnp.int32, (WINDOW, WINDOW), 0)
    columns = lax.broadcasted_iota(jnp.int32, (WINDOW, WINDOW), 1)
    return rows >= columns


def row_sums(square):
    ones = jnp.ones((8, HD), BF16)
    high, low = halves(square)
    return dot_rows(ones, high) + dot_rows(ones, low)


def wide_keys(k_high, k_low):
    return stack(side(k_high, k_high), side(k_low, jnp.zeros_like(k_low)))


def wide_state(state):
    high, low = halves(state)
    return stack(side(high, low), side(high, jnp.zeros_like(high)))


def folded(wide):
    half = wide.shape[1] // 2
    return wide[:, :half] + wide[:, half:]


def totals_kernel(k_ref, v_ref, keep_ref, send_ref, half_ref, tail_v_ref):
    core = lax.axis_index("ctx") % 2
    rows = k_ref.shape[0]
    middle = rows // 2
    for i in range(k_ref.shape[1] // (2 * HD)):
        states = []
        for j in (2 * i, 2 * i + 1):
            columns = slice(j * HD, (j + 1) * HD)
            k_high, k_low = halves(k_ref[:, columns])
            v_high, v_low = halves(v_ref[:, columns])
            first = outer_state(k_high[:middle], k_low[:middle], v_high[:middle], v_low[:middle])
            second = outer_state(k_high[middle:], k_low[middle:], v_high[middle:], v_low[middle:])
            half_ref[j] = first
            states.append(first + second)
        keep_ref[i] = jnp.where(core == 0, states[0], states[1])
        send_ref[i] = jnp.where(core == 0, states[1], states[0])
    tail_v_ref[...] = v_ref[rows - WINDOW :, :]


def weights_of(scores):
    biggest = jnp.max(scores, axis=1, keepdims=True)
    weights = jnp.exp2((scores - biggest) * EXP2_SCALE)
    return weights, jnp.sum(weights, axis=1, keepdims=True)


def masked_pair(weights, below, above):
    high, low = halves(weights)
    return side(high * above, high * below), side(low * above, low * below)


def local_kernel(start, extra, gain_ref, q_ref, k_ref, v_ref, *refs):
    a_ref, b_ref, qq_ref, sum_ref, square_ref = refs[extra:]
    step = pl.program_id(0)
    lower = lower_mask()
    below = jnp.where(lower, 1.0, 0.0).astype(BF16)
    above = jnp.where(lower, 0.0, 1.0).astype(BF16)
    rows = q_ref.shape[0]
    tiles = rows // WINDOW
    head = start + 2 * step

    @pl.when(step == 0)
    def _():
        square_ref[...] = jnp.zeros_like(square_ref)

    def tile(n):
        return slice(n * WINDOW, (n + 1) * WINDOW)

    scores = []
    for j in range(2):
        columns = slice(j * HD, (j + 1) * HD)
        qq = side(*halves(q_ref[:, columns]))
        qq_ref[:, 2 * j * HD : 2 * (j + 1) * HD] = qq
        k_high, k_low = halves(k_ref[:, columns])
        now, before = [], [None]
        for n in range(tiles):
            keys = wide_keys(k_high[tile(n)], k_low[tile(n)])
            found = folded(dot_rows(qq[n * WINDOW : min((n + 2) * WINDOW, rows)], keys))
            now.append(found[:WINDOW])
            before.append(found[WINDOW:])
        scores.append((now, before))
    for j in range(2):
        columns = slice(j * HD, (j + 1) * HD)
        v_high, v_low = halves(v_ref[:, columns])
        vv = side(v_high, v_low)
        now, before = scores[j]
        gain_a = gain_ref[0, head + j]
        for n in range(tiles):
            inner_high, inner_low = halves(jnp.where(lower, now[n], 0.0))
            if n == 0:
                wide = dot(stack(inner_high, inner_low), vv[tile(0)])
                b_ref[tile(0), columns] = folded(wide[:WINDOW]) + wide[WINDOW:, :HD]
                a_ref[tile(0), columns] = jnp.zeros((WINDOW, HD), F32)
                continue
            weights, total = weights_of(jnp.where(lower, now[n], before[n]))
            pair_high, pair_low = masked_pair(weights, below, above)
            if n % 2:
                before_high, before_low = halves(before[n])
            else:
                before_high = before_low = jnp.zeros((WINDOW, HD), BF16)
            left = jnp.concatenate(
                [pair_high, pair_low, side(before_high, inner_high), side(before_low, inner_low)], axis=0
            )
            wide = dot(left, vv[(n - 1) * WINDOW : (n + 1) * WINDOW])
            a = (folded(wide[tile(0)]) + wide[tile(1), :HD]) * (gain_a / total)
            a_ref[tile(n), columns] = a
            square_ref[tile(n), :] += a * a
            b_ref[tile(n), columns] = folded(wide[tile(2)]) + wide[tile(3), :HD]

    @pl.when(step == pl.num_programs(0) - 1)
    def _():
        sum_ref[...] = row_sums(square_ref[...])


def message_kernel(first_ref, chip_ref, *refs):
    out_ref = refs[-2]
    index = lax.axis_index("ctx")
    core, x, y = index % 2, (index >> 1) % 2, index >> 2
    first = jnp.where((core == 0) | (y == 1), first_ref[...], 0.0)
    out_ref[...] = first + jnp.where((core == 0) | (x == 0), chip_ref[...], 0.0)


def prefix_kernel(first_ref, second_ref, keep_ref, beside_ref, *refs):
    mine_ref, other_ref = refs[-2:]
    index = lax.axis_index("ctx")
    core, x, y = index % 2, (index >> 1) % 2, index >> 2
    use_first = jnp.where(core == 0, x, y) == 1
    use_second = (core == 1) & ((x == 1) | (y == 1)) | (core == 0) & (y == 1)
    earlier = jnp.where(use_first, first_ref[...], 0.0) + jnp.where(use_second, second_ref[...], 0.0)
    mine_ref[...] = earlier + jnp.where(core == 1, beside_ref[...], 0.0)
    other_ref[...] = earlier + jnp.where(core == 0, keep_ref[...], 0.0)


def earlier_kernel(gain_ref, *refs):
    parts, (half_ref, mine_ref, other_ref, sum_low_ref, sum_high_ref), outs = refs[:4], refs[4:9], refs[9:]
    sums_ref, square_ref = outs[2:]
    core = lax.axis_index("ctx") % 2
    rows = parts[1].shape[0]
    middle = rows // 2
    begin = 0
    square_ref[...] = jnp.zeros_like(square_ref)
    for side_number in range(2):
        qq_ref, b_ref = parts[2 * side_number : 2 * side_number + 2]
        out_ref = outs[side_number]
        for j in range(b_ref.shape[1] // HD):
            head = begin + j
            columns = slice(j * HD, (j + 1) * HD)
            state = jnp.where(core == head % 2, mine_ref[head // 2], other_ref[head // 2])
            gain_b = gain_ref[1, head]
            for part, held in ((slice(0, middle), state), (slice(middle, rows), state + half_ref[head])):
                qq = qq_ref[part, 2 * j * HD : 2 * (j + 1) * HD]
                b = gain_b * (b_ref[part, columns] + folded(dot(qq, wide_state(held))))
                out_ref[part, columns] = b
                square_ref[part, :] += b * b
        begin += b_ref.shape[1] // HD
    row = lax.broadcasted_iota(jnp.int32, sums_ref.shape, 0)
    sums_ref[...] = jnp.where(row == 0, sum_low_ref[...] + sum_high_ref[...], row_sums(square_ref[...]))


def first_weights_kernel(gain_ref, q_ref, k_ref, v_ref, tail_k_ref, weights_ref, out_ref):
    step = pl.program_id(0)
    count = q_ref.shape[1] // HD
    lower = lower_mask()
    reachable = jnp.logical_or(lower, lax.axis_index("ctx") > 0)
    scores = []
    for j in range(count):
        columns = slice(j * HD, (j + 1) * HD)
        qq = side(*halves(q_ref[:, columns]))
        now = folded(dot_rows(qq, wide_keys(*halves(k_ref[:, columns]))))
        before = folded(dot_rows(qq, wide_keys(*halves(tail_k_ref[:, columns]))))
        scores.append(jnp.where(reachable, jnp.where(lower, now, before), -jnp.inf))
    for j in range(count):
        columns = slice(j * HD, (j + 1) * HD)
        weights, total = weights_of(scores[j])
        weights = weights * (gain_ref[0, count * step + j] / total)
        now_high, now_low = halves(jnp.where(lower, weights, 0.0))
        vv = side(*halves(v_ref[:, columns]))
        wide = dot(stack(now_high, now_low), vv)
        out_ref[:, columns] = folded(wide[:WINDOW]) + wide[WINDOW:, :HD]
        weights_ref[:, 2 * j * HD : 2 * (j + 1) * HD] = side(*halves(jnp.where(lower, 0.0, weights)))


def first_values_kernel(weights_ref, now_ref, tail_v_ref, a_ref, sum_ref):
    square = jnp.zeros((WINDOW, HD), F32)
    for j in range(now_ref.shape[1] // HD):
        columns = slice(j * HD, (j + 1) * HD)
        high = weights_ref[:, 2 * j * HD : (2 * j + 1) * HD]
        low = weights_ref[:, (2 * j + 1) * HD : 2 * (j + 1) * HD]
        wide = dot(stack(high, low), side(*halves(tail_v_ref[:, columns])))
        a = now_ref[:, columns] + (folded(wide[:WINDOW]) + wide[WINDOW:, :HD])
        a_ref[:, columns] = a
        square = square + a * a
    sum_ref[...] = row_sums(square)


def inverse_norm(total):
    return 1.0 / jnp.sqrt(total / (HEADS * HD) + EPS)


def scale_kernel(parts, *refs):
    sums, (a_low, a_high, b_low, b_high, out_ref) = refs[:parts], refs[-5:]
    total = sums[0][...]
    for part in sums[1:parts]:
        total = total + part[...]
    columns = inverse_norm(total).T
    half = a_low.shape[1]
    out_ref[:, :half] = a_low[...] * columns[:, 0:1] + b_low[...] * columns[:, 1:2]
    out_ref[:, half:] = a_high[...] * columns[:, 0:1] + b_high[...] * columns[:, 1:2]


def first_scale_kernel(parts, *refs):
    sums_b, sums_a = refs[:parts], refs[parts : 2 * parts]
    a_ref, b_low, b_high, _, out_ref = refs[-5:]
    total_a, total_b = sums_a[0][...], sums_b[0][...]
    for part_a, part_b in zip(sums_a[1:], sums_b[1:]):
        total_a, total_b = total_a + part_a[...], total_b + part_b[...]
    inverse_a = inverse_norm(total_a).T[:, 0:1]
    inverse_b = inverse_norm(total_b).T[:, 1:2]
    half = b_low.shape[1]
    out_ref[:, :half] = a_ref[:, :half] * inverse_a + b_low[...] * inverse_b
    out_ref[:, half:] = a_ref[:, half:] * inverse_a + b_high[...] * inverse_b


def swap(block, axis, bit):
    return lax.ppermute(block, axis, [(i, i ^ bit) for i in range(lax.axis_size(axis))])


def everyone(block, axis):
    return [block] + [swap(block, axis, bits) for bits in range(1, lax.axis_size(axis))]


def chip_totals(keep, send):
    beside = swap(send, "ctx", 1)
    return beside, keep + beside


def first_phase(chip):
    return lax.ppermute(chip, "ctx", [(i, i ^ (2 if i % 2 == 0 else 4)) for i in range(8)])


def second_phase(message):
    return lax.ppermute(message, "ctx", [(i, i ^ (4 if i % 2 == 0 else 2)) for i in range(8)])


def doubled_prefix(chip):
    index = lax.axis_index("ctx")
    earlier = jnp.zeros_like(chip)
    running = chip
    bit = 2
    while bit < lax.axis_size("ctx"):
        partner = swap(running, "ctx", bit)
        earlier = earlier + jnp.where((index & bit) != 0, partner, 0.0)
        running = running + partner
        bit *= 2
    return earlier


def shards(queries, keys, values, head_gain):
    rows, width = queries.shape
    heads = head_gain.shape[1]
    steps = heads // 2
    parts = lax.axis_size("head")
    tail_k = keys[rows - WINDOW :]
    queries, keys, values = (
        pltpu.with_memory_space_constraint(x, pltpu.HBM) for x in (queries, keys, values)
    )
    smem = pl.BlockSpec(memory_space=pltpu.SMEM)
    anywhere = pl.BlockSpec(memory_space=pl.ANY)
    whole = pl.BlockSpec((rows, 2 * HD), lambda i: (0, i))
    whole_four = pl.BlockSpec((rows, 4 * HD), lambda i: (0, i))
    top_four = pl.BlockSpec((WINDOW, 4 * HD), lambda i: (0, i))
    doubled = pl.BlockSpec((rows, 4 * HD), lambda i: (0, i))
    state_pair = pl.BlockSpec((2, HD, HD), lambda i: (i, 0, 0))
    state_four = pl.BlockSpec((4, HD, HD), lambda i: (i, 0, 0))
    sums_block = pl.BlockSpec((8, rows), lambda i: (0, 0))
    first_sums_block = pl.BlockSpec((8, WINDOW), lambda i: (0, 0))

    def array(*shape):
        return jax.ShapeDtypeStruct(shape, F32)

    def call(kernel, name, flops, moved, **kwargs):
        return pl.pallas_call(
            kernel,
            name=name,
            compiler_params=pltpu.CompilerParams(vmem_limit_bytes=VMEM_BYTES),
            cost_estimate=pl.CostEstimate(flops=flops, bytes_accessed=moved, transcendentals=0),
            **kwargs,
        )

    size = rows * width * 4
    unit = 2 * rows * width * HD
    packed = array(steps, HD, HD)
    route = [(i, i + 1) for i in range(lax.axis_size("ctx") - 1)]
    before_k = lax.ppermute(tail_k, "ctx", route)

    keep, send, half, tail_v = call(
        totals_kernel,
        "totals",
        4 * unit,
        2 * size,
        grid=(heads // 4,),
        in_specs=[whole_four, whole_four],
        out_specs=[state_pair, state_pair, state_four, top_four],
        out_shape=[packed, packed, array(heads, HD, HD), array(WINDOW, width)],
    )(keys, values)
    beside, chip = chip_totals(keep, send)

    first_weights, first_now = call(
        first_weights_kernel,
        "first_weights",
        4 * unit,
        size,
        grid=(heads // 4,),
        in_specs=[smem] + [top_four] * 4,
        out_specs=[pl.BlockSpec((WINDOW, 8 * HD), lambda i: (0, i)), top_four],
        out_shape=[jax.ShapeDtypeStruct((WINDOW, 2 * width), BF16), array(WINDOW, width)],
    )(head_gain, queries, keys, values, before_k)

    def local(begin, count, *after):
        block = pl.BlockSpec((rows, 2 * HD), lambda i: (0, i + begin))
        taken = 2 * count * HD
        return call(
            functools.partial(local_kernel, 2 * begin, len(after)),
            "local",
            3 * count * unit // 2,
            5 * size * count // steps,
            grid=(count,),
            in_specs=[smem, block, block, block] + [anywhere] * len(after),
            out_specs=[whole, whole, doubled, sums_block],
            out_shape=[
                array(rows, taken),
                array(rows, taken),
                jax.ShapeDtypeStruct((rows, 2 * taken), BF16),
                array(8, rows),
            ],
            scratch_shapes=[pltpu.VMEM((rows, HD), F32)],
        )(head_gain, queries, keys, values, *after)

    low_steps = 3 * steps // 8
    window_low, linear_low, qq_low, sum_low = local(0, low_steps, first_now)
    window_high, linear_high, qq_high, sum_high = local(low_steps, steps - low_steps)

    if lax.axis_size("ctx") == 8:
        first = first_phase(chip)
        message, tail_v = call(
            message_kernel,
            "message",
            0,
            size // 4,
            in_specs=[pl.BlockSpec(), pl.BlockSpec(), anywhere, anywhere],
            out_specs=[pl.BlockSpec(), anywhere],
            out_shape=[packed, array(WINDOW, width)],
            input_output_aliases={3: 1},
        )(first, chip, sum_low, tail_v)
        second = second_phase(message)
        mine, other = call(
            prefix_kernel,
            "prefix",
            0,
            size // 2,
            in_specs=[pl.BlockSpec()] * 4 + [anywhere],
            out_shape=[packed, packed],
        )(first, second, keep, beside, sum_high)
    else:
        earlier = doubled_prefix(chip)
        core = lax.axis_index("ctx") % 2
        mine = earlier + jnp.where(core == 1, beside, 0.0)
        other = earlier + jnp.where(core == 0, keep, 0.0)
    before_v = lax.ppermute(tail_v, "ctx", route)
    other = swap(other, "ctx", 1)

    linear_low, linear_high, sums = call(
        earlier_kernel,
        "earlier",
        3 * unit,
        3 * size,
        in_specs=[smem] + [pl.BlockSpec()] * 9,
        out_shape=[array(*linear_low.shape), array(*linear_high.shape), array(8, rows)],
        scratch_shapes=[pltpu.VMEM((rows, HD), F32)],
    )(head_gain, qq_low, linear_low, qq_high, linear_high, half, mine, other, sum_low, sum_high)
    all_sums = everyone(sums, "head")

    first_a, first_sum = call(
        first_values_kernel,
        "first_values",
        unit,
        size // 2,
        out_shape=[array(WINDOW, width), array(8, WINDOW)],
    )(first_weights, first_now, before_v)
    all_first = everyone(first_sum, "head")

    row_block = pl.BlockSpec((WINDOW, width), lambda i: (i + 1, 0))
    row_parts = [pl.BlockSpec((WINDOW, x.shape[1]), lambda i: (i + 1, 0)) for x in (window_low, window_high)]
    first_block = pl.BlockSpec((WINDOW, width), lambda i: (0, 0))
    first_parts = [pl.BlockSpec((WINDOW, x.shape[1]), lambda i: (0, 0)) for x in (window_low, window_high)]
    out = call(
        functools.partial(scale_kernel, parts),
        "scale",
        unit // 64,
        2 * size,
        grid=(rows // WINDOW - 1,),
        in_specs=[pl.BlockSpec((8, WINDOW), lambda i: (0, i + 1))] * parts + row_parts * 2,
        out_specs=row_block,
        out_shape=array(rows, width),
    )(*all_sums, window_low, window_high, linear_low, linear_high)
    return call(
        functools.partial(first_scale_kernel, parts),
        "first_scale",
        unit // 256,
        size // 2,
        grid=(1,),
        in_specs=[first_sums_block] * (2 * parts) + [first_block, *first_parts, anywhere],
        out_specs=first_block,
        out_shape=array(rows, width),
        input_output_aliases={2 * parts + 3: 0},
    )(*all_sums, *all_first, first_a, linear_low, linear_high, out)


def solution(mesh):
    in_specs = (P("ctx", "head"), P("ctx", "head"), P("ctx", "head"), P(None, "head"))
    out_specs = P("ctx", "head")
    return jax.shard_map(shards, mesh=mesh, in_specs=in_specs, out_specs=out_specs, check_vma=False)
```

```python
import functools
import math

import jax
import jax.numpy as jnp
from jax import lax
from jax.experimental import pallas as pl
from jax.experimental.pallas import tpu as pltpu
from jax.sharding import PartitionSpec as P

HEADS = 64
HD = 128
WINDOW = 128
EPS = 1e-06
F32 = jnp.float32
BF16 = jnp.bfloat16
EXP2_SCALE = math.log2(math.e) / math.sqrt(HD)
VMEM_BYTES = 20 * 1024 * 1024
GROUP = 4


def halves(x):
    high = x.astype(BF16)
    low = (x - high.astype(F32)).astype(BF16)
    return high, low


def dot(a, b):
    return lax.dot_general(a, b, (((1,), (0,)), ((), ())), preferred_element_type=F32)


def dot_rows(a, b):
    return lax.dot_general(a, b, (((1,), (1,)), ((), ())), preferred_element_type=F32)


def dot_columns(a, b):
    return lax.dot_general(a, b, (((0,), (0,)), ((), ())), preferred_element_type=F32)


def side(a, b):
    return jnp.concatenate([a, b], axis=1)


def stack(a, b):
    return jnp.concatenate([a, b], axis=0)


def outer_state(k_high, k_low, v_high, v_low):
    grid = dot_columns(side(k_high, k_low), side(v_high, v_low))
    return grid[:HD, :HD] + (grid[:HD, HD:] + grid[HD:, :HD]) + grid[HD:, HD:]


def lower_mask():
    rows = lax.broadcasted_iota(jnp.int32, (WINDOW, WINDOW), 0)
    columns = lax.broadcasted_iota(jnp.int32, (WINDOW, WINDOW), 1)
    return rows >= columns


def row_sums(square):
    ones = jnp.ones((8, HD), BF16)
    high, low = halves(square)
    return dot_rows(ones, high) + dot_rows(ones, low)


def wide_keys(k_high, k_low):
    return stack(side(k_high, k_high), side(k_low, jnp.zeros_like(k_low)))


def wide_state(state):
    high, low = halves(state)
    return stack(side(high, low), side(high, jnp.zeros_like(high)))


def folded(wide):
    half = wide.shape[1] // 2
    return wide[:, :half] + wide[:, half:]


def head_columns(head, count=1, width=HD):
    return pl.ds(pl.multiple_of(head * width, width), count * width)


def tails_kernel(k_ref, v_ref, tail_k_ref, tail_v_ref, sems):
    rows = k_ref.shape[0]
    copies = [
        pltpu.make_async_copy(source.at[pl.ds(rows - WINDOW, WINDOW), :], target, sems.at[i])
        for i, (source, target) in enumerate(((k_ref, tail_k_ref), (v_ref, tail_v_ref)))
    ]
    for copy in copies:
        copy.start()
    for copy in copies:
        copy.wait()


def totals_kernel(k_hbm, v_hbm, keep_ref, send_ref, half_ref, k_ref, v_ref, sems):
    core = lax.axis_index("ctx") % 2
    rows, width = k_ref.shape
    middle = rows // 2
    groups = width // (GROUP * HD)

    def copies(group):
        columns = head_columns(group, 1, GROUP * HD)
        return [
            pltpu.make_async_copy(source.at[:, columns], target.at[:, columns], sems.at[i, group])
            for i, (source, target) in enumerate(((k_hbm, k_ref), (v_hbm, v_ref)))
        ]

    for group in range(groups):
        for copy in copies(group):
            copy.start()

    @pl.loop(0, groups)
    def _(group):
        for copy in copies(group):
            copy.wait()
        for i in range(GROUP // 2):
            states = []
            for j in (2 * i, 2 * i + 1):
                head = GROUP * group + j
                columns = head_columns(head)
                k_high, k_low = halves(k_ref[:, columns])
                v_high, v_low = halves(v_ref[:, columns])
                first = outer_state(k_high[:middle], k_low[:middle], v_high[:middle], v_low[:middle])
                second = outer_state(k_high[middle:], k_low[middle:], v_high[middle:], v_low[middle:])
                half_ref[head] = first
                states.append(first + second)
            pair = GROUP // 2 * group + i
            keep_ref[pair] = jnp.where(core == 0, states[0], states[1])
            send_ref[pair] = jnp.where(core == 0, states[1], states[0])


def weights_of(scores):
    biggest = jnp.max(scores, axis=1, keepdims=True)
    weights = jnp.exp2((scores - biggest) * EXP2_SCALE)
    return weights, jnp.sum(weights, axis=1, keepdims=True)


def masked_pair(weights, below, above):
    high, low = halves(weights)
    return side(high * above, high * below), side(low * above, low * below)


def local_kernel(begin, gain_ref, q_hbm, k_ref, v_ref, *refs):
    a_ref, b_ref, qq_ref, sum_ref, q_ref, square_ref, sems = refs[-7:]
    lower = lower_mask()
    below = jnp.where(lower, 1.0, 0.0).astype(BF16)
    above = jnp.where(lower, 0.0, 1.0).astype(BF16)
    rows, width = a_ref.shape
    tiles = rows // WINDOW
    groups = width // (GROUP * HD)

    def load(group):
        source = pl.ds(pl.multiple_of(begin * HD + group * (GROUP * HD), HD), GROUP * HD)
        target = head_columns(group, 1, GROUP * HD)
        return pltpu.make_async_copy(q_hbm.at[:, source], q_ref.at[:, target], sems.at[group])

    for group in range(groups):
        load(group).start()
    square_ref[...] = jnp.zeros_like(square_ref)

    def tile(n):
        return slice(n * WINDOW, (n + 1) * WINDOW)

    @pl.loop(0, groups)
    def _(group):
        load(group).wait()
        scores = []
        for j in range(GROUP):
            head = GROUP * group + j
            qq = side(*halves(q_ref[:, head_columns(head)]))
            qq_ref[:, head_columns(head, 1, 2 * HD)] = qq
            k_high, k_low = halves(k_ref[:, head_columns(begin + head)])
            now, before = [], [None]
            for n in range(tiles):
                keys = wide_keys(k_high[tile(n)], k_low[tile(n)])
                found = folded(dot_rows(qq[n * WINDOW : min((n + 2) * WINDOW, rows)], keys))
                now.append(found[:WINDOW])
                before.append(found[WINDOW:])
            scores.append((now, before))
        for j in range(GROUP):
            head = GROUP * group + j
            columns = head_columns(head)
            vv = side(*halves(v_ref[:, head_columns(begin + head)]))
            now, before = scores[j]
            gain_a = gain_ref[0, begin + head]
            for n in range(tiles):
                inner_high, inner_low = halves(jnp.where(lower, now[n], 0.0))
                if n == 0:
                    wide = dot(stack(inner_high, inner_low), vv[tile(0)])
                    b_ref[tile(0), columns] = folded(wide[:WINDOW]) + wide[WINDOW:, :HD]
                    a_ref[tile(0), columns] = jnp.zeros((WINDOW, HD), F32)
                    continue
                weights, total = weights_of(jnp.where(lower, now[n], before[n]))
                pair_high, pair_low = masked_pair(weights, below, above)
                if n % 2:
                    before_high, before_low = halves(before[n])
                else:
                    before_high = before_low = jnp.zeros((WINDOW, HD), BF16)
                left = jnp.concatenate(
                    [pair_high, pair_low, side(before_high, inner_high), side(before_low, inner_low)], axis=0
                )
                wide = dot(left, vv[(n - 1) * WINDOW : (n + 1) * WINDOW])
                a = (folded(wide[tile(0)]) + wide[tile(1), :HD]) * (gain_a / total)
                a_ref[tile(n), columns] = a
                square_ref[tile(n), :] += a * a
                b_ref[tile(n), columns] = folded(wide[tile(2)]) + wide[tile(3), :HD]

    sum_ref[...] = row_sums(square_ref[...])


def message_kernel(first_ref, chip_ref, *refs):
    out_ref = refs[-2]
    index = lax.axis_index("ctx")
    core, x, y = index % 2, (index >> 1) % 2, index >> 2
    first = jnp.where((core == 0) | (y == 1), first_ref[...], 0.0)
    out_ref[...] = first + jnp.where((core == 0) | (x == 0), chip_ref[...], 0.0)


def prefix_kernel(first_ref, second_ref, keep_ref, beside_ref, *refs):
    mine_ref, other_ref = refs[-2:]
    index = lax.axis_index("ctx")
    core, x, y = index % 2, (index >> 1) % 2, index >> 2
    use_first = jnp.where(core == 0, x, y) == 1
    use_second = (core == 1) & ((x == 1) | (y == 1)) | (core == 0) & (y == 1)
    earlier = jnp.where(use_first, first_ref[...], 0.0) + jnp.where(use_second, second_ref[...], 0.0)
    mine_ref[...] = earlier + jnp.where(core == 1, beside_ref[...], 0.0)
    other_ref[...] = earlier + jnp.where(core == 0, keep_ref[...], 0.0)


def earlier_kernel(gain_ref, *refs):
    parts, (half_ref, mine_ref, other_ref, sum_low_ref, sum_high_ref), outs = refs[:4], refs[4:9], refs[9:]
    sums_ref, square_ref = outs[2:]
    core = lax.axis_index("ctx") % 2
    rows = parts[1].shape[0]
    middle = rows // 2
    begin = 0
    square_ref[...] = jnp.zeros_like(square_ref)
    for side_number in range(2):
        qq_ref, b_ref = parts[2 * side_number : 2 * side_number + 2]
        out_ref = outs[side_number]
        for j in range(b_ref.shape[1] // HD):
            head = begin + j
            columns = slice(j * HD, (j + 1) * HD)
            state = jnp.where(core == head % 2, mine_ref[head // 2], other_ref[head // 2])
            gain_b = gain_ref[1, head]
            for part, held in ((slice(0, middle), state), (slice(middle, rows), state + half_ref[head])):
                qq = qq_ref[part, 2 * j * HD : 2 * (j + 1) * HD]
                b = gain_b * (b_ref[part, columns] + folded(dot(qq, wide_state(held))))
                out_ref[part, columns] = b
                square_ref[part, :] += b * b
        begin += b_ref.shape[1] // HD
    own = row_sums(square_ref[...])
    row = lax.broadcasted_iota(jnp.int32, own.shape, 0)
    own = jnp.where(row == 0, sum_low_ref[...] + sum_high_ref[...], own)
    for i in range(sums_ref.shape[0]):
        sums_ref[i] = own


def first_weights_kernel(gain_ref, qq_low_ref, qq_high_ref, k_ref, v_ref, tail_k_ref, weights_ref, out_ref):
    lower = lower_mask()
    reachable = jnp.logical_or(lower, lax.axis_index("ctx") > 0)
    top = slice(0, WINDOW)
    begin = 0
    for qq_ref in (qq_low_ref, qq_high_ref):
        count = qq_ref.shape[1] // (2 * HD)

        @pl.loop(0, count // GROUP)
        def _(group):
            scores = []
            for j in range(GROUP):
                head = GROUP * group + j
                columns = head_columns(begin + head)
                qq = qq_ref[top, head_columns(head, 1, 2 * HD)]
                now = folded(dot_rows(qq, wide_keys(*halves(k_ref[top, columns]))))
                before = folded(dot_rows(qq, wide_keys(*halves(tail_k_ref[:, columns]))))
                scores.append(jnp.where(reachable, jnp.where(lower, now, before), -jnp.inf))
            for j in range(GROUP):
                head = begin + GROUP * group + j
                columns = head_columns(head)
                weights, total = weights_of(scores[j])
                weights = weights * (gain_ref[0, head] / total)
                now_high, now_low = halves(jnp.where(lower, weights, 0.0))
                vv = side(*halves(v_ref[top, columns]))
                wide = dot(stack(now_high, now_low), vv)
                out_ref[:, columns] = folded(wide[:WINDOW]) + wide[WINDOW:, :HD]
                weights_ref[:, head_columns(head, 1, 2 * HD)] = side(*halves(jnp.where(lower, 0.0, weights)))

        begin += count


def first_values_kernel(weights_ref, now_ref, tail_v_ref, _, a_ref, sums_ref):
    square = jnp.zeros((WINDOW, HD), F32)
    for j in range(now_ref.shape[1] // HD):
        columns = slice(j * HD, (j + 1) * HD)
        high = weights_ref[:, 2 * j * HD : (2 * j + 1) * HD]
        low = weights_ref[:, (2 * j + 1) * HD : 2 * (j + 1) * HD]
        wide = dot(stack(high, low), side(*halves(tail_v_ref[:, columns])))
        a = now_ref[:, columns] + (folded(wide[:WINDOW]) + wide[WINDOW:, :HD])
        a_ref[:, columns] = a
        square = square + a * a
    own = row_sums(square)
    for i in range(sums_ref.shape[0]):
        sums_ref[i] = own


def inverse_norm(total):
    return 1.0 / jnp.sqrt(total / (HEADS * HD) + EPS)


def scale_kernel(sums_ref, a_low, a_high, b_low, b_high, out_hbm, written_ref, out_ref, sems):
    inverse = inverse_norm(jnp.sum(sums_ref[...], axis=0)).T
    middle = a_low.shape[1]
    written_ref[...] = inverse[:8]
    copies = []
    for n in range(out_ref.shape[0] // WINDOW):
        held = slice(n * WINDOW, (n + 1) * WINDOW)
        rows = slice((n + 1) * WINDOW, (n + 2) * WINDOW)
        inverse_a, inverse_b = inverse[rows, 0:1], inverse[rows, 1:2]
        out_ref[held, :middle] = a_low[rows, :] * inverse_a + b_low[rows, :] * inverse_b
        out_ref[held, middle:] = a_high[rows, :] * inverse_a + b_high[rows, :] * inverse_b
        copy = pltpu.make_async_copy(out_ref.at[held, :], out_hbm.at[rows, :], sems.at[n])
        copy.start()
        copies.append(copy)
    for copy in copies:
        copy.wait()


def first_scale_kernel(sums_b_ref, sums_a_ref, a_ref, b_low, b_high, _, out_hbm, out_ref, sems):
    inverse_a = inverse_norm(jnp.sum(sums_a_ref[...], axis=0)).T[:, 0:1]
    inverse_b = inverse_norm(jnp.sum(sums_b_ref[:, :, :WINDOW], axis=0)).T[:, 1:2]
    middle = b_low.shape[1]
    copies = []
    for n in range(sems.shape[0]):
        rows = slice(n * WINDOW // sems.shape[0], (n + 1) * WINDOW // sems.shape[0])
        scale_a, scale_b = inverse_a[rows], inverse_b[rows]
        out_ref[rows, :middle] = a_ref[rows, :middle] * scale_a + b_low[rows, :] * scale_b
        out_ref[rows, middle:] = a_ref[rows, middle:] * scale_a + b_high[rows, :] * scale_b
        copy = pltpu.make_async_copy(out_ref.at[rows, :], out_hbm.at[rows, :], sems.at[n])
        copy.start()
        copies.append(copy)
    for copy in copies:
        copy.wait()


def swap(block, axis, bit):
    return lax.ppermute(block, axis, [(i, i ^ bit) for i in range(lax.axis_size(axis))])


def chip_totals(keep, send):
    beside = swap(send, "ctx", 1)
    return beside, keep + beside


def first_phase(chip):
    return lax.ppermute(chip, "ctx", [(i, i ^ (2 if i % 2 == 0 else 4)) for i in range(8)])


def second_phase(message):
    return lax.ppermute(message, "ctx", [(i, i ^ (4 if i % 2 == 0 else 2)) for i in range(8)])


def doubled_prefix(chip):
    index = lax.axis_index("ctx")
    earlier = jnp.zeros_like(chip)
    running = chip
    bit = 2
    while bit < lax.axis_size("ctx"):
        partner = swap(running, "ctx", bit)
        earlier = earlier + jnp.where((index & bit) != 0, partner, 0.0)
        running = running + partner
        bit *= 2
    return earlier


def shards(queries, keys, values, head_gain):
    rows, width = queries.shape
    heads = head_gain.shape[1]
    parts = lax.axis_size("head")
    queries, keys, values = (
        pltpu.with_memory_space_constraint(x, pltpu.HBM) for x in (queries, keys, values)
    )
    smem = pl.BlockSpec(memory_space=pltpu.SMEM)
    anywhere = pl.BlockSpec(memory_space=pl.ANY)
    vmem = pl.BlockSpec()

    def array(*shape, dtype=F32):
        return jax.ShapeDtypeStruct(shape, dtype)

    def call(kernel, name, flops, moved, **kwargs):
        return pl.pallas_call(
            kernel,
            name=name,
            compiler_params=pltpu.CompilerParams(vmem_limit_bytes=VMEM_BYTES),
            cost_estimate=pl.CostEstimate(flops=flops, bytes_accessed=moved, transcendentals=0),
            **kwargs,
        )

    size = rows * width * 4
    unit = 2 * rows * width * HD
    packed = array(heads // 2, HD, HD)
    first_tile = array(WINDOW, width)
    dma = pltpu.SemaphoreType.DMA
    tail_k, tail_v = call(
        tails_kernel,
        "tails",
        0,
        size,
        in_specs=[anywhere, anywhere],
        out_shape=[first_tile, first_tile],
        scratch_shapes=[dma((2,))],
    )(keys, values)
    route = [(i, i + 1) for i in range(lax.axis_size("ctx") - 1)]
    before_k = lax.ppermute(tail_k, "ctx", route)

    keep, send, half, held_k, held_v = call(
        totals_kernel,
        "totals",
        4 * unit,
        2 * size,
        in_specs=[anywhere, anywhere],
        out_shape=[packed, packed, array(heads, HD, HD), array(rows, width), array(rows, width)],
        scratch_shapes=[dma((2, heads // GROUP))],
    )(keys, values)
    beside, chip = chip_totals(keep, send)

    def local(begin, count, *after):
        taken = count * HD
        return call(
            functools.partial(local_kernel, begin),
            "local",
            count * unit,
            4 * size * count // heads,
            in_specs=[smem, anywhere, vmem, vmem] + [anywhere] * len(after),
            out_shape=[
                array(rows, taken),
                array(rows, taken),
                array(rows, 2 * taken, dtype=BF16),
                array(8, rows),
            ],
            scratch_shapes=[
                pltpu.VMEM((rows, taken), F32),
                pltpu.VMEM((rows, HD), F32),
                dma((count // GROUP,)),
            ],
        )(head_gain, queries, held_k, held_v, *after)

    low_heads = heads // 8 * 4
    window_low, linear_low, qq_low, sum_low = local(0, low_heads, before_k)
    window_high, linear_high, qq_high, sum_high = local(low_heads, heads - low_heads)
    first_weights, first_now = call(
        first_weights_kernel,
        "first_weights",
        4 * unit,
        size,
        in_specs=[smem] + [vmem] * 5,
        out_shape=[array(WINDOW, 2 * width, dtype=BF16), first_tile],
    )(head_gain, qq_low, qq_high, held_k, held_v, before_k)

    if lax.axis_size("ctx") == 8:
        first = first_phase(chip)
        message, tail_v = call(
            message_kernel,
            "message",
            0,
            size // 4,
            in_specs=[vmem, vmem, anywhere, anywhere],
            out_specs=[vmem, anywhere],
            out_shape=[packed, first_tile],
            input_output_aliases={3: 1},
        )(first, chip, sum_low, tail_v)
        second = second_phase(message)
        mine, other = call(
            prefix_kernel,
            "prefix",
            0,
            size // 2,
            in_specs=[vmem] * 4 + [anywhere],
            out_shape=[packed, packed],
        )(first, second, keep, beside, first_now)
    else:
        earlier = doubled_prefix(chip)
        core = lax.axis_index("ctx") % 2
        mine = earlier + jnp.where(core == 1, beside, 0.0)
        other = earlier + jnp.where(core == 0, keep, 0.0)
    before_v = lax.ppermute(tail_v, "ctx", route)
    other = swap(other, "ctx", 1)

    linear_low, linear_high, sums = call(
        earlier_kernel,
        "earlier",
        3 * unit,
        3 * size,
        in_specs=[smem] + [vmem] * 9,
        out_shape=[array(*linear_low.shape), array(*linear_high.shape), array(parts, 8, rows)],
        scratch_shapes=[pltpu.VMEM((rows, HD), F32)],
    )(head_gain, qq_low, linear_low, qq_high, linear_high, half, mine, other, sum_low, sum_high)
    sums = lax.all_to_all(sums, "head", 0, 0)

    out, written = call(
        scale_kernel,
        "scale",
        unit // 64,
        2 * size,
        out_specs=[anywhere, vmem],
        out_shape=[array(rows, width), array(8, 8)],
        scratch_shapes=[pltpu.VMEM((rows - WINDOW, width), F32), dma((rows // WINDOW - 1,))],
    )(sums, window_low, window_high, linear_low, linear_high)

    first_a, first_sums = call(
        first_values_kernel,
        "first_values",
        unit,
        size // 2,
        in_specs=[vmem] * 3 + [anywhere],
        out_shape=[first_tile, array(parts, 8, WINDOW)],
    )(first_weights, first_now, before_v, written)
    first_sums = lax.all_to_all(first_sums, "head", 0, 0)
    return call(
        first_scale_kernel,
        "first_scale",
        unit // 256,
        size // 2,
        in_specs=[vmem] * 5 + [anywhere],
        out_specs=anywhere,
        out_shape=array(rows, width),
        scratch_shapes=[pltpu.VMEM((WINDOW, width), F32), dma((4,))],
        input_output_aliases={5: 0},
    )(sums, first_sums, first_a, linear_low, linear_high, out)


def solution(mesh):
    in_specs = (P("ctx", "head"), P("ctx", "head"), P("ctx", "head"), P(None, "head"))
    out_specs = P("ctx", "head")
    return jax.shard_map(shards, mesh=mesh, in_specs=in_specs, out_specs=out_specs, check_vma=False)
```

```python
import functools
import math

import jax
import jax.numpy as jnp
from jax import lax
from jax.experimental import pallas as pl
from jax.experimental.pallas import tpu as pltpu
from jax.sharding import PartitionSpec as P

HEADS = 64
HD = 128
WINDOW = 128
EPS = 1e-06
F32 = jnp.float32
BF16 = jnp.bfloat16
EXP2_SCALE = math.log2(math.e) / math.sqrt(HD)
VMEM_BYTES = 20 * 1024 * 1024
GROUP = 4


def halves(x):
    high = x.astype(BF16)
    low = (x - high.astype(F32)).astype(BF16)
    return high, low


def dot(a, b):
    return lax.dot_general(a, b, (((1,), (0,)), ((), ())), preferred_element_type=F32)


def dot_rows(a, b):
    return lax.dot_general(a, b, (((1,), (1,)), ((), ())), preferred_element_type=F32)


def dot_columns(a, b):
    return lax.dot_general(a, b, (((0,), (0,)), ((), ())), preferred_element_type=F32)


def side(a, b):
    return jnp.concatenate([a, b], axis=1)


def stack(a, b):
    return jnp.concatenate([a, b], axis=0)


def outer_state(k_high, k_low, v_high, v_low):
    grid = dot_columns(side(k_high, k_low), side(v_high, v_low))
    return grid[:HD, :HD] + (grid[:HD, HD:] + grid[HD:, :HD]) + grid[HD:, HD:]


def lower_mask():
    rows = lax.broadcasted_iota(jnp.int32, (WINDOW, WINDOW), 0)
    columns = lax.broadcasted_iota(jnp.int32, (WINDOW, WINDOW), 1)
    return rows >= columns


def row_sums(square):
    ones = jnp.ones((8, HD), BF16)
    high, low = halves(square)
    return dot_rows(ones, high) + dot_rows(ones, low)


def wide_keys(k_high, k_low):
    return stack(side(k_high, k_high), side(k_low, jnp.zeros_like(k_low)))


def wide_state(state):
    high, low = halves(state)
    return stack(side(high, low), side(high, jnp.zeros_like(high)))


def folded(wide):
    half = wide.shape[1] // 2
    return wide[:, :half] + wide[:, half:]


def head_columns(head, count=1, width=HD):
    return pl.ds(pl.multiple_of(head * width, width), count * width)


def tail_kernel(k_ref, tail_ref, sem):
    rows = k_ref.shape[0]
    copy = pltpu.make_async_copy(k_ref.at[pl.ds(rows - WINDOW, WINDOW), :], tail_ref, sem)
    copy.start()
    copy.wait()


def totals_kernel(k_hbm, v_hbm, keep_ref, send_ref, half_ref, k_ref, v_ref, tail_v_ref, sems):
    core = lax.axis_index("ctx") % 2
    rows, width = k_ref.shape
    middle = rows // 2
    groups = width // (GROUP * HD)

    def copies(group):
        columns = head_columns(group, 1, GROUP * HD)
        return [
            pltpu.make_async_copy(source.at[:, columns], target.at[:, columns], sems.at[i, group])
            for i, (source, target) in enumerate(((k_hbm, k_ref), (v_hbm, v_ref)))
        ]

    for group in range(groups):
        for copy in copies(group):
            copy.start()

    @pl.loop(0, groups)
    def _(group):
        for copy in copies(group):
            copy.wait()
        for i in range(GROUP // 2):
            states = []
            for j in (2 * i, 2 * i + 1):
                head = GROUP * group + j
                columns = head_columns(head)
                k_high, k_low = halves(k_ref[:, columns])
                v_high, v_low = halves(v_ref[:, columns])
                first = outer_state(k_high[:middle], k_low[:middle], v_high[:middle], v_low[:middle])
                second = outer_state(k_high[middle:], k_low[middle:], v_high[middle:], v_low[middle:])
                half_ref[head] = first
                states.append(first + second)
            pair = GROUP // 2 * group + i
            keep_ref[pair] = jnp.where(core == 0, states[0], states[1])
            send_ref[pair] = jnp.where(core == 0, states[1], states[0])
        columns = head_columns(group, 1, GROUP * HD)
        tail_v_ref[:, columns] = v_ref[rows - WINDOW :, columns]


def weights_of(scores):
    biggest = jnp.max(scores, axis=1, keepdims=True)
    weights = jnp.exp2((scores - biggest) * EXP2_SCALE)
    return weights, jnp.sum(weights, axis=1, keepdims=True)


def masked_pair(weights, below, above):
    high, low = halves(weights)
    return side(high * above, high * below), side(low * above, low * below)


def local_kernel(begin, extra, gain_ref, q_hbm, k_ref, v_ref, *refs):
    a_ref, b_ref, qq_ref, sum_ref = refs[extra : extra + 4]
    q_ref, square_ref, sems = refs[-3:]
    lower = lower_mask()
    below = jnp.where(lower, 1.0, 0.0).astype(BF16)
    above = jnp.where(lower, 0.0, 1.0).astype(BF16)
    rows, width = a_ref.shape
    tiles = rows // WINDOW
    groups = width // (GROUP * HD)

    def load(group):
        source = pl.ds(pl.multiple_of(begin * HD + group * (GROUP * HD), HD), GROUP * HD)
        target = head_columns(group, 1, GROUP * HD)
        return pltpu.make_async_copy(q_hbm.at[:, source], q_ref.at[:, target], sems.at[group])

    for group in range(groups):
        load(group).start()
    square_ref[...] = jnp.zeros_like(square_ref)

    def tile(n):
        return slice(n * WINDOW, (n + 1) * WINDOW)

    @pl.loop(0, groups)
    def _(group):
        load(group).wait()
        scores = []
        for j in range(GROUP):
            head = GROUP * group + j
            qq = side(*halves(q_ref[:, head_columns(head)]))
            qq_ref[:, head_columns(head, 1, 2 * HD)] = qq
            k_high, k_low = halves(k_ref[:, head_columns(begin + head)])
            now, before = [], [None]
            for n in range(tiles):
                keys = wide_keys(k_high[tile(n)], k_low[tile(n)])
                found = folded(dot_rows(qq[n * WINDOW : min((n + 2) * WINDOW, rows)], keys))
                now.append(found[:WINDOW])
                before.append(found[WINDOW:])
            scores.append((now, before))
        for j in range(GROUP):
            head = GROUP * group + j
            columns = head_columns(head)
            vv = side(*halves(v_ref[:, head_columns(begin + head)]))
            now, before = scores[j]
            gain_a = gain_ref[0, begin + head]
            for n in range(tiles):
                inner_high, inner_low = halves(jnp.where(lower, now[n], 0.0))
                if n == 0:
                    wide = dot(stack(inner_high, inner_low), vv[tile(0)])
                    b_ref[tile(0), columns] = folded(wide[:WINDOW]) + wide[WINDOW:, :HD]
                    a_ref[tile(0), columns] = jnp.zeros((WINDOW, HD), F32)
                    continue
                weights, total = weights_of(jnp.where(lower, now[n], before[n]))
                pair_high, pair_low = masked_pair(weights, below, above)
                if n % 2:
                    before_high, before_low = halves(before[n])
                else:
                    before_high = before_low = jnp.zeros((WINDOW, HD), BF16)
                left = jnp.concatenate(
                    [pair_high, pair_low, side(before_high, inner_high), side(before_low, inner_low)], axis=0
                )
                wide = dot(left, vv[(n - 1) * WINDOW : (n + 1) * WINDOW])
                a = (folded(wide[tile(0)]) + wide[tile(1), :HD]) * (gain_a / total)
                a_ref[tile(n), columns] = a
                square_ref[tile(n), :] += a * a
                b_ref[tile(n), columns] = folded(wide[tile(2)]) + wide[tile(3), :HD]

    sum_ref[...] = row_sums(square_ref[...])


def message_kernel(first_ref, chip_ref, _, out_ref):
    index = lax.axis_index("ctx")
    core, x, y = index % 2, (index >> 1) % 2, index >> 2
    first = jnp.where((core == 0) | (y == 1), first_ref[...], 0.0)
    out_ref[...] = first + jnp.where((core == 0) | (x == 0), chip_ref[...], 0.0)


def prefix_kernel(first_ref, second_ref, keep_ref, beside_ref, *refs):
    mine_ref, other_ref = refs[-2:]
    index = lax.axis_index("ctx")
    core, x, y = index % 2, (index >> 1) % 2, index >> 2
    use_first = jnp.where(core == 0, x, y) == 1
    use_second = (core == 1) & ((x == 1) | (y == 1)) | (core == 0) & (y == 1)
    earlier = jnp.where(use_first, first_ref[...], 0.0) + jnp.where(use_second, second_ref[...], 0.0)
    mine_ref[...] = earlier + jnp.where(core == 1, beside_ref[...], 0.0)
    other_ref[...] = earlier + jnp.where(core == 0, keep_ref[...], 0.0)


def earlier_kernel(count, gain_ref, half_ref, mine_ref, other_ref, *refs):
    qq_refs, b_refs, sum_refs, out_refs = (refs[i * count : (i + 1) * count] for i in range(4))
    sums_ref, square_ref = refs[4 * count :]
    core = lax.axis_index("ctx") % 2
    rows = b_refs[0].shape[0]
    middle = rows // 2
    head = 0
    square_ref[...] = jnp.zeros_like(square_ref)
    for qq_ref, b_ref, out_ref in zip(qq_refs, b_refs, out_refs):
        for j in range(b_ref.shape[1] // HD):
            columns = slice(j * HD, (j + 1) * HD)
            state = jnp.where(core == head % 2, mine_ref[head // 2], other_ref[head // 2])
            gain_b = gain_ref[1, head]
            for part, held in ((slice(0, middle), state), (slice(middle, rows), state + half_ref[head])):
                qq = qq_ref[part, 2 * j * HD : 2 * (j + 1) * HD]
                b = gain_b * (b_ref[part, columns] + folded(dot(qq, wide_state(held))))
                out_ref[part, columns] = b
                square_ref[part, :] += b * b
            head += 1
    sums = row_sums(square_ref[...])
    row = lax.broadcasted_iota(jnp.int32, sums.shape, 0)
    sums_ref[...] = jnp.where(row == 0, sum(ref[...] for ref in sum_refs), sums)


def first_weights_kernel(gain_ref, k_ref, v_ref, tail_k_ref, *refs):
    qq_refs, (weights_ref, out_ref) = refs[:-2], refs[-2:]
    lower = lower_mask()
    reachable = jnp.logical_or(lower, lax.axis_index("ctx") > 0)
    top = slice(0, WINDOW)
    begin = 0
    for qq_ref in qq_refs:
        count = qq_ref.shape[1] // (2 * HD)

        @pl.loop(0, count // GROUP)
        def _(group):
            scores = []
            for j in range(GROUP):
                head = GROUP * group + j
                columns = head_columns(begin + head)
                qq = qq_ref[top, head_columns(head, 1, 2 * HD)]
                now = folded(dot_rows(qq, wide_keys(*halves(k_ref[top, columns]))))
                before = folded(dot_rows(qq, wide_keys(*halves(tail_k_ref[:, columns]))))
                scores.append(jnp.where(reachable, jnp.where(lower, now, before), -jnp.inf))
            for j in range(GROUP):
                head = begin + GROUP * group + j
                columns = head_columns(head)
                weights, total = weights_of(scores[j])
                weights = weights * (gain_ref[0, head] / total)
                now_high, now_low = halves(jnp.where(lower, weights, 0.0))
                vv = side(*halves(v_ref[top, columns]))
                wide = dot(stack(now_high, now_low), vv)
                out_ref[:, columns] = folded(wide[:WINDOW]) + wide[WINDOW:, :HD]
                weights_ref[:, head_columns(head, 1, 2 * HD)] = side(*halves(jnp.where(lower, 0.0, weights)))

        begin += count


def first_values_kernel(weights_ref, now_ref, tail_v_ref, sums_ref, a_ref, out_ref):
    square = jnp.zeros((WINDOW, HD), F32)
    for j in range(now_ref.shape[1] // HD):
        columns = slice(j * HD, (j + 1) * HD)
        high = weights_ref[:, 2 * j * HD : (2 * j + 1) * HD]
        low = weights_ref[:, (2 * j + 1) * HD : 2 * (j + 1) * HD]
        wide = dot(stack(high, low), side(*halves(tail_v_ref[:, columns])))
        a = now_ref[:, columns] + (folded(wide[:WINDOW]) + wide[WINDOW:, :HD])
        a_ref[:, columns] = a
        square = square + a * a
    own = row_sums(square)
    row = lax.broadcasted_iota(jnp.int32, own.shape, 0)
    out_ref[:, :WINDOW] = jnp.where(row == 0, own, sums_ref[:, :WINDOW])
    out_ref[:, WINDOW:] = sums_ref[:, WINDOW:]


def inverse_norm(total):
    return 1.0 / jnp.sqrt(total / (HEADS * HD) + EPS)


def scale_kernel(count, sums, first_ref, *refs):
    a_refs, b_refs, (out_hbm, out_ref, sems) = refs[:count], refs[count : 2 * count], refs[2 * count :]
    total = sums[0][...]
    for part in sums[1:]:
        total = total + part[...]
    inverse = inverse_norm(total).T
    copies = []
    for n in range(out_ref.shape[0] // WINDOW):
        rows = slice(n * WINDOW, (n + 1) * WINDOW)
        inverse_a, inverse_b = inverse[rows, 0:1], inverse[rows, 1:2]
        begin = 0
        for a_ref, b_ref in zip(a_refs, b_refs):
            columns = slice(begin, begin + a_ref.shape[1])
            a = a_ref[rows, :] if n else first_ref[:, columns]
            out_ref[rows, columns] = a * inverse_a + b_ref[rows, :] * inverse_b
            begin = columns.stop
        copy = pltpu.make_async_copy(out_ref.at[rows, :], out_hbm.at[rows, :], sems.at[n])
        copy.start()
        copies.append(copy)
    for copy in copies:
        copy.wait()


def scale_first(parts, count, *refs):
    scale_kernel(count, refs[:parts], *refs[parts:])


def swap(block, axis, bit):
    return lax.ppermute(block, axis, [(i, i ^ bit) for i in range(lax.axis_size(axis))])


def chip_totals(keep, send):
    beside = swap(send, "ctx", 1)
    return beside, keep + beside


def first_phase(chip):
    return lax.ppermute(chip, "ctx", [(i, i ^ (2 if i % 2 == 0 else 4)) for i in range(8)])


def second_phase(message):
    return lax.ppermute(message, "ctx", [(i, i ^ (4 if i % 2 == 0 else 2)) for i in range(8)])


def doubled_prefix(chip):
    index = lax.axis_index("ctx")
    earlier = jnp.zeros_like(chip)
    running = chip
    bit = 2
    while bit < lax.axis_size("ctx"):
        partner = swap(running, "ctx", bit)
        earlier = earlier + jnp.where((index & bit) != 0, partner, 0.0)
        running = running + partner
        bit *= 2
    return earlier


def shards(queries, keys, values, head_gain):
    rows, width = queries.shape
    heads = head_gain.shape[1]
    queries, keys, values = (
        pltpu.with_memory_space_constraint(x, pltpu.HBM) for x in (queries, keys, values)
    )
    smem = pl.BlockSpec(memory_space=pltpu.SMEM)
    anywhere = pl.BlockSpec(memory_space=pl.ANY)
    vmem = pl.BlockSpec()

    def array(*shape, dtype=F32):
        return jax.ShapeDtypeStruct(shape, dtype)

    def call(kernel, name, flops, moved, **kwargs):
        return pl.pallas_call(
            kernel,
            name=name,
            compiler_params=pltpu.CompilerParams(vmem_limit_bytes=VMEM_BYTES),
            cost_estimate=pl.CostEstimate(flops=flops, bytes_accessed=moved, transcendentals=0),
            **kwargs,
        )

    size = rows * width * 4
    unit = 2 * rows * width * HD
    packed = array(heads // 2, HD, HD)
    first_tile = array(WINDOW, width)
    dma = pltpu.SemaphoreType.DMA
    tail_k = call(
        tail_kernel,
        "tail",
        0,
        size // 2,
        in_specs=[anywhere],
        out_shape=first_tile,
        scratch_shapes=[dma],
    )(keys)
    route = [(i, i + 1) for i in range(lax.axis_size("ctx") - 1)]
    before_k = lax.ppermute(tail_k, "ctx", route)

    keep, send, half, held_k, held_v, tail_v = call(
        totals_kernel,
        "totals",
        4 * unit,
        2 * size,
        in_specs=[anywhere, anywhere],
        out_shape=[packed, packed, array(heads, HD, HD), array(rows, width), array(rows, width), first_tile],
        scratch_shapes=[dma((2, heads // GROUP))],
    )(keys, values)
    beside, chip = chip_totals(keep, send)

    def local(begin, count, *after):
        taken = count * HD
        return call(
            functools.partial(local_kernel, begin, len(after)),
            "local",
            0,
            0,
            in_specs=[smem, anywhere, vmem, vmem] + [anywhere] * len(after),
            out_specs=[vmem] * 4 + [anywhere] * (len(after) // 2),
            out_shape=[
                array(rows, taken),
                array(rows, taken),
                array(rows, 2 * taken, dtype=BF16),
                array(8, rows),
            ]
            + [first_tile] * (len(after) // 2),
            scratch_shapes=[
                pltpu.VMEM((rows, taken), F32),
                pltpu.VMEM((rows, HD), F32),
                dma((count // GROUP,)),
            ],
            input_output_aliases={5: 4} if after else {},
        )(head_gain, queries, held_k, held_v, *after)

    begin = heads // 2
    parts = [local(0, begin)]
    *part, before_k = local(begin, GROUP, parts[0][3], before_k)
    parts.append(part)
    message = None
    if lax.axis_size("ctx") == 8:
        first = first_phase(chip)
        message = call(
            message_kernel,
            "message",
            0,
            size // 4,
            in_specs=[vmem, vmem, anywhere],
            out_shape=packed,
        )(first, chip, parts[1][3])
    after = parts[1][3] if message is None else message
    for begin in range(begin + GROUP, heads, GROUP):
        *part, tail_v = local(begin, GROUP, after, tail_v)
        parts.append(part)
    window, linear, qq, window_sums = zip(*parts)
    first_weights, first_now = call(
        first_weights_kernel,
        "first_weights",
        4 * unit,
        size,
        in_specs=[smem] + [vmem] * (3 + len(qq)),
        out_shape=[array(WINDOW, 2 * width, dtype=BF16), first_tile],
    )(head_gain, held_k, held_v, before_k, *qq)

    if message is not None:
        second = second_phase(message)
        mine, other = call(
            prefix_kernel,
            "prefix",
            0,
            size // 2,
            in_specs=[vmem] * 4 + [anywhere],
            out_shape=[packed, packed],
        )(first, second, keep, beside, first_now)
    else:
        earlier = doubled_prefix(chip)
        core = lax.axis_index("ctx") % 2
        mine = earlier + jnp.where(core == 1, beside, 0.0)
        other = earlier + jnp.where(core == 0, keep, 0.0)
    before_v = lax.ppermute(tail_v, "ctx", route)
    other = swap(other, "ctx", 1)

    *linear, sums = call(
        functools.partial(earlier_kernel, len(parts)),
        "earlier",
        3 * unit,
        3 * size,
        in_specs=[smem] + [vmem] * (3 + 3 * len(parts)),
        out_shape=[array(*x.shape) for x in linear] + [array(8, rows)],
        scratch_shapes=[pltpu.VMEM((rows, HD), F32)],
    )(head_gain, half, mine, other, *qq, *linear, *window_sums)
    first_a, sums = call(
        first_values_kernel,
        "first_values",
        unit,
        size // 2,
        out_shape=[first_tile, array(8, rows)],
    )(first_weights, first_now, before_v, sums)
    all_sums = [sums] + [swap(sums, "head", bits) for bits in range(1, lax.axis_size("head"))]
    return call(
        functools.partial(scale_first, len(all_sums), len(parts)),
        "scale",
        unit // 64,
        2 * size,
        out_specs=anywhere,
        out_shape=array(rows, width),
        scratch_shapes=[pltpu.VMEM((rows, width), F32), dma((rows // WINDOW,))],
    )(*all_sums, first_a, *window, *linear)


def solution(mesh):
    in_specs = (P("ctx", "head"), P("ctx", "head"), P("ctx", "head"), P(None, "head"))
    out_specs = P("ctx", "head")
    return jax.shard_map(shards, mesh=mesh, in_specs=in_specs, out_specs=out_specs, check_vma=False)
```

```python
import functools
import math

import jax
import jax.numpy as jnp
from jax import lax
from jax.experimental import pallas as pl
from jax.experimental.pallas import tpu as pltpu
from jax.sharding import PartitionSpec as P

HEADS = 64
HD = 128
WINDOW = 128
EPS = 1e-06
F32 = jnp.float32
BF16 = jnp.bfloat16
EXP2_SCALE = math.log2(math.e) / math.sqrt(HD)
VMEM_BYTES = 20 * 1024 * 1024
GROUP = 4


def halves(x):
    high = x.astype(BF16)
    low = (x - high.astype(F32)).astype(BF16)
    return high, low


def dot(a, b):
    return lax.dot_general(a, b, (((1,), (0,)), ((), ())), preferred_element_type=F32)


def dot_rows(a, b):
    return lax.dot_general(a, b, (((1,), (1,)), ((), ())), preferred_element_type=F32)


def dot_columns(a, b):
    return lax.dot_general(a, b, (((0,), (0,)), ((), ())), preferred_element_type=F32)


def side(a, b):
    return jnp.concatenate([a, b], axis=1)


def stack(a, b):
    return jnp.concatenate([a, b], axis=0)


def outer_state(k_high, k_low, v_high, v_low):
    grid = dot_columns(side(k_high, k_low), side(v_high, v_low))
    return grid[:HD, :HD] + (grid[:HD, HD:] + grid[HD:, :HD]) + grid[HD:, HD:]


def lower_mask():
    rows = lax.broadcasted_iota(jnp.int32, (WINDOW, WINDOW), 0)
    columns = lax.broadcasted_iota(jnp.int32, (WINDOW, WINDOW), 1)
    return rows >= columns


def row_sums(square):
    ones = jnp.ones((8, HD), BF16)
    high, low = halves(square)
    return dot_rows(ones, high) + dot_rows(ones, low)


def wide_keys(k_high, k_low):
    return stack(side(k_high, k_high), side(k_low, jnp.zeros_like(k_low)))


def wide_state(state):
    high, low = halves(state)
    return stack(side(high, low), side(high, jnp.zeros_like(high)))


def folded(wide):
    half = wide.shape[1] // 2
    return wide[:, :half] + wide[:, half:]


def head_columns(head, count=1, width=HD):
    return pl.ds(pl.multiple_of(head * width, width), count * width)


def tail_kernel(k_ref, low_ref, high_ref, sems):
    rows, width = k_ref.shape
    middle = width // 2
    copies = [
        pltpu.make_async_copy(
            k_ref.at[pl.ds(rows - WINDOW, WINDOW), pl.ds(i * middle, middle)], target, sems.at[i]
        )
        for i, target in enumerate((low_ref, high_ref))
    ]
    for copy in copies:
        copy.start()
    for copy in copies:
        copy.wait()


def load_kernel(q_hbm, q_ref, sems):
    width = q_ref.shape[1] // sems.shape[0]
    copies = []
    for i in range(sems.shape[0]):
        columns = pl.ds(i * width, width)
        copies.append(pltpu.make_async_copy(q_hbm.at[:, columns], q_ref.at[:, columns], sems.at[i]))
    for copy in copies:
        copy.start()
    for copy in copies:
        copy.wait()


def chip_kernel(keep_ref, beside_ref, _, out_ref):
    out_ref[...] = keep_ref[...] + beside_ref[...]


def totals_kernel(k_hbm, v_hbm, keep_ref, send_ref, half_ref, k_ref, v_ref, tail_v_ref, sems):
    core = lax.axis_index("ctx") % 2
    rows, width = k_ref.shape
    middle = rows // 2
    groups = width // (GROUP * HD)

    def copies(group):
        columns = head_columns(group, 1, GROUP * HD)
        return [
            pltpu.make_async_copy(source.at[:, columns], target.at[:, columns], sems.at[i, group])
            for i, (source, target) in enumerate(((k_hbm, k_ref), (v_hbm, v_ref)))
        ]

    for group in range(groups):
        for copy in copies(group):
            copy.start()

    @pl.loop(0, groups)
    def _(group):
        for copy in copies(group):
            copy.wait()
        for i in range(GROUP // 2):
            states = []
            for j in (2 * i, 2 * i + 1):
                head = GROUP * group + j
                columns = head_columns(head)
                k_high, k_low = halves(k_ref[:, columns])
                v_high, v_low = halves(v_ref[:, columns])
                first = outer_state(k_high[:middle], k_low[:middle], v_high[:middle], v_low[:middle])
                second = outer_state(k_high[middle:], k_low[middle:], v_high[middle:], v_low[middle:])
                half_ref[head] = first
                states.append(first + second)
            pair = GROUP // 2 * group + i
            keep_ref[pair] = jnp.where(core == 0, states[0], states[1])
            send_ref[pair] = jnp.where(core == 0, states[1], states[0])
        columns = head_columns(group, 1, GROUP * HD)
        tail_v_ref[:, columns] = v_ref[rows - WINDOW :, columns]


def weights_of(scores):
    biggest = jnp.max(scores, axis=1, keepdims=True)
    weights = jnp.exp2((scores - biggest) * EXP2_SCALE)
    return weights, jnp.sum(weights, axis=1, keepdims=True)


def masked_pair(weights, below, above):
    high, low = halves(weights)
    return side(high * above, high * below), side(low * above, low * below)


def local_kernel(begin, extra, gain_ref, q_ref, k_ref, v_ref, *refs):
    a_ref, b_ref, sum_ref = refs[extra : extra + 3]
    square_ref = refs[-1]
    lower = lower_mask()
    below = jnp.where(lower, 1.0, 0.0).astype(BF16)
    above = jnp.where(lower, 0.0, 1.0).astype(BF16)
    rows, width = a_ref.shape
    tiles = rows // WINDOW
    groups = width // (GROUP * HD)
    square_ref[...] = jnp.zeros_like(square_ref)

    def tile(n):
        return slice(n * WINDOW, (n + 1) * WINDOW)

    @pl.loop(0, groups)
    def _(group):
        scores = []
        for j in range(GROUP):
            columns = head_columns(begin + GROUP * group + j)
            qq = side(*halves(q_ref[:, columns]))
            k_high, k_low = halves(k_ref[:, columns])
            now, before = [], [None]
            for n in range(tiles):
                keys = wide_keys(k_high[tile(n)], k_low[tile(n)])
                found = folded(dot_rows(qq[n * WINDOW : min((n + 2) * WINDOW, rows)], keys))
                now.append(found[:WINDOW])
                before.append(found[WINDOW:])
            scores.append((now, before))
        for j in range(GROUP):
            head = GROUP * group + j
            columns = head_columns(head)
            vv = side(*halves(v_ref[:, head_columns(begin + head)]))
            now, before = scores[j]
            gain_a = gain_ref[0, begin + head]
            for n in range(tiles):
                inner_high, inner_low = halves(jnp.where(lower, now[n], 0.0))
                if n == 0:
                    wide = dot(stack(inner_high, inner_low), vv[tile(0)])
                    b_ref[tile(0), columns] = folded(wide[:WINDOW]) + wide[WINDOW:, :HD]
                    a_ref[tile(0), columns] = jnp.zeros((WINDOW, HD), F32)
                    continue
                weights, total = weights_of(jnp.where(lower, now[n], before[n]))
                pair_high, pair_low = masked_pair(weights, below, above)
                if n % 2:
                    before_high, before_low = halves(before[n])
                else:
                    before_high = before_low = jnp.zeros((WINDOW, HD), BF16)
                left = jnp.concatenate(
                    [pair_high, pair_low, side(before_high, inner_high), side(before_low, inner_low)], axis=0
                )
                wide = dot(left, vv[(n - 1) * WINDOW : (n + 1) * WINDOW])
                a = (folded(wide[tile(0)]) + wide[tile(1), :HD]) * (gain_a / total)
                a_ref[tile(n), columns] = a
                square_ref[tile(n), :] += a * a
                b_ref[tile(n), columns] = folded(wide[tile(2)]) + wide[tile(3), :HD]

    sum_ref[...] = row_sums(square_ref[...])


def message_kernel(first_ref, chip_ref, _, out_ref):
    index = lax.axis_index("ctx")
    core, x, y = index % 2, (index >> 1) % 2, index >> 2
    first = jnp.where((core == 0) | (y == 1), first_ref[...], 0.0)
    out_ref[...] = first + jnp.where((core == 0) | (x == 0), chip_ref[...], 0.0)


def prefix_kernel(first_ref, second_ref, keep_ref, beside_ref, *refs):
    mine_ref, other_ref = refs[-2:]
    index = lax.axis_index("ctx")
    core, x, y = index % 2, (index >> 1) % 2, index >> 2
    use_first = jnp.where(core == 0, x, y) == 1
    use_second = (core == 1) & ((x == 1) | (y == 1)) | (core == 0) & (y == 1)
    earlier = jnp.where(use_first, first_ref[...], 0.0) + jnp.where(use_second, second_ref[...], 0.0)
    mine_ref[...] = earlier + jnp.where(core == 1, beside_ref[...], 0.0)
    other_ref[...] = earlier + jnp.where(core == 0, keep_ref[...], 0.0)


def earlier_kernel(count, gain_ref, half_ref, mine_ref, other_ref, q_ref, *refs):
    b_refs, sum_refs, out_refs = (refs[i * count : (i + 1) * count] for i in range(3))
    sums_ref, square_ref = refs[3 * count :]
    core = lax.axis_index("ctx") % 2
    rows = b_refs[0].shape[0]
    middle = rows // 2
    head = 0
    square_ref[...] = jnp.zeros_like(square_ref)
    for b_ref, out_ref in zip(b_refs, out_refs):
        for j in range(b_ref.shape[1] // HD):
            columns = slice(j * HD, (j + 1) * HD)
            state = jnp.where(core == head % 2, mine_ref[head // 2], other_ref[head // 2])
            gain_b = gain_ref[1, head]
            for part, held in ((slice(0, middle), state), (slice(middle, rows), state + half_ref[head])):
                qq = side(*halves(q_ref[part, head * HD : (head + 1) * HD]))
                b = gain_b * (b_ref[part, columns] + folded(dot(qq, wide_state(held))))
                out_ref[part, columns] = b
                square_ref[part, :] += b * b
            head += 1
    sums = row_sums(square_ref[...])
    row = lax.broadcasted_iota(jnp.int32, sums.shape, 0)
    sums_ref[...] = jnp.where(row == 0, sum(ref[...] for ref in sum_refs), sums)


def first_weights_kernel(gain_ref, q_ref, k_ref, v_ref, low_ref, high_ref, weights_ref, out_ref):
    lower = lower_mask()
    reachable = jnp.logical_or(lower, lax.axis_index("ctx") > 0)
    top = slice(0, WINDOW)
    count = low_ref.shape[1] // HD
    for part, tail_ref in enumerate((low_ref, high_ref)):
        scores = []
        for j in range(count):
            columns = slice((part * count + j) * HD, (part * count + j + 1) * HD)
            qq = side(*halves(q_ref[top, columns]))
            now = folded(dot_rows(qq, wide_keys(*halves(k_ref[top, columns]))))
            before = folded(dot_rows(qq, wide_keys(*halves(tail_ref[:, j * HD : (j + 1) * HD]))))
            scores.append(jnp.where(reachable, jnp.where(lower, now, before), -jnp.inf))
        for j in range(count):
            head = part * count + j
            columns = slice(head * HD, (head + 1) * HD)
            weights, total = weights_of(scores[j])
            weights = weights * (gain_ref[0, head] / total)
            now_high, now_low = halves(jnp.where(lower, weights, 0.0))
            vv = side(*halves(v_ref[top, columns]))
            wide = dot(stack(now_high, now_low), vv)
            out_ref[:, columns] = folded(wide[:WINDOW]) + wide[WINDOW:, :HD]
            weights_ref[:, 2 * head * HD : 2 * (head + 1) * HD] = side(*halves(jnp.where(lower, 0.0, weights)))


def first_values_kernel(weights_ref, now_ref, tail_v_ref, a_ref, sums_ref):
    square = jnp.zeros((WINDOW, HD), F32)
    for j in range(now_ref.shape[1] // HD):
        columns = slice(j * HD, (j + 1) * HD)
        high = weights_ref[:, 2 * j * HD : (2 * j + 1) * HD]
        low = weights_ref[:, (2 * j + 1) * HD : 2 * (j + 1) * HD]
        wide = dot(stack(high, low), side(*halves(tail_v_ref[:, columns])))
        a = now_ref[:, columns] + (folded(wide[:WINDOW]) + wide[WINDOW:, :HD])
        a_ref[:, columns] = a
        square = square + a * a
    sums_ref[...] = row_sums(square)


def inverse_norm(total):
    return 1.0 / jnp.sqrt(total / (HEADS * HD) + EPS)


def scale_kernel(count, sums_ref, _, *refs):
    a_refs, b_refs, (out_hbm, out_ref, sems) = refs[:count], refs[count : 2 * count], refs[2 * count :]
    inverse = inverse_norm(jnp.sum(sums_ref[...], axis=0)).T
    copies = []
    for n in range(out_ref.shape[0] // WINDOW):
        held = slice(n * WINDOW, (n + 1) * WINDOW)
        rows = slice((n + 1) * WINDOW, (n + 2) * WINDOW)
        inverse_a, inverse_b = inverse[rows, 0:1], inverse[rows, 1:2]
        begin = 0
        for a_ref, b_ref in zip(a_refs, b_refs):
            columns = slice(begin, begin + a_ref.shape[1])
            out_ref[held, columns] = a_ref[rows, :] * inverse_a + b_ref[rows, :] * inverse_b
            begin = columns.stop
        copy = pltpu.make_async_copy(out_ref.at[held, :], out_hbm.at[rows, :], sems.at[n])
        copy.start()
        copies.append(copy)
    for copy in copies:
        copy.wait()


def first_scale_kernel(count, parts, sums_ref, a_ref, _, *refs):
    b_refs, sums, (out_hbm, out_ref, sems) = refs[:count], refs[count : count + parts], refs[count + parts :]
    total = sums[0][...]
    for part in sums[1:]:
        total = total + part[...]
    inverse_a = inverse_norm(total).T[:, 0:1]
    inverse_b = inverse_norm(jnp.sum(sums_ref[:, :, :WINDOW], axis=0)).T[:, 1:2]
    copies = []
    for n in range(sems.shape[0]):
        rows = slice(n * WINDOW // sems.shape[0], (n + 1) * WINDOW // sems.shape[0])
        begin = 0
        for b_ref in b_refs:
            columns = slice(begin, begin + b_ref.shape[1])
            out_ref[rows, columns] = a_ref[rows, columns] * inverse_a[rows] + b_ref[rows, :] * inverse_b[rows]
            begin = columns.stop
        copy = pltpu.make_async_copy(out_ref.at[rows, :], out_hbm.at[rows, :], sems.at[n])
        copy.start()
        copies.append(copy)
    for copy in copies:
        copy.wait()


def swap(block, axis, bit):
    return lax.ppermute(block, axis, [(i, i ^ bit) for i in range(lax.axis_size(axis))])


def first_phase(chip):
    return lax.ppermute(chip, "ctx", [(i, i ^ (2 if i % 2 == 0 else 4)) for i in range(8)])


def second_phase(message):
    return lax.ppermute(message, "ctx", [(i, i ^ (4 if i % 2 == 0 else 2)) for i in range(8)])


def doubled_prefix(chip):
    index = lax.axis_index("ctx")
    earlier = jnp.zeros_like(chip)
    running = chip
    bit = 2
    while bit < lax.axis_size("ctx"):
        partner = swap(running, "ctx", bit)
        earlier = earlier + jnp.where((index & bit) != 0, partner, 0.0)
        running = running + partner
        bit *= 2
    return earlier


def shards(queries, keys, values, head_gain):
    rows, width = queries.shape
    heads = head_gain.shape[1]
    queries, keys, values = (
        pltpu.with_memory_space_constraint(x, pltpu.HBM) for x in (queries, keys, values)
    )
    smem = pl.BlockSpec(memory_space=pltpu.SMEM)
    anywhere = pl.BlockSpec(memory_space=pl.ANY)
    vmem = pl.BlockSpec()

    def array(*shape, dtype=F32):
        return jax.ShapeDtypeStruct(shape, dtype)

    def call(kernel, name, flops, moved, **kwargs):
        return pl.pallas_call(
            kernel,
            name=name,
            compiler_params=pltpu.CompilerParams(vmem_limit_bytes=VMEM_BYTES),
            cost_estimate=pl.CostEstimate(flops=flops, bytes_accessed=moved, transcendentals=0),
            **kwargs,
        )

    size = rows * width * 4
    unit = 2 * rows * width * HD
    packed = array(heads // 2, HD, HD)
    first_tile = array(WINDOW, width)
    dma = pltpu.SemaphoreType.DMA
    tail_low, tail_high = call(
        tail_kernel,
        "tail",
        0,
        size // 2,
        in_specs=[anywhere],
        out_shape=[array(WINDOW, width // 2)] * 2,
        scratch_shapes=[dma((2,))],
    )(keys)
    route = [(i, i + 1) for i in range(lax.axis_size("ctx") - 1)]
    before_low = lax.ppermute(tail_low, "ctx", route)
    before_high = lax.ppermute(tail_high, "ctx", route)

    keep, send, half, held_k, held_v, tail_v = call(
        totals_kernel,
        "totals",
        4 * unit,
        2 * size,
        in_specs=[anywhere, anywhere],
        out_shape=[packed, packed, array(heads, HD, HD), array(rows, width), array(rows, width), first_tile],
        scratch_shapes=[dma((2, heads // GROUP))],
    )(keys, values)
    held_q = call(
        load_kernel,
        "load",
        0,
        2 * size,
        in_specs=[anywhere],
        out_shape=array(rows, width),
        scratch_shapes=[dma((4,))],
    )(queries)
    beside = swap(send, "ctx", 1)
    chip = call(
        chip_kernel,
        "chip",
        0,
        size // 4,
        in_specs=[vmem, vmem, anywhere],
        out_shape=packed,
    )(keep, beside, held_q)

    def local(begin, count, after, *passed):
        taken = count * HD
        return call(
            functools.partial(local_kernel, begin, 1 + len(passed)),
            "local",
            0,
            0,
            in_specs=[smem, vmem, vmem, vmem] + [anywhere] * (1 + len(passed)),
            out_specs=[vmem] * 3 + [anywhere] * len(passed),
            out_shape=[array(rows, taken), array(rows, taken), array(8, rows)] + [first_tile] * len(passed),
            scratch_shapes=[pltpu.VMEM((rows, HD), F32)],
            input_output_aliases={5: 3} if passed else {},
        )(head_gain, held_q, held_k, held_v, after, *passed)

    begin = heads * 3 // 4 // GROUP * GROUP
    parts = [local(0, begin, before_low)]
    message = None
    if lax.axis_size("ctx") == 8:
        first = first_phase(chip)
        message = call(
            message_kernel,
            "message",
            0,
            size // 4,
            in_specs=[vmem, vmem, anywhere],
            out_shape=packed,
        )(first, chip, parts[0][2])
    *part, tail_v = local(begin, heads - begin, parts[0][2] if message is None else message, tail_v)
    parts.append(part)
    window, linear, window_sums = zip(*parts)
    before_v = lax.ppermute(tail_v, "ctx", route)
    first_weights, first_now = call(
        first_weights_kernel,
        "first_weights",
        4 * unit,
        size,
        in_specs=[smem] + [vmem] * 5,
        out_shape=[array(WINDOW, 2 * width, dtype=BF16), first_tile],
    )(head_gain, held_q, held_k, held_v, before_low, before_high)

    if message is not None:
        second = second_phase(message)
        mine, other = call(
            prefix_kernel,
            "prefix",
            0,
            size // 2,
            in_specs=[vmem] * 4 + [anywhere],
            out_shape=[packed, packed],
        )(first, second, keep, beside, first_now)
    else:
        earlier = doubled_prefix(chip)
        core = lax.axis_index("ctx") % 2
        mine = earlier + jnp.where(core == 1, beside, 0.0)
        other = earlier + jnp.where(core == 0, keep, 0.0)
    other = swap(other, "ctx", 1)

    *linear, sums = call(
        functools.partial(earlier_kernel, len(parts)),
        "earlier",
        3 * unit,
        3 * size,
        in_specs=[smem] + [vmem] * (4 + 2 * len(parts)),
        out_shape=[array(*x.shape) for x in linear] + [array(8, rows)],
        scratch_shapes=[pltpu.VMEM((rows, HD), F32)],
    )(head_gain, half, mine, other, held_q, *linear, *window_sums)
    sums = lax.all_gather(sums, "head")
    first_a, first_sums = call(
        first_values_kernel,
        "first_values",
        unit,
        size // 2,
        out_shape=[first_tile, array(8, WINDOW)],
    )(first_weights, first_now, before_v)
    first_sums = [first_sums] + [swap(first_sums, "head", bits) for bits in range(1, lax.axis_size("head"))]
    out = call(
        functools.partial(scale_kernel, len(parts)),
        "scale",
        unit // 64,
        2 * size,
        in_specs=[vmem, anywhere] + [vmem] * (2 * len(parts)),
        out_specs=anywhere,
        out_shape=array(rows, width),
        scratch_shapes=[pltpu.VMEM((rows - WINDOW, width), F32), dma((rows // WINDOW - 1,))],
    )(sums, first_sums[0], *window, *linear)
    return call(
        functools.partial(first_scale_kernel, len(parts), len(first_sums)),
        "first_scale",
        unit // 256,
        size // 2,
        in_specs=[vmem, vmem, anywhere] + [vmem] * (len(parts) + len(first_sums)),
        out_specs=anywhere,
        out_shape=array(rows, width),
        scratch_shapes=[pltpu.VMEM((WINDOW, width), F32), dma((4,))],
        input_output_aliases={2: 0},
    )(sums, first_a, out, *linear, *first_sums)


def solution(mesh):
    in_specs = (P("ctx", "head"), P("ctx", "head"), P("ctx", "head"), P(None, "head"))
    out_specs = P("ctx", "head")
    return jax.shard_map(shards, mesh=mesh, in_specs=in_specs, out_specs=out_specs, check_vma=False)
```

```python
import functools
import math

import jax
import jax.numpy as jnp
from jax import lax
from jax.experimental import pallas as pl
from jax.experimental.pallas import tpu as pltpu
from jax.sharding import PartitionSpec as P

HEADS = 64
HD = 128
WINDOW = 128
EPS = 1e-06
F32 = jnp.float32
BF16 = jnp.bfloat16
EXP2_SCALE = math.log2(math.e) / math.sqrt(HD)
VMEM_BYTES = 20 * 1024 * 1024
GROUP = 4


def halves(x):
    high = x.astype(BF16)
    low = (x - high.astype(F32)).astype(BF16)
    return high, low


def dot(a, b):
    return lax.dot_general(a, b, (((1,), (0,)), ((), ())), preferred_element_type=F32)


def dot_rows(a, b):
    return lax.dot_general(a, b, (((1,), (1,)), ((), ())), preferred_element_type=F32)


def dot_columns(a, b):
    return lax.dot_general(a, b, (((0,), (0,)), ((), ())), preferred_element_type=F32)


def side(a, b):
    return jnp.concatenate([a, b], axis=1)


def stack(a, b):
    return jnp.concatenate([a, b], axis=0)


def outer_state(k_high, k_low, v_high, v_low):
    grid = dot_columns(side(k_high, k_low), side(v_high, v_low))
    return grid[:HD, :HD] + (grid[:HD, HD:] + grid[HD:, :HD]) + grid[HD:, HD:]


def lower_mask():
    rows = lax.broadcasted_iota(jnp.int32, (WINDOW, WINDOW), 0)
    columns = lax.broadcasted_iota(jnp.int32, (WINDOW, WINDOW), 1)
    return rows >= columns


def row_sums(square):
    ones = jnp.ones((8, HD), BF16)
    high, low = halves(square)
    return dot_rows(ones, high) + dot_rows(ones, low)


def wide_keys(k_high, k_low):
    return stack(side(k_high, k_high), side(k_low, jnp.zeros_like(k_low)))


def wide_state(state):
    high, low = halves(state)
    return stack(side(high, low), side(high, jnp.zeros_like(high)))


def folded(wide):
    half = wide.shape[1] // 2
    return wide[:, :half] + wide[:, half:]


def head_columns(head, count=1, width=HD):
    return pl.ds(pl.multiple_of(head * width, width), count * width)


def load_kernel(q_hbm, _, q_ref, sems):
    width = q_ref.shape[1] // sems.shape[0]
    copies = []
    for i in range(sems.shape[0]):
        columns = pl.ds(i * width, width)
        copies.append(pltpu.make_async_copy(q_hbm.at[:, columns], q_ref.at[:, columns], sems.at[i]))
    for copy in copies:
        copy.start()
    for copy in copies:
        copy.wait()


def pass_kernel(*_):
    pass


def chip_kernel(keep_ref, beside_ref, _, out_ref, __):
    out_ref[...] = keep_ref[...] + beside_ref[...]


def totals_kernel(k_hbm, v_hbm, keep_ref, send_ref, half_ref, k_ref, v_ref, tail_k_ref, tail_v_ref, sems):
    core = lax.axis_index("ctx") % 2
    rows, width = k_ref.shape
    middle = rows // 2
    groups = width // (GROUP * HD)

    def copies(group):
        columns = head_columns(group, 1, GROUP * HD)
        return [
            pltpu.make_async_copy(source.at[:, columns], target.at[:, columns], sems.at[i, group])
            for i, (source, target) in enumerate(((k_hbm, k_ref), (v_hbm, v_ref)))
        ]

    for group in range(groups):
        for copy in copies(group):
            copy.start()

    @pl.loop(0, groups)
    def _(group):
        for copy in copies(group):
            copy.wait()
        for i in range(GROUP // 2):
            states = []
            for j in (2 * i, 2 * i + 1):
                head = GROUP * group + j
                columns = head_columns(head)
                k_high, k_low = halves(k_ref[:, columns])
                v_high, v_low = halves(v_ref[:, columns])
                first = outer_state(k_high[:middle], k_low[:middle], v_high[:middle], v_low[:middle])
                second = outer_state(k_high[middle:], k_low[middle:], v_high[middle:], v_low[middle:])
                half_ref[head] = first
                states.append(first + second)
            pair = GROUP // 2 * group + i
            keep_ref[pair] = jnp.where(core == 0, states[0], states[1])
            send_ref[pair] = jnp.where(core == 0, states[1], states[0])
        columns = head_columns(group, 1, GROUP * HD)
        tail_k_ref[:, columns] = k_ref[rows - WINDOW :, columns]
        tail_v_ref[:, columns] = v_ref[rows - WINDOW :, columns]


def weights_of(scores):
    biggest = jnp.max(scores, axis=1, keepdims=True)
    weights = jnp.exp2((scores - biggest) * EXP2_SCALE)
    return weights, jnp.sum(weights, axis=1, keepdims=True)


def masked_pair(weights, below, above):
    high, low = halves(weights)
    return side(high * above, high * below), side(low * above, low * below)


def local_kernel(begin, extra, gain_ref, q_ref, k_ref, v_ref, *refs):
    a_ref, b_ref, sum_ref, square_ref = refs[extra:]
    lower = lower_mask()
    below = jnp.where(lower, 1.0, 0.0).astype(BF16)
    above = jnp.where(lower, 0.0, 1.0).astype(BF16)
    rows, width = a_ref.shape
    tiles = rows // WINDOW
    groups = width // (GROUP * HD)
    square_ref[...] = jnp.zeros_like(square_ref)

    def tile(n):
        return slice(n * WINDOW, (n + 1) * WINDOW)

    @pl.loop(0, groups)
    def _(group):
        scores = []
        for j in range(GROUP):
            columns = head_columns(begin + GROUP * group + j)
            qq = side(*halves(q_ref[:, columns]))
            k_high, k_low = halves(k_ref[:, columns])
            now, before = [], [None]
            for n in range(tiles):
                keys = wide_keys(k_high[tile(n)], k_low[tile(n)])
                found = folded(dot_rows(qq[n * WINDOW : min((n + 2) * WINDOW, rows)], keys))
                now.append(found[:WINDOW])
                before.append(found[WINDOW:])
            scores.append((now, before))
        for j in range(GROUP):
            head = GROUP * group + j
            columns = head_columns(head)
            vv = side(*halves(v_ref[:, head_columns(begin + head)]))
            now, before = scores[j]
            gain_a = gain_ref[0, begin + head]
            for n in range(tiles):
                inner_high, inner_low = halves(jnp.where(lower, now[n], 0.0))
                if n == 0:
                    wide = dot(stack(inner_high, inner_low), vv[tile(0)])
                    b_ref[tile(0), columns] = folded(wide[:WINDOW]) + wide[WINDOW:, :HD]
                    a_ref[tile(0), columns] = jnp.zeros((WINDOW, HD), F32)
                    continue
                weights, total = weights_of(jnp.where(lower, now[n], before[n]))
                pair_high, pair_low = masked_pair(weights, below, above)
                if n % 2:
                    before_high, before_low = halves(before[n])
                else:
                    before_high = before_low = jnp.zeros((WINDOW, HD), BF16)
                left = jnp.concatenate(
                    [pair_high, pair_low, side(before_high, inner_high), side(before_low, inner_low)], axis=0
                )
                wide = dot(left, vv[(n - 1) * WINDOW : (n + 1) * WINDOW])
                a = (folded(wide[tile(0)]) + wide[tile(1), :HD]) * (gain_a / total)
                a_ref[tile(n), columns] = a
                square_ref[tile(n), :] += a * a
                b_ref[tile(n), columns] = folded(wide[tile(2)]) + wide[tile(3), :HD]

    sum_ref[...] = row_sums(square_ref[...])


def message_kernel(first_ref, chip_ref, _, out_ref):
    index = lax.axis_index("ctx")
    core, x, y = index % 2, (index >> 1) % 2, index >> 2
    first = jnp.where((core == 0) | (y == 1), first_ref[...], 0.0)
    out_ref[...] = first + jnp.where((core == 0) | (x == 0), chip_ref[...], 0.0)


def prefix_kernel(first_ref, second_ref, keep_ref, beside_ref, *refs):
    mine_ref, other_ref = refs[-2:]
    index = lax.axis_index("ctx")
    core, x, y = index % 2, (index >> 1) % 2, index >> 2
    use_first = jnp.where(core == 0, x, y) == 1
    use_second = (core == 1) & ((x == 1) | (y == 1)) | (core == 0) & (y == 1)
    earlier = jnp.where(use_first, first_ref[...], 0.0) + jnp.where(use_second, second_ref[...], 0.0)
    mine_ref[...] = earlier + jnp.where(core == 1, beside_ref[...], 0.0)
    other_ref[...] = earlier + jnp.where(core == 0, keep_ref[...], 0.0)


def earlier_kernel(count, gain_ref, half_ref, mine_ref, other_ref, q_ref, *refs):
    b_refs, sum_refs, out_refs = (refs[i * count : (i + 1) * count] for i in range(3))
    sums_ref, square_ref = refs[3 * count :]
    core = lax.axis_index("ctx") % 2
    rows = b_refs[0].shape[0]
    middle = rows // 2
    head = 0
    square_ref[...] = jnp.zeros_like(square_ref)
    for b_ref, out_ref in zip(b_refs, out_refs):
        for j in range(b_ref.shape[1] // HD):
            columns = slice(j * HD, (j + 1) * HD)
            state = jnp.where(core == head % 2, mine_ref[head // 2], other_ref[head // 2])
            gain_b = gain_ref[1, head]
            for part, held in ((slice(0, middle), state), (slice(middle, rows), state + half_ref[head])):
                qq = side(*halves(q_ref[part, head * HD : (head + 1) * HD]))
                b = gain_b * (b_ref[part, columns] + folded(dot(qq, wide_state(held))))
                out_ref[part, columns] = b
                square_ref[part, :] += b * b
            head += 1
    sums = row_sums(square_ref[...])
    row = lax.broadcasted_iota(jnp.int32, sums.shape, 0)
    sums_ref[...] = jnp.where(row == 0, sum(ref[...] for ref in sum_refs), sums)


def first_weights_kernel(gain_ref, q_ref, k_ref, v_ref, tail_ref, weights_ref, out_ref):
    lower = lower_mask()
    reachable = jnp.logical_or(lower, lax.axis_index("ctx") > 0)
    top = slice(0, WINDOW)
    count = tail_ref.shape[1] // (2 * HD)
    for part in range(2):
        scores = []
        for j in range(count):
            columns = slice((part * count + j) * HD, (part * count + j + 1) * HD)
            qq = side(*halves(q_ref[top, columns]))
            now = folded(dot_rows(qq, wide_keys(*halves(k_ref[top, columns]))))
            before = folded(dot_rows(qq, wide_keys(*halves(tail_ref[:, columns]))))
            scores.append(jnp.where(reachable, jnp.where(lower, now, before), -jnp.inf))
        for j in range(count):
            head = part * count + j
            columns = slice(head * HD, (head + 1) * HD)
            weights, total = weights_of(scores[j])
            weights = weights * (gain_ref[0, head] / total)
            now_high, now_low = halves(jnp.where(lower, weights, 0.0))
            vv = side(*halves(v_ref[top, columns]))
            wide = dot(stack(now_high, now_low), vv)
            out_ref[:, columns] = folded(wide[:WINDOW]) + wide[WINDOW:, :HD]
            weights_ref[:, 2 * head * HD : 2 * (head + 1) * HD] = side(*halves(jnp.where(lower, 0.0, weights)))


def first_values_kernel(weights_ref, now_ref, tail_v_ref, _, a_ref, sums_ref):
    square = jnp.zeros((WINDOW, HD), F32)
    for j in range(now_ref.shape[1] // HD):
        columns = slice(j * HD, (j + 1) * HD)
        high = weights_ref[:, 2 * j * HD : (2 * j + 1) * HD]
        low = weights_ref[:, (2 * j + 1) * HD : 2 * (j + 1) * HD]
        wide = dot(stack(high, low), side(*halves(tail_v_ref[:, columns])))
        a = now_ref[:, columns] + (folded(wide[:WINDOW]) + wide[WINDOW:, :HD])
        a_ref[:, columns] = a
        square = square + a * a
    sums_ref[...] = row_sums(square)


def inverse_norm(total):
    return 1.0 / jnp.sqrt(total / (HEADS * HD) + EPS)


def added(refs):
    total = refs[0][...]
    for ref in refs[1:]:
        total = total + ref[...]
    return total


def scale_kernel(count, parts, _, *refs):
    sums, refs = refs[:parts], refs[parts:]
    a_refs, b_refs, (out_hbm, out_ref, sems) = refs[:count], refs[count : 2 * count], refs[2 * count :]
    inverse = inverse_norm(added(sums)).T
    copies = []
    for n in range(out_ref.shape[0] // WINDOW):
        held = slice(n * WINDOW, (n + 1) * WINDOW)
        rows = slice((n + 1) * WINDOW, (n + 2) * WINDOW)
        inverse_a, inverse_b = inverse[rows, 0:1], inverse[rows, 1:2]
        begin = 0
        for a_ref, b_ref in zip(a_refs, b_refs):
            columns = slice(begin, begin + a_ref.shape[1])
            out_ref[held, columns] = a_ref[rows, :] * inverse_a + b_ref[rows, :] * inverse_b
            begin = columns.stop
        copy = pltpu.make_async_copy(out_ref.at[held, :], out_hbm.at[rows, :], sems.at[n])
        copy.start()
        copies.append(copy)
    for copy in copies:
        copy.wait()


def first_scale_kernel(count, parts, a_ref, _, *refs):
    b_refs, refs = refs[:count], refs[count:]
    sums, first_sums, (out_hbm, out_ref, sems) = refs[:parts], refs[parts : 2 * parts], refs[2 * parts :]
    inverse_a = inverse_norm(added(first_sums)).T[:, 0:1]
    inverse_b = inverse_norm(added(sums)[:, :WINDOW]).T[:, 1:2]
    copies = []
    for n in range(sems.shape[0]):
        rows = slice(n * WINDOW // sems.shape[0], (n + 1) * WINDOW // sems.shape[0])
        begin = 0
        for b_ref in b_refs:
            columns = slice(begin, begin + b_ref.shape[1])
            out_ref[rows, columns] = a_ref[rows, columns] * inverse_a[rows] + b_ref[rows, :] * inverse_b[rows]
            begin = columns.stop
        copy = pltpu.make_async_copy(out_ref.at[rows, :], out_hbm.at[rows, :], sems.at[n])
        copy.start()
        copies.append(copy)
    for copy in copies:
        copy.wait()


def swap(block, axis, bit):
    return lax.ppermute(block, axis, [(i, i ^ bit) for i in range(lax.axis_size(axis))])


def everyone(block, axis):
    return [block] + [swap(block, axis, bits) for bits in range(1, lax.axis_size(axis))]


def first_phase(chip):
    return lax.ppermute(chip, "ctx", [(i, i ^ (2 if i % 2 == 0 else 4)) for i in range(8)])


def second_phase(message):
    return lax.ppermute(message, "ctx", [(i, i ^ (4 if i % 2 == 0 else 2)) for i in range(8)])


def doubled_prefix(chip):
    index = lax.axis_index("ctx")
    earlier = jnp.zeros_like(chip)
    running = chip
    bit = 2
    while bit < lax.axis_size("ctx"):
        partner = swap(running, "ctx", bit)
        earlier = earlier + jnp.where((index & bit) != 0, partner, 0.0)
        running = running + partner
        bit *= 2
    return earlier


def shards(queries, keys, values, head_gain):
    rows, width = queries.shape
    heads = head_gain.shape[1]
    queries, keys, values = (
        pltpu.with_memory_space_constraint(x, pltpu.HBM) for x in (queries, keys, values)
    )
    smem = pl.BlockSpec(memory_space=pltpu.SMEM)
    anywhere = pl.BlockSpec(memory_space=pl.ANY)
    vmem = pl.BlockSpec()

    def array(*shape, dtype=F32):
        return jax.ShapeDtypeStruct(shape, dtype)

    def call(kernel, name, **kwargs):
        return pl.pallas_call(
            kernel,
            name=name,
            compiler_params=pltpu.CompilerParams(vmem_limit_bytes=VMEM_BYTES),
            cost_estimate=pl.CostEstimate(flops=0, bytes_accessed=0, transcendentals=0),
            **kwargs,
        )

    packed = array(heads // 2, HD, HD)
    first_tile = array(WINDOW, width)
    dma = pltpu.SemaphoreType.DMA
    keep, send, half, held_k, held_v, tail_k, tail_v = call(
        totals_kernel,
        "totals",
        in_specs=[anywhere, anywhere],
        out_shape=[
            packed,
            packed,
            array(heads, HD, HD),
            array(rows, width),
            array(rows, width),
            first_tile,
            first_tile,
        ],
        scratch_shapes=[dma((2, heads // GROUP))],
    )(keys, values)
    beside = swap(send, "ctx", 1)
    chip, tail_k = call(
        chip_kernel,
        "chip",
        in_specs=[vmem, vmem, anywhere],
        out_specs=[vmem, anywhere],
        out_shape=[packed, first_tile],
        input_output_aliases={2: 1},
    )(keep, beside, tail_k)
    held_q = call(
        load_kernel,
        "load",
        in_specs=[anywhere, anywhere],
        out_shape=array(rows, width),
        scratch_shapes=[dma((4,))],
    )(queries, chip)
    route = [(i, i + 1) for i in range(lax.axis_size("ctx") - 1)]
    before_k = lax.ppermute(tail_k, "ctx", route)

    def local(begin, count, after):
        taken = count * HD
        after = [] if after is None else [after]
        return call(
            functools.partial(local_kernel, begin, len(after)),
            "local",
            in_specs=[smem, vmem, vmem, vmem] + [anywhere] * len(after),
            out_shape=[array(rows, taken), array(rows, taken), array(8, rows)],
            scratch_shapes=[pltpu.VMEM((rows, HD), F32)],
        )(head_gain, held_q, held_k, held_v, *after)

    def pass_on(array_now, after):
        return call(
            pass_kernel,
            "pass",
            in_specs=[anywhere, anywhere],
            out_specs=anywhere,
            out_shape=array(*array_now.shape),
            input_output_aliases={0: 0},
        )(array_now, after)

    begin = heads * 3 // 4 // GROUP * GROUP
    parts = [local(0, begin, None)]
    message = None
    if lax.axis_size("ctx") == 8:
        first = first_phase(chip)
        message = call(
            message_kernel,
            "message",
            in_specs=[vmem, vmem, anywhere],
            out_shape=packed,
        )(first, chip, parts[0][2])
    parts.append(local(begin, heads - begin, message))
    window, linear, window_sums = zip(*parts)
    before_v = lax.ppermute(pass_on(tail_v, window_sums[1]), "ctx", route)
    first_weights, first_now = call(
        first_weights_kernel,
        "first_weights",
        in_specs=[smem] + [vmem] * 4,
        out_shape=[array(WINDOW, 2 * width, dtype=BF16), first_tile],
    )(head_gain, held_q, held_k, held_v, before_k)

    if message is not None:
        second = second_phase(message)
        mine, other = call(
            prefix_kernel,
            "prefix",
            in_specs=[vmem] * 4 + [anywhere],
            out_shape=[packed, packed],
        )(first, second, keep, beside, first_now)
    else:
        earlier = doubled_prefix(chip)
        core = lax.axis_index("ctx") % 2
        mine = earlier + jnp.where(core == 1, beside, 0.0)
        other = earlier + jnp.where(core == 0, keep, 0.0)
    other = swap(other, "ctx", 1)

    *linear, sums = call(
        functools.partial(earlier_kernel, len(parts)),
        "earlier",
        in_specs=[smem] + [vmem] * (4 + 2 * len(parts)),
        out_shape=[array(*x.shape) for x in linear] + [array(8, rows)],
        scratch_shapes=[pltpu.VMEM((rows, HD), F32)],
    )(head_gain, half, mine, other, held_q, *linear, *window_sums)
    sums = everyone(sums, "head")
    first_a, first_sums = call(
        first_values_kernel,
        "first_values",
        in_specs=[vmem] * 3 + [anywhere],
        out_shape=[first_tile, array(8, WINDOW)],
    )(first_weights, first_now, before_v, sums[0])
    first_sums = everyone(first_sums, "head")
    out = call(
        functools.partial(scale_kernel, len(parts), len(sums)),
        "scale",
        in_specs=[anywhere] + [vmem] * (2 * len(parts) + len(sums)),
        out_specs=anywhere,
        out_shape=array(rows, width),
        scratch_shapes=[pltpu.VMEM((rows - WINDOW, width), F32), dma((rows // WINDOW - 1,))],
    )(first_sums[0], *sums, *window, *linear)
    return call(
        functools.partial(first_scale_kernel, len(parts), len(sums)),
        "first_scale",
        in_specs=[vmem, anywhere] + [vmem] * (len(parts) + 2 * len(sums)),
        out_specs=anywhere,
        out_shape=array(rows, width),
        scratch_shapes=[pltpu.VMEM((WINDOW, width), F32), dma((4,))],
        input_output_aliases={1: 0},
    )(first_a, out, *linear, *sums, *first_sums)


def solution(mesh):
    in_specs = (P("ctx", "head"), P("ctx", "head"), P("ctx", "head"), P(None, "head"))
    out_specs = P("ctx", "head")
    return jax.shard_map(shards, mesh=mesh, in_specs=in_specs, out_specs=out_specs, check_vma=False)
```

```python
import functools
import math

import jax
import jax.numpy as jnp
from jax import lax
from jax.experimental import pallas as pl
from jax.experimental.pallas import tpu as pltpu
from jax.sharding import PartitionSpec as P

HEADS = 64
HD = 128
WINDOW = 128
EPS = 1e-06
F32 = jnp.float32
BF16 = jnp.bfloat16
EXP2_SCALE = math.log2(math.e) / math.sqrt(HD)
VMEM_BYTES = 20 * 1024 * 1024
GROUP = 4


def halves(x):
    high = x.astype(BF16)
    low = (x - high.astype(F32)).astype(BF16)
    return high, low


def dot(a, b):
    return lax.dot_general(a, b, (((1,), (0,)), ((), ())), preferred_element_type=F32)


def dot_rows(a, b):
    return lax.dot_general(a, b, (((1,), (1,)), ((), ())), preferred_element_type=F32)


def dot_columns(a, b):
    return lax.dot_general(a, b, (((0,), (0,)), ((), ())), preferred_element_type=F32)


def side(a, b):
    return jnp.concatenate([a, b], axis=1)


def stack(a, b):
    return jnp.concatenate([a, b], axis=0)


def outer_state(k_high, k_low, v_high, v_low):
    grid = dot_columns(side(k_high, k_low), side(v_high, v_low))
    return grid[:HD, :HD] + (grid[:HD, HD:] + grid[HD:, :HD]) + grid[HD:, HD:]


def lower_mask():
    rows = lax.broadcasted_iota(jnp.int32, (WINDOW, WINDOW), 0)
    columns = lax.broadcasted_iota(jnp.int32, (WINDOW, WINDOW), 1)
    return rows >= columns


def row_sums(square):
    ones = jnp.ones((8, HD), BF16)
    high, low = halves(square)
    return dot_rows(ones, high) + dot_rows(ones, low)


def wide_keys(k_high, k_low):
    return stack(side(k_high, k_high), side(k_low, jnp.zeros_like(k_low)))


def wide_state(state):
    high, low = halves(state)
    return stack(side(high, low), side(high, jnp.zeros_like(high)))


def folded(wide):
    half = wide.shape[1] // 2
    return wide[:, :half] + wide[:, half:]


def head_columns(head, count=1, width=HD):
    return pl.ds(pl.multiple_of(head * width, width), count * width)


def first_head(part, heads):
    core = lax.axis_index("ctx") % 2
    return jnp.where(core == part, heads // 2, 0)


def column_copies(part, sources, targets, sems):
    begin = first_head(part, sources[0].shape[1] // HD) * HD
    width = GROUP * HD
    copies = []
    for group in range(targets[0].shape[1] // width):
        there = pl.ds(pl.multiple_of(begin + group * width, HD), width)
        here = pl.ds(group * width, width)
        copies.append(
            [
                pltpu.make_async_copy(source.at[:, there], target.at[:, here], sems.at[i, group])
                for i, (source, target) in enumerate(zip(sources, targets))
            ]
        )
    return copies


def totals_kernel(part, k_hbm, v_hbm, _, total_ref, half_ref, k_ref, v_ref, sems):
    middle = k_ref.shape[0] // 2
    copies = column_copies(part, (k_hbm, v_hbm), (k_ref, v_ref), sems)
    for group in copies:
        for copy in group:
            copy.start()
    for i, group in enumerate(copies):
        for copy in group:
            copy.wait()
        for head in range(i * GROUP, (i + 1) * GROUP):
            columns = slice(head * HD, (head + 1) * HD)
            k_high, k_low = halves(k_ref[:, columns])
            v_high, v_low = halves(v_ref[:, columns])
            first = outer_state(k_high[:middle], k_low[:middle], v_high[:middle], v_low[:middle])
            second = outer_state(k_high[middle:], k_low[middle:], v_high[middle:], v_low[middle:])
            half_ref[head] = first
            total_ref[head] = first + second


def chip_kernel(keep_ref, beside_ref, out_ref):
    out_ref[...] = keep_ref[...] + beside_ref[...]


def tail_kernel(first_ref, second_ref, _, tail_ref):
    rows, width = first_ref.shape
    for part, ref in enumerate((first_ref, second_ref)):
        begin = first_head(part, 2 * width // HD) * HD
        tail_ref[:, pl.ds(pl.multiple_of(begin, HD), width)] = ref[rows - WINDOW :, :]


def weights_of(scores):
    biggest = jnp.max(scores, axis=1, keepdims=True)
    weights = jnp.exp2((scores - biggest) * EXP2_SCALE)
    return weights, jnp.sum(weights, axis=1, keepdims=True)


def masked_pair(weights, below, above):
    high, low = halves(weights)
    return side(high * above, high * below), side(low * above, low * below)


def local_kernel(part, gain_ref, q_hbm, k_ref, v_ref, _, a_ref, b_ref, sum_ref, q_ref, square_ref, sems):
    lower = lower_mask()
    below = jnp.where(lower, 1.0, 0.0).astype(BF16)
    above = jnp.where(lower, 0.0, 1.0).astype(BF16)
    rows, width = a_ref.shape
    tiles = rows // WINDOW
    groups = width // (GROUP * HD)
    begin = first_head(part, 2 * width // HD)

    def load(group):
        there = pl.ds(pl.multiple_of((begin + group * GROUP) * HD, HD), GROUP * HD)
        here = head_columns(group, 1, GROUP * HD)
        return pltpu.make_async_copy(q_hbm.at[:, there], q_ref.at[:, here], sems.at[group])

    for group in range(groups):
        load(group).start()
    square_ref[...] = jnp.zeros_like(square_ref)

    def tile(n):
        return slice(n * WINDOW, (n + 1) * WINDOW)

    @pl.loop(0, groups)
    def _(group):
        load(group).wait()
        scores = []
        for j in range(GROUP):
            columns = head_columns(GROUP * group + j)
            qq = side(*halves(q_ref[:, columns]))
            k_high, k_low = halves(k_ref[:, columns])
            now, before = [], [None]
            for n in range(tiles):
                keys = wide_keys(k_high[tile(n)], k_low[tile(n)])
                found = folded(dot_rows(qq[n * WINDOW : min((n + 2) * WINDOW, rows)], keys))
                now.append(found[:WINDOW])
                before.append(found[WINDOW:])
            scores.append((now, before))
        for j in range(GROUP):
            head = GROUP * group + j
            columns = head_columns(head)
            vv = side(*halves(v_ref[:, columns]))
            now, before = scores[j]
            gain_a = gain_ref[0, begin + head]
            for n in range(tiles):
                inner_high, inner_low = halves(jnp.where(lower, now[n], 0.0))
                if n == 0:
                    wide = dot(stack(inner_high, inner_low), vv[tile(0)])
                    b_ref[tile(0), columns] = folded(wide[:WINDOW]) + wide[WINDOW:, :HD]
                    a_ref[tile(0), columns] = jnp.zeros((WINDOW, HD), F32)
                    continue
                weights, total = weights_of(jnp.where(lower, now[n], before[n]))
                pair_high, pair_low = masked_pair(weights, below, above)
                if n % 2:
                    before_high, before_low = halves(before[n])
                else:
                    before_high = before_low = jnp.zeros((WINDOW, HD), BF16)
                left = jnp.concatenate(
                    [pair_high, pair_low, side(before_high, inner_high), side(before_low, inner_low)], axis=0
                )
                wide = dot(left, vv[(n - 1) * WINDOW : (n + 1) * WINDOW])
                a = (folded(wide[tile(0)]) + wide[tile(1), :HD]) * (gain_a / total)
                a_ref[tile(n), columns] = a
                square_ref[tile(n), :] += a * a
                b_ref[tile(n), columns] = folded(wide[tile(2)]) + wide[tile(3), :HD]

    sum_ref[...] = row_sums(square_ref[...])


def message_kernel(first_ref, chip_ref, _, out_ref):
    index = lax.axis_index("ctx")
    core, x, y = index % 2, (index >> 1) % 2, index >> 2
    first = jnp.where((core == 0) | (y == 1), first_ref[...], 0.0)
    out_ref[...] = first + jnp.where((core == 0) | (x == 0), chip_ref[...], 0.0)


def prefix_kernel(first_ref, second_ref, keep_ref, beside_ref, mine_ref, other_ref):
    index = lax.axis_index("ctx")
    core, x, y = index % 2, (index >> 1) % 2, index >> 2
    use_first = jnp.where(core == 0, x, y) == 1
    use_second = (core == 1) & ((x == 1) | (y == 1)) | (core == 0) & (y == 1)
    earlier = jnp.where(use_first, first_ref[...], 0.0) + jnp.where(use_second, second_ref[...], 0.0)
    mine_ref[...] = earlier + jnp.where(core == 1, beside_ref[...], 0.0)
    other_ref[...] = earlier + jnp.where(core == 0, keep_ref[...], 0.0)


def earlier_kernel(gain_ref, _, *refs):
    state_refs, half_refs, q_refs, b_refs, sum_refs, out_refs = (refs[2 * i : 2 * i + 2] for i in range(6))
    sums_ref, square_ref = refs[12:]
    rows, width = b_refs[0].shape
    middle = rows // 2
    square_ref[...] = jnp.zeros_like(square_ref)
    for part in range(2):
        begin = first_head(part, 2 * width // HD)
        for head in range(width // HD):
            columns = slice(head * HD, (head + 1) * HD)
            state = state_refs[part][head]
            gain_b = gain_ref[1, begin + head]
            for span, held in ((slice(0, middle), state), (slice(middle, rows), state + half_refs[part][head])):
                qq = side(*halves(q_refs[part][span, columns]))
                b = gain_b * (b_refs[part][span, columns] + folded(dot(qq, wide_state(held))))
                out_refs[part][span, columns] = b
                square_ref[span, :] += b * b
    sums = row_sums(square_ref[...])
    row = lax.broadcasted_iota(jnp.int32, sums.shape, 0)
    sums_ref[...] = jnp.where(row == 0, sum(ref[...] for ref in sum_refs), sums)


def first_weights_kernel(gain_ref, *refs):
    q_refs, k_refs, v_refs = (refs[2 * i : 2 * i + 2] for i in range(3))
    tail_ref, weights_ref, out_ref = refs[6:]
    lower = lower_mask()
    reachable = jnp.logical_or(lower, lax.axis_index("ctx") > 0)
    top = slice(0, WINDOW)
    width = q_refs[0].shape[1]
    for part in range(2):
        begin = first_head(part, 2 * width // HD)
        scores = []
        for head in range(width // HD):
            columns = slice(head * HD, (head + 1) * HD)
            qq = side(*halves(q_refs[part][top, columns]))
            now = folded(dot_rows(qq, wide_keys(*halves(k_refs[part][top, columns]))))
            before = folded(dot_rows(qq, wide_keys(*halves(tail_ref[:, head_columns(begin + head)]))))
            scores.append(jnp.where(reachable, jnp.where(lower, now, before), -jnp.inf))
        for head in range(width // HD):
            columns = slice(head * HD, (head + 1) * HD)
            weights, total = weights_of(scores[head])
            weights = weights * (gain_ref[0, begin + head] / total)
            now_high, now_low = halves(jnp.where(lower, weights, 0.0))
            vv = side(*halves(v_refs[part][top, columns]))
            wide = dot(stack(now_high, now_low), vv)
            out_ref[:, part * width + head * HD : part * width + (head + 1) * HD] = (
                folded(wide[:WINDOW]) + wide[WINDOW:, :HD]
            )
            held = slice(2 * (part * width + head * HD), 2 * (part * width + (head + 1) * HD))
            weights_ref[:, held] = side(*halves(jnp.where(lower, 0.0, weights)))


def first_values_kernel(weights_ref, now_ref, tail_ref, _, a_ref, sums_ref):
    square = jnp.zeros((WINDOW, HD), F32)
    heads = now_ref.shape[1] // HD
    for part in range(2):
        begin = first_head(part, heads)
        for head in range(heads // 2):
            j = part * (heads // 2) + head
            columns = slice(j * HD, (j + 1) * HD)
            high = weights_ref[:, 2 * j * HD : (2 * j + 1) * HD]
            low = weights_ref[:, (2 * j + 1) * HD : 2 * (j + 1) * HD]
            wide = dot(stack(high, low), side(*halves(tail_ref[:, head_columns(begin + head)])))
            a = now_ref[:, columns] + (folded(wide[:WINDOW]) + wide[WINDOW:, :HD])
            a_ref[:, columns] = a
            square = square + a * a
    sums_ref[...] = row_sums(square)


def inverse_norm(total):
    return 1.0 / jnp.sqrt(total / (HEADS * HD) + EPS)


def added(refs):
    total = refs[0][...]
    for ref in refs[1:]:
        total = total + ref[...]
    return total


def write(part, rows, held, out_ref, out_hbm, sem):
    width = out_ref.shape[1] // 2
    begin = first_head(part, 2 * width // HD) * HD
    there = pl.ds(pl.multiple_of(begin, HD), width)
    copy = pltpu.make_async_copy(
        out_ref.at[held, pl.ds(part * width, width)], out_hbm.at[rows, there], sem
    )
    copy.start()
    return copy


def scale_kernel(parts, _, *refs):
    sums, refs = refs[:parts], refs[parts:]
    a_refs, b_refs, (out_hbm, out_ref, sems) = refs[:2], refs[2:4], refs[4:]
    inverse = inverse_norm(added(sums)).T
    width = a_refs[0].shape[1]
    copies = []
    for n in range(out_ref.shape[0] // WINDOW):
        held = slice(n * WINDOW, (n + 1) * WINDOW)
        rows = slice((n + 1) * WINDOW, (n + 2) * WINDOW)
        inverse_a, inverse_b = inverse[rows, 0:1], inverse[rows, 1:2]
        for part in range(2):
            columns = slice(part * width, (part + 1) * width)
            out_ref[held, columns] = a_refs[part][rows, :] * inverse_a + b_refs[part][rows, :] * inverse_b
            copies.append(write(part, rows, held, out_ref, out_hbm, sems.at[n, part]))
    for copy in copies:
        copy.wait()


def first_scale_kernel(parts, a_ref, _, *refs):
    b_refs, refs = refs[:2], refs[2:]
    sums, first_sums, (out_hbm, out_ref, sems) = refs[:parts], refs[parts : 2 * parts], refs[2 * parts :]
    inverse_a = inverse_norm(added(first_sums)).T[:, 0:1]
    inverse_b = inverse_norm(added(sums)[:, :WINDOW]).T[:, 1:2]
    width = b_refs[0].shape[1]
    copies = []
    pieces = sems.shape[0]
    for n in range(pieces):
        rows = slice(n * WINDOW // pieces, (n + 1) * WINDOW // pieces)
        for part in range(2):
            columns = slice(part * width, (part + 1) * width)
            out_ref[rows, columns] = (
                a_ref[rows, columns] * inverse_a[rows] + b_refs[part][rows, :] * inverse_b[rows]
            )
            copies.append(write(part, rows, rows, out_ref, out_hbm, sems.at[n, part]))
    for copy in copies:
        copy.wait()


def swap(block, axis, bit):
    return lax.ppermute(block, axis, [(i, i ^ bit) for i in range(lax.axis_size(axis))])


def everyone(block, axis):
    return [block] + [swap(block, axis, bits) for bits in range(1, lax.axis_size(axis))]


def first_phase(chip):
    return lax.ppermute(chip, "ctx", [(i, i ^ (2 if i % 2 == 0 else 4)) for i in range(8)])


def second_phase(message):
    return lax.ppermute(message, "ctx", [(i, i ^ (4 if i % 2 == 0 else 2)) for i in range(8)])


def doubled_prefix(chip):
    index = lax.axis_index("ctx")
    earlier = jnp.zeros_like(chip)
    running = chip
    bit = 2
    while bit < lax.axis_size("ctx"):
        partner = swap(running, "ctx", bit)
        earlier = earlier + jnp.where((index & bit) != 0, partner, 0.0)
        running = running + partner
        bit *= 2
    return earlier


def shards(queries, keys, values, head_gain):
    rows, width = queries.shape
    heads = head_gain.shape[1]
    queries, keys, values = (
        pltpu.with_memory_space_constraint(x, pltpu.HBM) for x in (queries, keys, values)
    )
    smem = pl.BlockSpec(memory_space=pltpu.SMEM)
    anywhere = pl.BlockSpec(memory_space=pl.ANY)
    vmem = pl.BlockSpec()

    def array(*shape, dtype=F32):
        return jax.ShapeDtypeStruct(shape, dtype)

    def call(kernel, name, **kwargs):
        return pl.pallas_call(
            kernel,
            name=name,
            compiler_params=pltpu.CompilerParams(vmem_limit_bytes=VMEM_BYTES),
            cost_estimate=pl.CostEstimate(flops=0, bytes_accessed=0, transcendentals=0),
            **kwargs,
        )

    packed = array(heads // 2, HD, HD)
    half = array(rows, width // 2)
    first_tile = array(WINDOW, width)
    dma = pltpu.SemaphoreType.DMA
    groups = heads // (2 * GROUP)

    def totals(part, after):
        return call(
            functools.partial(totals_kernel, part),
            "totals",
            in_specs=[anywhere] * 3,
            out_shape=[packed, packed, half, half],
            scratch_shapes=[dma((2, groups))],
        )(keys, values, after)

    def local(part, after):
        return call(
            functools.partial(local_kernel, part),
            "local",
            in_specs=[smem, anywhere, vmem, vmem, anywhere],
            out_shape=[half, half, array(8, rows), half],
            scratch_shapes=[pltpu.VMEM((rows, HD), F32), dma((groups,))],
        )(head_gain, queries, held_k[part], held_v[part], after)

    def tail(held, after):
        return call(
            tail_kernel, "tail", in_specs=[vmem, vmem, anywhere], out_shape=first_tile
        )(*held, after)

    route = [(i, i + 1) for i in range(lax.axis_size("ctx") - 1)]
    send, *held_0 = totals(0, queries)
    beside = swap(send, "ctx", 1)
    keep, *held_1 = totals(1, send)
    early, held_k, held_v = zip(held_0, held_1)
    chip = call(chip_kernel, "chip", in_specs=[vmem, vmem], out_shape=packed)(keep, beside)
    before_k = lax.ppermute(tail(held_k, chip), "ctx", route)
    local_0 = local(0, chip)
    message = local_0[2]
    if lax.axis_size("ctx") == 8:
        first = first_phase(chip)
        message = call(
            message_kernel,
            "message",
            in_specs=[vmem, vmem, anywhere],
            out_shape=packed,
        )(first, chip, message)
    window, linear, window_sums, held_q = zip(local_0, local(1, message))
    before_v = lax.ppermute(tail(held_v, window_sums[1]), "ctx", route)
    first_weights, first_now = call(
        first_weights_kernel,
        "first_weights",
        in_specs=[smem] + [vmem] * 7,
        out_shape=[array(WINDOW, 2 * width, dtype=BF16), first_tile],
    )(head_gain, *held_q, *held_k, *held_v, before_k)

    if lax.axis_size("ctx") == 8:
        second = second_phase(message)
        mine, other = call(
            prefix_kernel,
            "prefix",
            out_shape=[packed, packed],
        )(first, second, keep, beside)
    else:
        earlier = doubled_prefix(chip)
        core = lax.axis_index("ctx") % 2
        mine = earlier + jnp.where(core == 1, beside, 0.0)
        other = earlier + jnp.where(core == 0, keep, 0.0)
    other = swap(other, "ctx", 1)

    *linear, sums = call(
        earlier_kernel,
        "earlier",
        in_specs=[smem, anywhere] + [vmem] * 10,
        out_shape=[half, half, array(8, rows)],
        scratch_shapes=[pltpu.VMEM((rows, HD), F32)],
    )(head_gain, first_now, other, mine, *early, *held_q, *linear, *window_sums)
    sums = everyone(sums, "head")
    first_a, first_sums = call(
        first_values_kernel,
        "first_values",
        in_specs=[vmem] * 3 + [anywhere],
        out_shape=[first_tile, array(8, WINDOW)],
    )(first_weights, first_now, before_v, sums[0])
    first_sums = everyone(first_sums, "head")
    out = call(
        functools.partial(scale_kernel, len(sums)),
        "scale",
        in_specs=[anywhere] + [vmem] * (4 + len(sums)),
        out_specs=anywhere,
        out_shape=array(rows, width),
        scratch_shapes=[pltpu.VMEM((rows - WINDOW, width), F32), dma((rows // WINDOW - 1, 2))],
    )(first_sums[0], *sums, *window, *linear)
    return call(
        functools.partial(first_scale_kernel, len(sums)),
        "first_scale",
        in_specs=[vmem, anywhere] + [vmem] * (2 + 2 * len(sums)),
        out_specs=anywhere,
        out_shape=array(rows, width),
        scratch_shapes=[pltpu.VMEM((WINDOW, width), F32), dma((4, 2))],
        input_output_aliases={1: 0},
    )(first_a, out, *linear, *sums, *first_sums)


def solution(mesh):
    in_specs = (P("ctx", "head"), P("ctx", "head"), P("ctx", "head"), P(None, "head"))
    out_specs = P("ctx", "head")
    return jax.shard_map(shards, mesh=mesh, in_specs=in_specs, out_specs=out_specs, check_vma=False)
```

```python
import functools
import math

import jax
import jax.numpy as jnp
from jax import lax
from jax.experimental import pallas as pl
from jax.experimental.pallas import tpu as pltpu
from jax.sharding import PartitionSpec as P

HEADS = 64
HD = 128
WINDOW = 128
EPS = 1e-06
F32 = jnp.float32
BF16 = jnp.bfloat16
EXP2_SCALE = math.log2(math.e) / math.sqrt(HD)
VMEM_BYTES = 20 * 1024 * 1024
GROUP = 4


def halves(x):
    high = x.astype(BF16)
    low = (x - high.astype(F32)).astype(BF16)
    return high, low


def dot(a, b):
    return lax.dot_general(a, b, (((1,), (0,)), ((), ())), preferred_element_type=F32)


def dot_rows(a, b):
    return lax.dot_general(a, b, (((1,), (1,)), ((), ())), preferred_element_type=F32)


def dot_columns(a, b):
    return lax.dot_general(a, b, (((0,), (0,)), ((), ())), preferred_element_type=F32)


def side(a, b):
    return jnp.concatenate([a, b], axis=1)


def stack(a, b):
    return jnp.concatenate([a, b], axis=0)


def outer_state(k_high, k_low, v_high, v_low):
    grid = dot_columns(side(k_high, k_low), side(v_high, v_low))
    return grid[:HD, :HD] + (grid[:HD, HD:] + grid[HD:, :HD]) + grid[HD:, HD:]


def lower_mask():
    rows = lax.broadcasted_iota(jnp.int32, (WINDOW, WINDOW), 0)
    columns = lax.broadcasted_iota(jnp.int32, (WINDOW, WINDOW), 1)
    return rows >= columns


def row_sums(square):
    ones = jnp.ones((8, HD), BF16)
    high, low = halves(square)
    return dot_rows(ones, high) + dot_rows(ones, low)


def wide_keys(k_high, k_low):
    return stack(side(k_high, k_high), side(k_low, jnp.zeros_like(k_low)))


def wide_state(state):
    high, low = halves(state)
    return stack(side(high, low), side(high, jnp.zeros_like(high)))


def folded(wide):
    half = wide.shape[1] // 2
    return wide[:, :half] + wide[:, half:]


def head_columns(head, count=1, width=HD):
    return pl.ds(pl.multiple_of(head * width, width), count * width)


def first_head(part, heads):
    core = lax.axis_index("ctx") % 2
    return jnp.where(core == part, heads // 2, 0)


def column_copies(part, sources, targets, sems):
    begin = first_head(part, sources[0].shape[1] // HD) * HD
    width = GROUP * HD
    copies = []
    for group in range(targets[0].shape[1] // width):
        there = pl.ds(pl.multiple_of(begin + group * width, HD), width)
        here = pl.ds(group * width, width)
        copies.append(
            [
                pltpu.make_async_copy(source.at[:, there], target.at[:, here], sems.at[i, group])
                for i, (source, target) in enumerate(zip(sources, targets))
            ]
        )
    return copies


def totals_kernel(part, k_hbm, v_hbm, _, total_ref, half_ref, k_ref, v_ref, tail_ref, sems):
    middle = k_ref.shape[0] // 2
    copies = column_copies(part, (k_hbm, v_hbm), (k_ref, v_ref), sems)
    for group in copies:
        for copy in group:
            copy.start()
    for i, group in enumerate(copies):
        for copy in group:
            copy.wait()
        for head in range(i * GROUP, (i + 1) * GROUP):
            columns = slice(head * HD, (head + 1) * HD)
            k_high, k_low = halves(k_ref[:, columns])
            v_high, v_low = halves(v_ref[:, columns])
            first = outer_state(k_high[:middle], k_low[:middle], v_high[:middle], v_low[:middle])
            second = outer_state(k_high[middle:], k_low[middle:], v_high[middle:], v_low[middle:])
            half_ref[head] = first
            total_ref[head] = first + second
    tail_ref[...] = k_ref[k_ref.shape[0] - WINDOW :, :]


def chip_kernel(keep_ref, beside_ref, _, out_ref, __):
    out_ref[...] = keep_ref[...] + beside_ref[...]


def tail_kernel(first_ref, second_ref, _, tail_ref):
    rows, width = first_ref.shape
    tail_ref[:, :width] = first_ref[rows - WINDOW :, :]
    tail_ref[:, width:] = second_ref[rows - WINDOW :, :]


def weights_of(scores):
    biggest = jnp.max(scores, axis=1, keepdims=True)
    weights = jnp.exp2((scores - biggest) * EXP2_SCALE)
    return weights, jnp.sum(weights, axis=1, keepdims=True)


def masked_pair(weights, below, above):
    high, low = halves(weights)
    return side(high * above, high * below), side(low * above, low * below)


def local_kernel(part, gain_ref, q_in_ref, k_ref, v_ref, *refs):
    a_ref, b_ref, sum_ref = refs[2:5]
    square_ref = refs[-2]
    lower = lower_mask()
    below = jnp.where(lower, 1.0, 0.0).astype(BF16)
    above = jnp.where(lower, 0.0, 1.0).astype(BF16)
    rows, width = a_ref.shape
    tiles = rows // WINDOW
    groups = width // (GROUP * HD)
    begin = first_head(part, 2 * width // HD)
    if part == 0:
        q_refs, sems = refs[5:7], refs[-1]
        q_ref = q_refs[0]

        def load(number, group):
            there = pl.ds(pl.multiple_of((first_head(number, 2 * width // HD) + group * GROUP) * HD, HD), GROUP * HD)
            here = head_columns(group, 1, GROUP * HD)
            return pltpu.make_async_copy(
                q_in_ref.at[:, there], q_refs[number].at[:, here], sems.at[number, group]
            )

        for number in range(2):
            for group in range(groups):
                load(number, group).start()
    else:
        q_ref = q_in_ref
        square_ref = refs[-1]
    square_ref[...] = jnp.zeros_like(square_ref)

    def tile(n):
        return slice(n * WINDOW, (n + 1) * WINDOW)

    @pl.loop(0, groups)
    def _(group):
        if part == 0:
            load(0, group).wait()
        scores = []
        for j in range(GROUP):
            columns = head_columns(GROUP * group + j)
            qq = side(*halves(q_ref[:, columns]))
            k_high, k_low = halves(k_ref[:, columns])
            now, before = [], [None]
            for n in range(tiles):
                keys = wide_keys(k_high[tile(n)], k_low[tile(n)])
                found = folded(dot_rows(qq[n * WINDOW : min((n + 2) * WINDOW, rows)], keys))
                now.append(found[:WINDOW])
                before.append(found[WINDOW:])
            scores.append((now, before))
        for j in range(GROUP):
            head = GROUP * group + j
            columns = head_columns(head)
            vv = side(*halves(v_ref[:, columns]))
            now, before = scores[j]
            gain_a = gain_ref[0, begin + head]
            for n in range(tiles):
                inner_high, inner_low = halves(jnp.where(lower, now[n], 0.0))
                if n == 0:
                    wide = dot(stack(inner_high, inner_low), vv[tile(0)])
                    b_ref[tile(0), columns] = folded(wide[:WINDOW]) + wide[WINDOW:, :HD]
                    a_ref[tile(0), columns] = jnp.zeros((WINDOW, HD), F32)
                    continue
                weights, total = weights_of(jnp.where(lower, now[n], before[n]))
                pair_high, pair_low = masked_pair(weights, below, above)
                if n % 2:
                    before_high, before_low = halves(before[n])
                else:
                    before_high = before_low = jnp.zeros((WINDOW, HD), BF16)
                left = jnp.concatenate(
                    [pair_high, pair_low, side(before_high, inner_high), side(before_low, inner_low)], axis=0
                )
                wide = dot(left, vv[(n - 1) * WINDOW : (n + 1) * WINDOW])
                a = (folded(wide[tile(0)]) + wide[tile(1), :HD]) * (gain_a / total)
                a_ref[tile(n), columns] = a
                square_ref[tile(n), :] += a * a
                b_ref[tile(n), columns] = folded(wide[tile(2)]) + wide[tile(3), :HD]

    if part == 0:
        for group in range(groups):
            load(1, group).wait()
    sum_ref[...] = row_sums(square_ref[...])


def message_kernel(first_ref, chip_ref, _, out_ref):
    index = lax.axis_index("ctx")
    core, x, y = index % 2, (index >> 1) % 2, index >> 2
    first = jnp.where((core == 0) | (y == 1), first_ref[...], 0.0)
    out_ref[...] = first + jnp.where((core == 0) | (x == 0), chip_ref[...], 0.0)


def prefix_kernel(first_ref, second_ref, keep_ref, beside_ref, _, mine_ref, other_ref):
    index = lax.axis_index("ctx")
    core, x, y = index % 2, (index >> 1) % 2, index >> 2
    use_first = jnp.where(core == 0, x, y) == 1
    use_second = (core == 1) & ((x == 1) | (y == 1)) | (core == 0) & (y == 1)
    earlier = jnp.where(use_first, first_ref[...], 0.0) + jnp.where(use_second, second_ref[...], 0.0)
    mine_ref[...] = earlier + jnp.where(core == 1, beside_ref[...], 0.0)
    other_ref[...] = earlier + jnp.where(core == 0, keep_ref[...], 0.0)


def earlier_kernel(gain_ref, *refs):
    state_refs, half_refs, q_refs, b_refs, sum_refs, out_refs = (refs[2 * i : 2 * i + 2] for i in range(6))
    sums_ref, square_ref = refs[12:]
    rows, width = b_refs[0].shape
    middle = rows // 2
    square_ref[...] = jnp.zeros_like(square_ref)
    for part in range(2):
        begin = first_head(part, 2 * width // HD)
        for head in range(width // HD):
            columns = slice(head * HD, (head + 1) * HD)
            state = state_refs[part][head]
            gain_b = gain_ref[1, begin + head]
            for span, held in ((slice(0, middle), state), (slice(middle, rows), state + half_refs[part][head])):
                qq = side(*halves(q_refs[part][span, columns]))
                b = gain_b * (b_refs[part][span, columns] + folded(dot(qq, wide_state(held))))
                out_refs[part][span, columns] = b
                square_ref[span, :] += b * b
    sums = row_sums(square_ref[...])
    row = lax.broadcasted_iota(jnp.int32, sums.shape, 0)
    sums_ref[...] = jnp.where(row == 0, sum(ref[...] for ref in sum_refs), sums)


def first_weights_kernel(gain_ref, *refs):
    q_refs, k_refs, v_refs = (refs[2 * i : 2 * i + 2] for i in range(3))
    *tail_refs, weights_ref, out_ref = refs[6:]
    lower = lower_mask()
    reachable = jnp.logical_or(lower, lax.axis_index("ctx") > 0)
    top = slice(0, WINDOW)
    width = q_refs[0].shape[1]
    for part in range(2):
        begin = first_head(part, 2 * width // HD)
        scores = []
        for head in range(width // HD):
            columns = slice(head * HD, (head + 1) * HD)
            qq = side(*halves(q_refs[part][top, columns]))
            now = folded(dot_rows(qq, wide_keys(*halves(k_refs[part][top, columns]))))
            before = folded(dot_rows(qq, wide_keys(*halves(tail_refs[part][:, columns]))))
            scores.append(jnp.where(reachable, jnp.where(lower, now, before), -jnp.inf))
        for head in range(width // HD):
            columns = slice(head * HD, (head + 1) * HD)
            weights, total = weights_of(scores[head])
            weights = weights * (gain_ref[0, begin + head] / total)
            now_high, now_low = halves(jnp.where(lower, weights, 0.0))
            vv = side(*halves(v_refs[part][top, columns]))
            wide = dot(stack(now_high, now_low), vv)
            out_ref[:, part * width + head * HD : part * width + (head + 1) * HD] = (
                folded(wide[:WINDOW]) + wide[WINDOW:, :HD]
            )
            held = slice(2 * (part * width + head * HD), 2 * (part * width + (head + 1) * HD))
            weights_ref[:, held] = side(*halves(jnp.where(lower, 0.0, weights)))


def first_values_kernel(weights_ref, now_ref, tail_ref, _, a_ref, sums_ref):
    square = jnp.zeros((WINDOW, HD), F32)
    heads = now_ref.shape[1] // HD
    for part in range(2):
        for head in range(heads // 2):
            j = part * (heads // 2) + head
            sent = (1 - part) * (heads // 2) + head
            columns = slice(j * HD, (j + 1) * HD)
            high = weights_ref[:, 2 * j * HD : (2 * j + 1) * HD]
            low = weights_ref[:, (2 * j + 1) * HD : 2 * (j + 1) * HD]
            wide = dot(stack(high, low), side(*halves(tail_ref[:, sent * HD : (sent + 1) * HD])))
            a = now_ref[:, columns] + (folded(wide[:WINDOW]) + wide[WINDOW:, :HD])
            a_ref[:, columns] = a
            square = square + a * a
    sums_ref[...] = row_sums(square)


def inverse_norm(total):
    return 1.0 / jnp.sqrt(total / (HEADS * HD) + EPS)


def added(refs):
    total = refs[0][...]
    for ref in refs[1:]:
        total = total + ref[...]
    return total


def write(part, rows, held, out_ref, out_hbm, sem):
    width = out_ref.shape[1] // 2
    begin = first_head(part, 2 * width // HD) * HD
    there = pl.ds(pl.multiple_of(begin, HD), width)
    copy = pltpu.make_async_copy(
        out_ref.at[held, pl.ds(part * width, width)], out_hbm.at[rows, there], sem
    )
    copy.start()
    return copy


def scale_kernel(parts, _, *refs):
    sums, refs = refs[:parts], refs[parts:]
    a_refs, b_refs, (out_hbm, out_ref, sems) = refs[:2], refs[2:4], refs[4:]
    inverse = inverse_norm(added(sums)).T
    width = a_refs[0].shape[1]
    copies = []
    for n in range(out_ref.shape[0] // WINDOW):
        held = slice(n * WINDOW, (n + 1) * WINDOW)
        rows = slice((n + 1) * WINDOW, (n + 2) * WINDOW)
        inverse_a, inverse_b = inverse[rows, 0:1], inverse[rows, 1:2]
        for part in range(2):
            columns = slice(part * width, (part + 1) * width)
            out_ref[held, columns] = a_refs[part][rows, :] * inverse_a + b_refs[part][rows, :] * inverse_b
            copies.append(write(part, rows, held, out_ref, out_hbm, sems.at[n, part]))
    for copy in copies:
        copy.wait()


def first_scale_kernel(parts, a_ref, _, *refs):
    b_refs, refs = refs[:2], refs[2:]
    sums, first_sums, (out_hbm, out_ref, sems) = refs[:parts], refs[parts : 2 * parts], refs[2 * parts :]
    inverse_a = inverse_norm(added(first_sums)).T[:, 0:1]
    inverse_b = inverse_norm(added(sums)[:, :WINDOW]).T[:, 1:2]
    width = b_refs[0].shape[1]
    copies = []
    pieces = sems.shape[0]
    for n in range(pieces):
        rows = slice(n * WINDOW // pieces, (n + 1) * WINDOW // pieces)
        for part in range(2):
            columns = slice(part * width, (part + 1) * width)
            out_ref[rows, columns] = (
                a_ref[rows, columns] * inverse_a[rows] + b_refs[part][rows, :] * inverse_b[rows]
            )
            copies.append(write(part, rows, rows, out_ref, out_hbm, sems.at[n, part]))
    for copy in copies:
        copy.wait()


def swap(block, axis, bit):
    return lax.ppermute(block, axis, [(i, i ^ bit) for i in range(lax.axis_size(axis))])


def everyone(block, axis):
    return [block] + [swap(block, axis, bits) for bits in range(1, lax.axis_size(axis))]


def first_phase(chip):
    return lax.ppermute(chip, "ctx", [(i, i ^ (2 if i % 2 == 0 else 4)) for i in range(8)])


def second_phase(message):
    return lax.ppermute(message, "ctx", [(i, i ^ (4 if i % 2 == 0 else 2)) for i in range(8)])


def doubled_prefix(chip):
    index = lax.axis_index("ctx")
    earlier = jnp.zeros_like(chip)
    running = chip
    bit = 2
    while bit < lax.axis_size("ctx"):
        partner = swap(running, "ctx", bit)
        earlier = earlier + jnp.where((index & bit) != 0, partner, 0.0)
        running = running + partner
        bit *= 2
    return earlier


def shards(queries, keys, values, head_gain):
    rows, width = queries.shape
    heads = head_gain.shape[1]
    queries, keys, values = (
        pltpu.with_memory_space_constraint(x, pltpu.HBM) for x in (queries, keys, values)
    )
    smem = pl.BlockSpec(memory_space=pltpu.SMEM)
    anywhere = pl.BlockSpec(memory_space=pl.ANY)
    vmem = pl.BlockSpec()

    def array(*shape, dtype=F32):
        return jax.ShapeDtypeStruct(shape, dtype)

    def call(kernel, name, **kwargs):
        return pl.pallas_call(
            kernel,
            name=name,
            compiler_params=pltpu.CompilerParams(vmem_limit_bytes=VMEM_BYTES),
            cost_estimate=pl.CostEstimate(flops=0, bytes_accessed=0, transcendentals=0),
            **kwargs,
        )

    packed = array(heads // 2, HD, HD)
    half = array(rows, width // 2)
    first_tile = array(WINDOW, width)
    dma = pltpu.SemaphoreType.DMA
    half_tile = array(WINDOW, width // 2)
    groups = heads // (2 * GROUP)

    def totals(part, after):
        return call(
            functools.partial(totals_kernel, part),
            "totals",
            in_specs=[anywhere] * 3,
            out_shape=[packed, packed, half, half, half_tile],
            scratch_shapes=[dma((2, groups))],
        )(keys, values, after)

    def local(part, query_source, *after):
        return call(
            functools.partial(local_kernel, part),
            "local",
            in_specs=[smem, vmem if part else anywhere, vmem, vmem, anywhere, anywhere],
            out_shape=[half, half, array(8, rows)] + ([] if part else [half, half]),
            scratch_shapes=[pltpu.VMEM((rows, HD), F32)] + ([] if part else [dma((2, groups))]),
        )(head_gain, query_source, held_k[part], held_v[part], *after)

    route = [(i, i + 1) for i in range(lax.axis_size("ctx") - 1)]
    send, *held_0, tail_0 = totals(0, queries)
    beside = swap(send, "ctx", 1)
    before_1 = lax.ppermute(tail_0, "ctx", route)
    keep, *held_1, tail_1 = totals(1, send)
    early, held_k, held_v = zip(held_0, held_1)
    chip, tail_1 = call(
        chip_kernel,
        "chip",
        in_specs=[vmem, vmem, anywhere],
        out_specs=[vmem, anywhere],
        out_shape=[packed, half_tile],
        input_output_aliases={2: 1},
    )(keep, beside, tail_1)
    before_0 = lax.ppermute(tail_1, "ctx", route)
    *local_0, query_0, query_1 = local(0, queries, chip, before_1)
    message = local_0[2]
    if lax.axis_size("ctx") == 8:
        first = first_phase(chip)
        message = call(
            message_kernel,
            "message",
            in_specs=[vmem, vmem, anywhere],
            out_shape=packed,
        )(first, chip, message)
    held_q = query_0, query_1
    window, linear, window_sums = zip(local_0, local(1, query_1, message, message))
    tail_v = call(
        tail_kernel, "tail", in_specs=[vmem, vmem, anywhere], out_shape=first_tile
    )(*held_v, window_sums[1])
    before_v = lax.ppermute(tail_v, "ctx", route)
    first_weights, first_now = call(
        first_weights_kernel,
        "first_weights",
        in_specs=[smem] + [vmem] * 8,
        out_shape=[array(WINDOW, 2 * width, dtype=BF16), first_tile],
    )(head_gain, *held_q, *held_k, *held_v, before_0, before_1)

    if lax.axis_size("ctx") == 8:
        second = second_phase(message)
        mine, other = call(
            prefix_kernel,
            "prefix",
            in_specs=[vmem] * 4 + [anywhere],
            out_shape=[packed, packed],
        )(first, second, keep, beside, first_now)
    else:
        earlier = doubled_prefix(chip)
        core = lax.axis_index("ctx") % 2
        mine = earlier + jnp.where(core == 1, beside, 0.0)
        other = earlier + jnp.where(core == 0, keep, 0.0)
    other = swap(other, "ctx", 1)

    *linear, sums = call(
        earlier_kernel,
        "earlier",
        in_specs=[smem] + [vmem] * 10,
        out_shape=[half, half, array(8, rows)],
        scratch_shapes=[pltpu.VMEM((rows, HD), F32)],
    )(head_gain, other, mine, *early, *held_q, *linear, *window_sums)
    sums = everyone(sums, "head")
    first_a, first_sums = call(
        first_values_kernel,
        "first_values",
        in_specs=[vmem] * 3 + [anywhere],
        out_shape=[first_tile, array(8, WINDOW)],
    )(first_weights, first_now, before_v, sums[0])
    first_sums = everyone(first_sums, "head")
    out = call(
        functools.partial(scale_kernel, len(sums)),
        "scale",
        in_specs=[anywhere] + [vmem] * (4 + len(sums)),
        out_specs=anywhere,
        out_shape=array(rows, width),
        scratch_shapes=[pltpu.VMEM((rows - WINDOW, width), F32), dma((rows // WINDOW - 1, 2))],
    )(first_sums[0], *sums, *window, *linear)
    return call(
        functools.partial(first_scale_kernel, len(sums)),
        "first_scale",
        in_specs=[vmem, anywhere] + [vmem] * (2 + 2 * len(sums)),
        out_specs=anywhere,
        out_shape=array(rows, width),
        scratch_shapes=[pltpu.VMEM((WINDOW, width), F32), dma((4, 2))],
        input_output_aliases={1: 0},
    )(first_a, out, *linear, *sums, *first_sums)


def solution(mesh):
    in_specs = (P("ctx", "head"), P("ctx", "head"), P("ctx", "head"), P(None, "head"))
    out_specs = P("ctx", "head")
    return jax.shard_map(shards, mesh=mesh, in_specs=in_specs, out_specs=out_specs, check_vma=False)
```

```python
import functools
import math

import jax
import jax.numpy as jnp
from jax import lax
from jax.experimental import pallas as pl
from jax.experimental.pallas import tpu as pltpu
from jax.sharding import PartitionSpec as P

HEADS = 64
HD = 128
WINDOW = 128
EPS = 1e-06
F32 = jnp.float32
BF16 = jnp.bfloat16
EXP2_SCALE = math.log2(math.e) / math.sqrt(HD)
VMEM_BYTES = 20 * 1024 * 1024
GROUP = 4


def halves(x):
    high = x.astype(BF16)
    low = (x - high.astype(F32)).astype(BF16)
    return high, low


def dot(a, b):
    return lax.dot_general(a, b, (((1,), (0,)), ((), ())), preferred_element_type=F32)


def dot_rows(a, b):
    return lax.dot_general(a, b, (((1,), (1,)), ((), ())), preferred_element_type=F32)


def dot_columns(a, b):
    return lax.dot_general(a, b, (((0,), (0,)), ((), ())), preferred_element_type=F32)


def side(a, b):
    return jnp.concatenate([a, b], axis=1)


def stack(a, b):
    return jnp.concatenate([a, b], axis=0)


def outer_state(k_high, k_low, v_high, v_low):
    grid = dot_columns(side(k_high, k_low), side(v_high, v_low))
    return grid[:HD, :HD] + (grid[:HD, HD:] + grid[HD:, :HD]) + grid[HD:, HD:]


def lower_mask():
    rows = lax.broadcasted_iota(jnp.int32, (WINDOW, WINDOW), 0)
    columns = lax.broadcasted_iota(jnp.int32, (WINDOW, WINDOW), 1)
    return rows >= columns


def row_sums(square):
    ones = jnp.ones((8, HD), BF16)
    high, low = halves(square)
    return dot_rows(ones, high) + dot_rows(ones, low)


def wide_keys(k_high, k_low):
    return stack(side(k_high, k_high), side(k_low, jnp.zeros_like(k_low)))


def wide_state(state):
    high, low = halves(state)
    return stack(side(high, low), side(high, jnp.zeros_like(high)))


def folded(wide):
    half = wide.shape[1] // 2
    return wide[:, :half] + wide[:, half:]


def head_columns(head, count=1, width=HD):
    return pl.ds(pl.multiple_of(head * width, width), count * width)


def load_kernel(q_hbm, _, q_ref, sems):
    width = q_ref.shape[1] // sems.shape[0]
    copies = []
    for i in range(sems.shape[0]):
        columns = pl.ds(i * width, width)
        copies.append(pltpu.make_async_copy(q_hbm.at[:, columns], q_ref.at[:, columns], sems.at[i]))
    for copy in copies:
        copy.start()
    for copy in copies:
        copy.wait()


def tail_kernel(k_ref, tail_ref, sem):
    rows = k_ref.shape[0]
    copy = pltpu.make_async_copy(k_ref.at[pl.ds(rows - WINDOW, WINDOW), :], tail_ref, sem)
    copy.start()
    copy.wait()


def pass_kernel(*_):
    pass


def chip_kernel(keep_ref, beside_ref, out_ref):
    out_ref[...] = keep_ref[...] + beside_ref[...]


def totals_kernel(k_hbm, v_hbm, keep_ref, send_ref, half_ref, k_ref, v_ref, tail_v_ref, sems):
    core = lax.axis_index("ctx") % 2
    rows, width = k_ref.shape
    middle = rows // 2
    groups = width // (GROUP * HD)

    def copies(group):
        columns = head_columns(group, 1, GROUP * HD)
        return [
            pltpu.make_async_copy(source.at[:, columns], target.at[:, columns], sems.at[i, group])
            for i, (source, target) in enumerate(((k_hbm, k_ref), (v_hbm, v_ref)))
        ]

    for group in range(groups):
        for copy in copies(group):
            copy.start()

    @pl.loop(0, groups)
    def _(group):
        for copy in copies(group):
            copy.wait()
        for i in range(GROUP // 2):
            states = []
            for j in (2 * i, 2 * i + 1):
                head = GROUP * group + j
                columns = head_columns(head)
                k_high, k_low = halves(k_ref[:, columns])
                v_high, v_low = halves(v_ref[:, columns])
                first = outer_state(k_high[:middle], k_low[:middle], v_high[:middle], v_low[:middle])
                second = outer_state(k_high[middle:], k_low[middle:], v_high[middle:], v_low[middle:])
                half_ref[head] = first
                states.append(first + second)
            pair = GROUP // 2 * group + i
            keep_ref[pair] = jnp.where(core == 0, states[0], states[1])
            send_ref[pair] = jnp.where(core == 0, states[1], states[0])
        columns = head_columns(group, 1, GROUP * HD)
        tail_v_ref[:, columns] = v_ref[rows - WINDOW :, columns]


def weights_of(scores):
    biggest = jnp.max(scores, axis=1, keepdims=True)
    weights = jnp.exp2((scores - biggest) * EXP2_SCALE)
    return weights, jnp.sum(weights, axis=1, keepdims=True)


def masked_pair(weights, below, above):
    high, low = halves(weights)
    return side(high * above, high * below), side(low * above, low * below)


def local_kernel(begin, extra, gain_ref, q_ref, k_ref, v_ref, *refs):
    a_ref, b_ref, sum_ref, square_ref = refs[extra:]
    lower = lower_mask()
    below = jnp.where(lower, 1.0, 0.0).astype(BF16)
    above = jnp.where(lower, 0.0, 1.0).astype(BF16)
    rows, width = a_ref.shape
    tiles = rows // WINDOW
    groups = width // (GROUP * HD)
    square_ref[...] = jnp.zeros_like(square_ref)

    def tile(n):
        return slice(n * WINDOW, (n + 1) * WINDOW)

    @pl.loop(0, groups)
    def _(group):
        scores = []
        for j in range(GROUP):
            columns = head_columns(begin + GROUP * group + j)
            qq = side(*halves(q_ref[:, columns]))
            k_high, k_low = halves(k_ref[:, columns])
            now, before = [], [None]
            for n in range(tiles):
                keys = wide_keys(k_high[tile(n)], k_low[tile(n)])
                found = folded(dot_rows(qq[n * WINDOW : min((n + 2) * WINDOW, rows)], keys))
                now.append(found[:WINDOW])
                before.append(found[WINDOW:])
            scores.append((now, before))
        for j in range(GROUP):
            head = GROUP * group + j
            columns = head_columns(head)
            vv = side(*halves(v_ref[:, head_columns(begin + head)]))
            now, before = scores[j]
            gain_a = gain_ref[0, begin + head]
            for n in range(tiles):
                inner_high, inner_low = halves(jnp.where(lower, now[n], 0.0))
                if n == 0:
                    wide = dot(stack(inner_high, inner_low), vv[tile(0)])
                    b_ref[tile(0), columns] = folded(wide[:WINDOW]) + wide[WINDOW:, :HD]
                    a_ref[tile(0), columns] = jnp.zeros((WINDOW, HD), F32)
                    continue
                weights, total = weights_of(jnp.where(lower, now[n], before[n]))
                pair_high, pair_low = masked_pair(weights, below, above)
                if n % 2:
                    before_high, before_low = halves(before[n])
                else:
                    before_high = before_low = jnp.zeros((WINDOW, HD), BF16)
                left = jnp.concatenate(
                    [pair_high, pair_low, side(before_high, inner_high), side(before_low, inner_low)], axis=0
                )
                wide = dot(left, vv[(n - 1) * WINDOW : (n + 1) * WINDOW])
                a = (folded(wide[tile(0)]) + wide[tile(1), :HD]) * (gain_a / total)
                a_ref[tile(n), columns] = a
                square_ref[tile(n), :] += a * a
                b_ref[tile(n), columns] = folded(wide[tile(2)]) + wide[tile(3), :HD]

    sum_ref[...] = row_sums(square_ref[...])


def message_kernel(first_ref, chip_ref, _, out_ref):
    index = lax.axis_index("ctx")
    core, x, y = index % 2, (index >> 1) % 2, index >> 2
    first = jnp.where((core == 0) | (y == 1), first_ref[...], 0.0)
    out_ref[...] = first + jnp.where((core == 0) | (x == 0), chip_ref[...], 0.0)


def prefix_kernel(first_ref, second_ref, keep_ref, beside_ref, *refs):
    mine_ref, other_ref = refs[-2:]
    index = lax.axis_index("ctx")
    core, x, y = index % 2, (index >> 1) % 2, index >> 2
    use_first = jnp.where(core == 0, x, y) == 1
    use_second = (core == 1) & ((x == 1) | (y == 1)) | (core == 0) & (y == 1)
    earlier = jnp.where(use_first, first_ref[...], 0.0) + jnp.where(use_second, second_ref[...], 0.0)
    mine_ref[...] = earlier + jnp.where(core == 1, beside_ref[...], 0.0)
    other_ref[...] = earlier + jnp.where(core == 0, keep_ref[...], 0.0)


def earlier_kernel(count, gain_ref, half_ref, mine_ref, other_ref, q_ref, *refs):
    b_refs, sum_refs, out_refs = (refs[i * count : (i + 1) * count] for i in range(3))
    sums_ref, square_ref = refs[3 * count :]
    core = lax.axis_index("ctx") % 2
    rows = b_refs[0].shape[0]
    middle = rows // 2
    head = 0
    square_ref[...] = jnp.zeros_like(square_ref)
    for b_ref, out_ref in zip(b_refs, out_refs):
        for j in range(b_ref.shape[1] // HD):
            columns = slice(j * HD, (j + 1) * HD)
            state = jnp.where(core == head % 2, mine_ref[head // 2], other_ref[head // 2])
            gain_b = gain_ref[1, head]
            for part, held in ((slice(0, middle), state), (slice(middle, rows), state + half_ref[head])):
                qq = side(*halves(q_ref[part, head * HD : (head + 1) * HD]))
                b = gain_b * (b_ref[part, columns] + folded(dot(qq, wide_state(held))))
                out_ref[part, columns] = b
                square_ref[part, :] += b * b
            head += 1
    sums = row_sums(square_ref[...])
    row = lax.broadcasted_iota(jnp.int32, sums.shape, 0)
    sums_ref[...] = jnp.where(row == 0, sum(ref[...] for ref in sum_refs), sums)


def first_weights_kernel(gain_ref, q_ref, k_ref, v_ref, tail_ref, weights_ref, out_ref):
    lower = lower_mask()
    reachable = jnp.logical_or(lower, lax.axis_index("ctx") > 0)
    top = slice(0, WINDOW)
    count = tail_ref.shape[1] // (2 * HD)
    for part in range(2):
        scores = []
        for j in range(count):
            columns = slice((part * count + j) * HD, (part * count + j + 1) * HD)
            qq = side(*halves(q_ref[top, columns]))
            now = folded(dot_rows(qq, wide_keys(*halves(k_ref[top, columns]))))
            before = folded(dot_rows(qq, wide_keys(*halves(tail_ref[:, columns]))))
            scores.append(jnp.where(reachable, jnp.where(lower, now, before), -jnp.inf))
        for j in range(count):
            head = part * count + j
            columns = slice(head * HD, (head + 1) * HD)
            weights, total = weights_of(scores[j])
            weights = weights * (gain_ref[0, head] / total)
            now_high, now_low = halves(jnp.where(lower, weights, 0.0))
            vv = side(*halves(v_ref[top, columns]))
            wide = dot(stack(now_high, now_low), vv)
            out_ref[:, columns] = folded(wide[:WINDOW]) + wide[WINDOW:, :HD]
            weights_ref[:, 2 * head * HD : 2 * (head + 1) * HD] = side(*halves(jnp.where(lower, 0.0, weights)))


def first_values_kernel(weights_ref, now_ref, tail_v_ref, _, a_ref, sums_ref):
    square = jnp.zeros((WINDOW, HD), F32)
    for j in range(now_ref.shape[1] // HD):
        columns = slice(j * HD, (j + 1) * HD)
        high = weights_ref[:, 2 * j * HD : (2 * j + 1) * HD]
        low = weights_ref[:, (2 * j + 1) * HD : 2 * (j + 1) * HD]
        wide = dot(stack(high, low), side(*halves(tail_v_ref[:, columns])))
        a = now_ref[:, columns] + (folded(wide[:WINDOW]) + wide[WINDOW:, :HD])
        a_ref[:, columns] = a
        square = square + a * a
    sums_ref[...] = row_sums(square)


def inverse_norm(total):
    return 1.0 / jnp.sqrt(total / (HEADS * HD) + EPS)


def added(refs):
    total = refs[0][...]
    for ref in refs[1:]:
        total = total + ref[...]
    return total


def scale_kernel(count, parts, _, *refs):
    sums, refs = refs[:parts], refs[parts:]
    a_refs, b_refs, (out_hbm, out_ref, sems) = refs[:count], refs[count : 2 * count], refs[2 * count :]
    inverse = inverse_norm(added(sums)).T
    copies = []
    for n in range(out_ref.shape[0] // WINDOW):
        held = slice(n * WINDOW, (n + 1) * WINDOW)
        rows = slice((n + 1) * WINDOW, (n + 2) * WINDOW)
        inverse_a, inverse_b = inverse[rows, 0:1], inverse[rows, 1:2]
        begin = 0
        for a_ref, b_ref in zip(a_refs, b_refs):
            columns = slice(begin, begin + a_ref.shape[1])
            out_ref[held, columns] = a_ref[rows, :] * inverse_a + b_ref[rows, :] * inverse_b
            begin = columns.stop
        copy = pltpu.make_async_copy(out_ref.at[held, :], out_hbm.at[rows, :], sems.at[n])
        copy.start()
        copies.append(copy)
    for copy in copies:
        copy.wait()


def first_scale_kernel(count, parts, a_ref, _, *refs):
    b_refs, refs = refs[:count], refs[count:]
    sums, first_sums, (out_hbm, out_ref, sems) = refs[:parts], refs[parts : 2 * parts], refs[2 * parts :]
    inverse_a = inverse_norm(added(first_sums)).T[:, 0:1]
    inverse_b = inverse_norm(added(sums)[:, :WINDOW]).T[:, 1:2]
    copies = []
    for n in range(sems.shape[0]):
        rows = slice(n * WINDOW // sems.shape[0], (n + 1) * WINDOW // sems.shape[0])
        begin = 0
        for b_ref in b_refs:
            columns = slice(begin, begin + b_ref.shape[1])
            out_ref[rows, columns] = a_ref[rows, columns] * inverse_a[rows] + b_ref[rows, :] * inverse_b[rows]
            begin = columns.stop
        copy = pltpu.make_async_copy(out_ref.at[rows, :], out_hbm.at[rows, :], sems.at[n])
        copy.start()
        copies.append(copy)
    for copy in copies:
        copy.wait()


def swap(block, axis, bit):
    return lax.ppermute(block, axis, [(i, i ^ bit) for i in range(lax.axis_size(axis))])


def everyone(block, axis):
    return [block] + [swap(block, axis, bits) for bits in range(1, lax.axis_size(axis))]


def first_phase(chip):
    return lax.ppermute(chip, "ctx", [(i, i ^ (2 if i % 2 == 0 else 4)) for i in range(8)])


def second_phase(message):
    return lax.ppermute(message, "ctx", [(i, i ^ (4 if i % 2 == 0 else 2)) for i in range(8)])


def doubled_prefix(chip):
    index = lax.axis_index("ctx")
    earlier = jnp.zeros_like(chip)
    running = chip
    bit = 2
    while bit < lax.axis_size("ctx"):
        partner = swap(running, "ctx", bit)
        earlier = earlier + jnp.where((index & bit) != 0, partner, 0.0)
        running = running + partner
        bit *= 2
    return earlier


def shards(queries, keys, values, head_gain):
    rows, width = queries.shape
    heads = head_gain.shape[1]
    queries, keys, values = (
        pltpu.with_memory_space_constraint(x, pltpu.HBM) for x in (queries, keys, values)
    )
    smem = pl.BlockSpec(memory_space=pltpu.SMEM)
    anywhere = pl.BlockSpec(memory_space=pl.ANY)
    vmem = pl.BlockSpec()

    def array(*shape, dtype=F32):
        return jax.ShapeDtypeStruct(shape, dtype)

    def call(kernel, name, **kwargs):
        return pl.pallas_call(
            kernel,
            name=name,
            compiler_params=pltpu.CompilerParams(vmem_limit_bytes=VMEM_BYTES),
            cost_estimate=pl.CostEstimate(flops=0, bytes_accessed=0, transcendentals=0),
            **kwargs,
        )

    packed = array(heads // 2, HD, HD)
    first_tile = array(WINDOW, width)
    dma = pltpu.SemaphoreType.DMA
    route = [(i, i + 1) for i in range(lax.axis_size("ctx") - 1)]
    tail_k = call(
        tail_kernel, "tail", in_specs=[anywhere], out_shape=first_tile, scratch_shapes=[dma]
    )(keys)
    before_k = lax.ppermute(tail_k, "ctx", route)
    keep, send, half, held_k, held_v, tail_v = call(
        totals_kernel,
        "totals",
        in_specs=[anywhere, anywhere],
        out_shape=[
            packed,
            packed,
            array(heads, HD, HD),
            array(rows, width),
            array(rows, width),
            first_tile,
        ],
        scratch_shapes=[dma((2, heads // GROUP))],
    )(keys, values)
    beside = swap(send, "ctx", 1)
    chip = call(chip_kernel, "chip", in_specs=[vmem, vmem], out_shape=packed)(keep, beside)
    held_q = call(
        load_kernel,
        "load",
        in_specs=[anywhere, anywhere],
        out_shape=array(rows, width),
        scratch_shapes=[dma((4,))],
    )(queries, chip)

    def local(begin, count, after):
        taken = count * HD
        after = [] if after is None else [after]
        return call(
            functools.partial(local_kernel, begin, len(after)),
            "local",
            in_specs=[smem, vmem, vmem, vmem] + [anywhere] * len(after),
            out_shape=[array(rows, taken), array(rows, taken), array(8, rows)],
            scratch_shapes=[pltpu.VMEM((rows, HD), F32)],
        )(head_gain, held_q, held_k, held_v, *after)

    def pass_on(array_now, after):
        return call(
            pass_kernel,
            "pass",
            in_specs=[anywhere, anywhere],
            out_specs=anywhere,
            out_shape=array(*array_now.shape),
            input_output_aliases={0: 0},
        )(array_now, after)

    begin = heads // 2
    parts = [local(0, begin, before_k)]
    message = None
    if lax.axis_size("ctx") == 8:
        first = first_phase(chip)
        message = call(
            message_kernel,
            "message",
            in_specs=[vmem, vmem, anywhere],
            out_shape=packed,
        )(first, chip, parts[0][2])
    parts.append(local(begin, heads - begin, message))
    window, linear, window_sums = zip(*parts)
    before_v = lax.ppermute(pass_on(tail_v, window_sums[1]), "ctx", route)
    first_weights, first_now = call(
        first_weights_kernel,
        "first_weights",
        in_specs=[smem] + [vmem] * 4,
        out_shape=[array(WINDOW, 2 * width, dtype=BF16), first_tile],
    )(head_gain, held_q, held_k, held_v, before_k)

    if message is not None:
        second = second_phase(message)
        mine, other = call(
            prefix_kernel,
            "prefix",
            in_specs=[vmem] * 4 + [anywhere],
            out_shape=[packed, packed],
        )(first, second, keep, beside, first_now)
    else:
        earlier = doubled_prefix(chip)
        core = lax.axis_index("ctx") % 2
        mine = earlier + jnp.where(core == 1, beside, 0.0)
        other = earlier + jnp.where(core == 0, keep, 0.0)
    other = swap(other, "ctx", 1)

    *linear, sums = call(
        functools.partial(earlier_kernel, len(parts)),
        "earlier",
        in_specs=[smem] + [vmem] * (4 + 2 * len(parts)),
        out_shape=[array(*x.shape) for x in linear] + [array(8, rows)],
        scratch_shapes=[pltpu.VMEM((rows, HD), F32)],
    )(head_gain, half, mine, other, held_q, *linear, *window_sums)
    sums = everyone(sums, "head")
    first_a, first_sums = call(
        first_values_kernel,
        "first_values",
        in_specs=[vmem] * 3 + [anywhere],
        out_shape=[first_tile, array(8, WINDOW)],
    )(first_weights, first_now, before_v, sums[0])
    first_sums = everyone(first_sums, "head")
    out = call(
        functools.partial(scale_kernel, len(parts), len(sums)),
        "scale",
        in_specs=[anywhere] + [vmem] * (2 * len(parts) + len(sums)),
        out_specs=anywhere,
        out_shape=array(rows, width),
        scratch_shapes=[pltpu.VMEM((rows - WINDOW, width), F32), dma((rows // WINDOW - 1,))],
    )(first_sums[0], *sums, *window, *linear)
    return call(
        functools.partial(first_scale_kernel, len(parts), len(sums)),
        "first_scale",
        in_specs=[vmem, anywhere] + [vmem] * (len(parts) + 2 * len(sums)),
        out_specs=anywhere,
        out_shape=array(rows, width),
        scratch_shapes=[pltpu.VMEM((WINDOW, width), F32), dma((4,))],
        input_output_aliases={1: 0},
    )(first_a, out, *linear, *sums, *first_sums)


def solution(mesh):
    in_specs = (P("ctx", "head"), P("ctx", "head"), P("ctx", "head"), P(None, "head"))
    out_specs = P("ctx", "head")
    return jax.shard_map(shards, mesh=mesh, in_specs=in_specs, out_specs=out_specs, check_vma=False)
```

```python
import functools
import math

import jax
import jax.numpy as jnp
from jax import lax
from jax.experimental import pallas as pl
from jax.experimental.pallas import tpu as pltpu
from jax.sharding import PartitionSpec as P

HEADS = 64
HD = 128
WINDOW = 128
EPS = 1e-06
F32 = jnp.float32
BF16 = jnp.bfloat16
EXP2_SCALE = math.log2(math.e) / math.sqrt(HD)
VMEM_BYTES = 20 * 1024 * 1024
GROUP = 4


def halves(x):
    high = x.astype(BF16)
    low = (x - high.astype(F32)).astype(BF16)
    return high, low


def dot(a, b):
    return lax.dot_general(a, b, (((1,), (0,)), ((), ())), preferred_element_type=F32)


def dot_rows(a, b):
    return lax.dot_general(a, b, (((1,), (1,)), ((), ())), preferred_element_type=F32)


def dot_columns(a, b):
    return lax.dot_general(a, b, (((0,), (0,)), ((), ())), preferred_element_type=F32)


def side(a, b):
    return jnp.concatenate([a, b], axis=1)


def stack(a, b):
    return jnp.concatenate([a, b], axis=0)


def outer_state(k_high, k_low, v_high, v_low):
    grid = dot_columns(side(k_high, k_low), side(v_high, v_low))
    return grid[:HD, :HD] + (grid[:HD, HD:] + grid[HD:, :HD]) + grid[HD:, HD:]


def lower_mask():
    rows = lax.broadcasted_iota(jnp.int32, (WINDOW, WINDOW), 0)
    columns = lax.broadcasted_iota(jnp.int32, (WINDOW, WINDOW), 1)
    return rows >= columns


def row_sums(square):
    ones = jnp.ones((8, HD), BF16)
    high, low = halves(square)
    return dot_rows(ones, high) + dot_rows(ones, low)


def wide_keys(k_high, k_low):
    return stack(side(k_high, k_high), side(k_low, jnp.zeros_like(k_low)))


def wide_state(state):
    high, low = halves(state)
    return stack(side(high, low), side(high, jnp.zeros_like(high)))


def folded(wide):
    half = wide.shape[1] // 2
    return wide[:, :half] + wide[:, half:]


def head_columns(head, count=1, width=HD):
    return pl.ds(pl.multiple_of(head * width, width), count * width)


def first_head(part, heads):
    core = lax.axis_index("ctx") % 2
    return jnp.where(core == part, heads // 2, 0)


def column_copies(part, sources, targets, sems):
    begin = first_head(part, sources[0].shape[1] // HD) * HD
    width = GROUP * HD
    copies = []
    for group in range(targets[0].shape[1] // width):
        there = pl.ds(pl.multiple_of(begin + group * width, HD), width)
        here = pl.ds(group * width, width)
        copies.append(
            [
                pltpu.make_async_copy(source.at[:, there], target.at[:, here], sems.at[i, group])
                for i, (source, target) in enumerate(zip(sources, targets))
            ]
        )
    return copies


def totals_kernel(part, k_hbm, v_hbm, _, total_ref, half_ref, k_ref, v_ref, sems):
    middle = k_ref.shape[0] // 2
    copies = column_copies(part, (k_hbm, v_hbm), (k_ref, v_ref), sems)
    for group in copies:
        for copy in group:
            copy.start()
    for i, group in enumerate(copies):
        for copy in group:
            copy.wait()
        for head in range(i * GROUP, (i + 1) * GROUP):
            columns = slice(head * HD, (head + 1) * HD)
            k_high, k_low = halves(k_ref[:, columns])
            v_high, v_low = halves(v_ref[:, columns])
            first = outer_state(k_high[:middle], k_low[:middle], v_high[:middle], v_low[:middle])
            second = outer_state(k_high[middle:], k_low[middle:], v_high[middle:], v_low[middle:])
            half_ref[head] = first
            total_ref[head] = first + second


def chip_kernel(keep_ref, beside_ref, first_ref, second_ref, out_ref, tail_ref):
    out_ref[...] = keep_ref[...] + beside_ref[...]
    rows, width = first_ref.shape
    tail_ref[:, :width] = first_ref[rows - WINDOW :, :]
    tail_ref[:, width:] = second_ref[rows - WINDOW :, :]


def tail_kernel(first_ref, second_ref, _, tail_ref):
    rows, width = first_ref.shape
    tail_ref[:, :width] = first_ref[rows - WINDOW :, :]
    tail_ref[:, width:] = second_ref[rows - WINDOW :, :]


def weights_of(scores):
    biggest = jnp.max(scores, axis=1, keepdims=True)
    weights = jnp.exp2((scores - biggest) * EXP2_SCALE)
    return weights, jnp.sum(weights, axis=1, keepdims=True)


def masked_pair(weights, below, above):
    high, low = halves(weights)
    return side(high * above, high * below), side(low * above, low * below)


def local_kernel(part, gain_ref, q_in_ref, k_ref, v_ref, *refs):
    a_ref, b_ref, sum_ref = refs[1:4]
    square_ref = refs[-2]
    lower = lower_mask()
    below = jnp.where(lower, 1.0, 0.0).astype(BF16)
    above = jnp.where(lower, 0.0, 1.0).astype(BF16)
    rows, width = a_ref.shape
    tiles = rows // WINDOW
    groups = width // (GROUP * HD)
    begin = first_head(part, 2 * width // HD)
    if part == 0:
        q_refs, sems = refs[4:6], refs[-1]
        q_ref = q_refs[0]

        def load(number, group):
            there = pl.ds(pl.multiple_of((first_head(number, 2 * width // HD) + group * GROUP) * HD, HD), GROUP * HD)
            here = head_columns(group, 1, GROUP * HD)
            return pltpu.make_async_copy(
                q_in_ref.at[:, there], q_refs[number].at[:, here], sems.at[number, group]
            )

        for number in range(2):
            for group in range(groups):
                load(number, group).start()
    else:
        q_ref = q_in_ref
        square_ref = refs[-1]
    square_ref[...] = jnp.zeros_like(square_ref)

    def tile(n):
        return slice(n * WINDOW, (n + 1) * WINDOW)

    @pl.loop(0, groups)
    def _(group):
        if part == 0:
            load(0, group).wait()
        scores = []
        for j in range(GROUP):
            columns = head_columns(GROUP * group + j)
            qq = side(*halves(q_ref[:, columns]))
            k_high, k_low = halves(k_ref[:, columns])
            now, before = [], [None]
            for n in range(tiles):
                keys = wide_keys(k_high[tile(n)], k_low[tile(n)])
                found = folded(dot_rows(qq[n * WINDOW : min((n + 2) * WINDOW, rows)], keys))
                now.append(found[:WINDOW])
                before.append(found[WINDOW:])
            scores.append((now, before))
        for j in range(GROUP):
            head = GROUP * group + j
            columns = head_columns(head)
            vv = side(*halves(v_ref[:, columns]))
            now, before = scores[j]
            gain_a = gain_ref[0, begin + head]
            for n in range(tiles):
                inner_high, inner_low = halves(jnp.where(lower, now[n], 0.0))
                if n == 0:
                    wide = dot(stack(inner_high, inner_low), vv[tile(0)])
                    b_ref[tile(0), columns] = folded(wide[:WINDOW]) + wide[WINDOW:, :HD]
                    a_ref[tile(0), columns] = jnp.zeros((WINDOW, HD), F32)
                    continue
                weights, total = weights_of(jnp.where(lower, now[n], before[n]))
                pair_high, pair_low = masked_pair(weights, below, above)
                if n % 2:
                    before_high, before_low = halves(before[n])
                else:
                    before_high = before_low = jnp.zeros((WINDOW, HD), BF16)
                left = jnp.concatenate(
                    [pair_high, pair_low, side(before_high, inner_high), side(before_low, inner_low)], axis=0
                )
                wide = dot(left, vv[(n - 1) * WINDOW : (n + 1) * WINDOW])
                a = (folded(wide[tile(0)]) + wide[tile(1), :HD]) * (gain_a / total)
                a_ref[tile(n), columns] = a
                square_ref[tile(n), :] += a * a
                b_ref[tile(n), columns] = folded(wide[tile(2)]) + wide[tile(3), :HD]

    if part == 0:
        for group in range(groups):
            load(1, group).wait()
    sum_ref[...] = row_sums(square_ref[...])


def message_kernel(first_ref, chip_ref, _, out_ref):
    index = lax.axis_index("ctx")
    core, x, y = index % 2, (index >> 1) % 2, index >> 2
    first = jnp.where((core == 0) | (y == 1), first_ref[...], 0.0)
    out_ref[...] = first + jnp.where((core == 0) | (x == 0), chip_ref[...], 0.0)


def prefix_kernel(first_ref, second_ref, keep_ref, beside_ref, _, mine_ref, other_ref):
    index = lax.axis_index("ctx")
    core, x, y = index % 2, (index >> 1) % 2, index >> 2
    use_first = jnp.where(core == 0, x, y) == 1
    use_second = (core == 1) & ((x == 1) | (y == 1)) | (core == 0) & (y == 1)
    earlier = jnp.where(use_first, first_ref[...], 0.0) + jnp.where(use_second, second_ref[...], 0.0)
    mine_ref[...] = earlier + jnp.where(core == 1, beside_ref[...], 0.0)
    other_ref[...] = earlier + jnp.where(core == 0, keep_ref[...], 0.0)


def earlier_kernel(gain_ref, *refs):
    state_refs, half_refs, q_refs, b_refs, sum_refs, out_refs = (refs[2 * i : 2 * i + 2] for i in range(6))
    sums_ref, square_ref = refs[12:]
    rows, width = b_refs[0].shape
    middle = rows // 2
    square_ref[...] = jnp.zeros_like(square_ref)
    for part in range(2):
        begin = first_head(part, 2 * width // HD)
        for head in range(width // HD):
            columns = slice(head * HD, (head + 1) * HD)
            state = state_refs[part][head]
            gain_b = gain_ref[1, begin + head]
            for span, held in ((slice(0, middle), state), (slice(middle, rows), state + half_refs[part][head])):
                qq = side(*halves(q_refs[part][span, columns]))
                b = gain_b * (b_refs[part][span, columns] + folded(dot(qq, wide_state(held))))
                out_refs[part][span, columns] = b
                square_ref[span, :] += b * b
    sums = row_sums(square_ref[...])
    row = lax.broadcasted_iota(jnp.int32, sums.shape, 0)
    sums_ref[...] = jnp.where(row == 0, sum(ref[...] for ref in sum_refs), sums)


def first_weights_kernel(gain_ref, *refs):
    q_refs, k_refs, v_refs = (refs[2 * i : 2 * i + 2] for i in range(3))
    tail_ref, weights_ref, out_ref = refs[6:]
    lower = lower_mask()
    reachable = jnp.logical_or(lower, lax.axis_index("ctx") > 0)
    top = slice(0, WINDOW)
    width = q_refs[0].shape[1]
    for part in range(2):
        begin = first_head(part, 2 * width // HD)
        scores = []
        for head in range(width // HD):
            columns = slice(head * HD, (head + 1) * HD)
            sent = (1 - part) * width + head * HD
            qq = side(*halves(q_refs[part][top, columns]))
            now = folded(dot_rows(qq, wide_keys(*halves(k_refs[part][top, columns]))))
            before = folded(dot_rows(qq, wide_keys(*halves(tail_ref[:, sent : sent + HD]))))
            scores.append(jnp.where(reachable, jnp.where(lower, now, before), -jnp.inf))
        for head in range(width // HD):
            columns = slice(head * HD, (head + 1) * HD)
            weights, total = weights_of(scores[head])
            weights = weights * (gain_ref[0, begin + head] / total)
            now_high, now_low = halves(jnp.where(lower, weights, 0.0))
            vv = side(*halves(v_refs[part][top, columns]))
            wide = dot(stack(now_high, now_low), vv)
            out_ref[:, part * width + head * HD : part * width + (head + 1) * HD] = (
                folded(wide[:WINDOW]) + wide[WINDOW:, :HD]
            )
            held = slice(2 * (part * width + head * HD), 2 * (part * width + (head + 1) * HD))
            weights_ref[:, held] = side(*halves(jnp.where(lower, 0.0, weights)))


def first_values_kernel(weights_ref, now_ref, tail_ref, _, a_ref, sums_ref):
    square = jnp.zeros((WINDOW, HD), F32)
    heads = now_ref.shape[1] // HD
    for part in range(2):
        for head in range(heads // 2):
            j = part * (heads // 2) + head
            sent = (1 - part) * (heads // 2) + head
            columns = slice(j * HD, (j + 1) * HD)
            high = weights_ref[:, 2 * j * HD : (2 * j + 1) * HD]
            low = weights_ref[:, (2 * j + 1) * HD : 2 * (j + 1) * HD]
            wide = dot(stack(high, low), side(*halves(tail_ref[:, sent * HD : (sent + 1) * HD])))
            a = now_ref[:, columns] + (folded(wide[:WINDOW]) + wide[WINDOW:, :HD])
            a_ref[:, columns] = a
            square = square + a * a
    sums_ref[...] = row_sums(square)


def inverse_norm(total):
    return 1.0 / jnp.sqrt(total / (HEADS * HD) + EPS)


def added(refs):
    total = refs[0][...]
    for ref in refs[1:]:
        total = total + ref[...]
    return total


def write(part, rows, held, out_ref, out_hbm, sem):
    width = out_ref.shape[1] // 2
    begin = first_head(part, 2 * width // HD) * HD
    there = pl.ds(pl.multiple_of(begin, HD), width)
    copy = pltpu.make_async_copy(
        out_ref.at[held, pl.ds(part * width, width)], out_hbm.at[rows, there], sem
    )
    copy.start()
    return copy


def scale_kernel(parts, _, *refs):
    sums, refs = refs[:parts], refs[parts:]
    a_refs, b_refs, (out_hbm, out_ref, sems) = refs[:2], refs[2:4], refs[4:]
    inverse = inverse_norm(added(sums)).T
    width = a_refs[0].shape[1]
    copies = []
    for n in range(out_ref.shape[0] // WINDOW):
        held = slice(n * WINDOW, (n + 1) * WINDOW)
        rows = slice((n + 1) * WINDOW, (n + 2) * WINDOW)
        inverse_a, inverse_b = inverse[rows, 0:1], inverse[rows, 1:2]
        for part in range(2):
            columns = slice(part * width, (part + 1) * width)
            out_ref[held, columns] = a_refs[part][rows, :] * inverse_a + b_refs[part][rows, :] * inverse_b
            copies.append(write(part, rows, held, out_ref, out_hbm, sems.at[n, part]))
    for copy in copies:
        copy.wait()


def first_scale_kernel(parts, a_ref, _, *refs):
    b_refs, refs = refs[:2], refs[2:]
    sums, first_sums, (out_hbm, out_ref, sems) = refs[:parts], refs[parts : 2 * parts], refs[2 * parts :]
    inverse_a = inverse_norm(added(first_sums)).T[:, 0:1]
    inverse_b = inverse_norm(added(sums)[:, :WINDOW]).T[:, 1:2]
    width = b_refs[0].shape[1]
    copies = []
    pieces = sems.shape[0]
    for n in range(pieces):
        rows = slice(n * WINDOW // pieces, (n + 1) * WINDOW // pieces)
        for part in range(2):
            columns = slice(part * width, (part + 1) * width)
            out_ref[rows, columns] = (
                a_ref[rows, columns] * inverse_a[rows] + b_refs[part][rows, :] * inverse_b[rows]
            )
            copies.append(write(part, rows, rows, out_ref, out_hbm, sems.at[n, part]))
    for copy in copies:
        copy.wait()


def swap(block, axis, bit):
    return lax.ppermute(block, axis, [(i, i ^ bit) for i in range(lax.axis_size(axis))])


def everyone(block, axis):
    return [block] + [swap(block, axis, bits) for bits in range(1, lax.axis_size(axis))]


def first_phase(chip):
    return lax.ppermute(chip, "ctx", [(i, i ^ (2 if i % 2 == 0 else 4)) for i in range(8)])


def second_phase(message):
    return lax.ppermute(message, "ctx", [(i, i ^ (4 if i % 2 == 0 else 2)) for i in range(8)])


def doubled_prefix(chip):
    index = lax.axis_index("ctx")
    earlier = jnp.zeros_like(chip)
    running = chip
    bit = 2
    while bit < lax.axis_size("ctx"):
        partner = swap(running, "ctx", bit)
        earlier = earlier + jnp.where((index & bit) != 0, partner, 0.0)
        running = running + partner
        bit *= 2
    return earlier


def shards(queries, keys, values, head_gain):
    rows, width = queries.shape
    heads = head_gain.shape[1]
    queries, keys, values = (
        pltpu.with_memory_space_constraint(x, pltpu.HBM) for x in (queries, keys, values)
    )
    smem = pl.BlockSpec(memory_space=pltpu.SMEM)
    anywhere = pl.BlockSpec(memory_space=pl.ANY)
    vmem = pl.BlockSpec()

    def array(*shape, dtype=F32):
        return jax.ShapeDtypeStruct(shape, dtype)

    def call(kernel, name, **kwargs):
        return pl.pallas_call(
            kernel,
            name=name,
            compiler_params=pltpu.CompilerParams(vmem_limit_bytes=VMEM_BYTES),
            cost_estimate=pl.CostEstimate(flops=0, bytes_accessed=0, transcendentals=0),
            **kwargs,
        )

    packed = array(heads // 2, HD, HD)
    half = array(rows, width // 2)
    first_tile = array(WINDOW, width)
    dma = pltpu.SemaphoreType.DMA
    groups = heads // (2 * GROUP)

    def totals(part, after):
        return call(
            functools.partial(totals_kernel, part),
            "totals",
            in_specs=[anywhere] * 3,
            out_shape=[packed, packed, half, half],
            scratch_shapes=[dma((2, groups))],
        )(keys, values, after)

    def local(part, query_source, after):
        return call(
            functools.partial(local_kernel, part),
            "local",
            in_specs=[smem, vmem if part else anywhere, vmem, vmem, anywhere],
            out_shape=[half, half, array(8, rows)] + ([] if part else [half, half]),
            scratch_shapes=[pltpu.VMEM((rows, HD), F32)] + ([] if part else [dma((2, groups))]),
        )(head_gain, query_source, held_k[part], held_v[part], after)

    route = [(i, i + 1) for i in range(lax.axis_size("ctx") - 1)]
    send, *held_0 = totals(0, queries)
    beside = swap(send, "ctx", 1)
    keep, *held_1 = totals(1, send)
    early, held_k, held_v = zip(held_0, held_1)
    chip, tail_k = call(chip_kernel, "chip", out_shape=[packed, first_tile])(keep, beside, *held_k)
    before_k = lax.ppermute(tail_k, "ctx", route)
    *local_0, query_0, query_1 = local(0, queries, chip)
    message = local_0[2]
    if lax.axis_size("ctx") == 8:
        first = first_phase(chip)
        message = call(
            message_kernel,
            "message",
            in_specs=[vmem, vmem, anywhere],
            out_shape=packed,
        )(first, chip, message)
    held_q = query_0, query_1
    window, linear, window_sums = zip(local_0, local(1, query_1, message))
    tail_v = call(
        tail_kernel, "tail", in_specs=[vmem, vmem, anywhere], out_shape=first_tile
    )(*held_v, window_sums[1])
    before_v = lax.ppermute(tail_v, "ctx", route)
    first_weights, first_now = call(
        first_weights_kernel,
        "first_weights",
        in_specs=[smem] + [vmem] * 7,
        out_shape=[array(WINDOW, 2 * width, dtype=BF16), first_tile],
    )(head_gain, *held_q, *held_k, *held_v, before_k)

    if lax.axis_size("ctx") == 8:
        second = second_phase(message)
        mine, other = call(
            prefix_kernel,
            "prefix",
            in_specs=[vmem] * 4 + [anywhere],
            out_shape=[packed, packed],
        )(first, second, keep, beside, first_now)
    else:
        earlier = doubled_prefix(chip)
        core = lax.axis_index("ctx") % 2
        mine = earlier + jnp.where(core == 1, beside, 0.0)
        other = earlier + jnp.where(core == 0, keep, 0.0)
    other = swap(other, "ctx", 1)

    *linear, sums = call(
        earlier_kernel,
        "earlier",
        in_specs=[smem] + [vmem] * 10,
        out_shape=[half, half, array(8, rows)],
        scratch_shapes=[pltpu.VMEM((rows, HD), F32)],
    )(head_gain, other, mine, *early, *held_q, *linear, *window_sums)
    sums = everyone(sums, "head")
    first_a, first_sums = call(
        first_values_kernel,
        "first_values",
        in_specs=[vmem] * 3 + [anywhere],
        out_shape=[first_tile, array(8, WINDOW)],
    )(first_weights, first_now, before_v, sums[0])
    first_sums = everyone(first_sums, "head")
    out = call(
        functools.partial(scale_kernel, len(sums)),
        "scale",
        in_specs=[anywhere] + [vmem] * (4 + len(sums)),
        out_specs=anywhere,
        out_shape=array(rows, width),
        scratch_shapes=[pltpu.VMEM((rows - WINDOW, width), F32), dma((rows // WINDOW - 1, 2))],
    )(first_sums[0], *sums, *window, *linear)
    return call(
        functools.partial(first_scale_kernel, len(sums)),
        "first_scale",
        in_specs=[vmem, anywhere] + [vmem] * (2 + 2 * len(sums)),
        out_specs=anywhere,
        out_shape=array(rows, width),
        scratch_shapes=[pltpu.VMEM((WINDOW, width), F32), dma((4, 2))],
        input_output_aliases={1: 0},
    )(first_a, out, *linear, *sums, *first_sums)


def solution(mesh):
    in_specs = (P("ctx", "head"), P("ctx", "head"), P("ctx", "head"), P(None, "head"))
    out_specs = P("ctx", "head")
    return jax.shard_map(shards, mesh=mesh, in_specs=in_specs, out_specs=out_specs, check_vma=False)
```

```python
import functools
import math

import jax
import jax.numpy as jnp
from jax import lax
from jax.experimental import pallas as pl
from jax.experimental.pallas import tpu as pltpu
from jax.sharding import PartitionSpec as P

HEADS = 64
HD = 128
WINDOW = 128
EPS = 1e-06
F32 = jnp.float32
BF16 = jnp.bfloat16
EXP2_SCALE = math.log2(math.e) / math.sqrt(HD)
VMEM_BYTES = 20 * 1024 * 1024
GROUP = 4


def halves(x):
    high = x.astype(BF16)
    low = (x - high.astype(F32)).astype(BF16)
    return high, low


def dot(a, b):
    return lax.dot_general(a, b, (((1,), (0,)), ((), ())), preferred_element_type=F32)


def dot_rows(a, b):
    return lax.dot_general(a, b, (((1,), (1,)), ((), ())), preferred_element_type=F32)


def dot_columns(a, b):
    return lax.dot_general(a, b, (((0,), (0,)), ((), ())), preferred_element_type=F32)


def side(a, b):
    return jnp.concatenate([a, b], axis=1)


def stack(a, b):
    return jnp.concatenate([a, b], axis=0)


def outer_state(k_high, k_low, v_high, v_low):
    grid = dot_columns(side(k_high, k_low), side(v_high, v_low))
    return grid[:HD, :HD] + (grid[:HD, HD:] + grid[HD:, :HD]) + grid[HD:, HD:]


def lower_mask():
    rows = lax.broadcasted_iota(jnp.int32, (WINDOW, WINDOW), 0)
    columns = lax.broadcasted_iota(jnp.int32, (WINDOW, WINDOW), 1)
    return rows >= columns


def row_sums(square):
    ones = jnp.ones((8, HD), BF16)
    high, low = halves(square)
    return dot_rows(ones, high) + dot_rows(ones, low)


def wide_keys(k_high, k_low):
    return stack(side(k_high, k_high), side(k_low, jnp.zeros_like(k_low)))


def wide_state(state):
    high, low = halves(state)
    return stack(side(high, low), side(high, jnp.zeros_like(high)))


def folded(wide):
    half = wide.shape[1] // 2
    return wide[:, :half] + wide[:, half:]


def head_columns(head, count=1, width=HD):
    return pl.ds(pl.multiple_of(head * width, width), count * width)


def first_head(part, heads):
    core = lax.axis_index("ctx") % 2
    return jnp.where(core == part, heads // 2, 0)


def column_copies(part, sources, targets, sems):
    begin = first_head(part, sources[0].shape[1] // HD) * HD
    width = GROUP * HD
    copies = []
    for group in range(targets[0].shape[1] // width):
        there = pl.ds(pl.multiple_of(begin + group * width, HD), width)
        here = pl.ds(group * width, width)
        copies.append(
            [
                pltpu.make_async_copy(source.at[:, there], target.at[:, here], sems.at[i, group])
                for i, (source, target) in enumerate(zip(sources, targets))
            ]
        )
    return copies


def totals_kernel(part, k_hbm, v_hbm, _, total_ref, half_ref, k_ref, v_ref, sems):
    middle = k_ref.shape[0] // 2
    copies = column_copies(part, (k_hbm, v_hbm), (k_ref, v_ref), sems)
    for group in copies:
        for copy in group:
            copy.start()
    for i, group in enumerate(copies):
        for copy in group:
            copy.wait()
        for head in range(i * GROUP, (i + 1) * GROUP):
            columns = slice(head * HD, (head + 1) * HD)
            k_high, k_low = halves(k_ref[:, columns])
            v_high, v_low = halves(v_ref[:, columns])
            first = outer_state(k_high[:middle], k_low[:middle], v_high[:middle], v_low[:middle])
            second = outer_state(k_high[middle:], k_low[middle:], v_high[middle:], v_low[middle:])
            half_ref[head] = first
            total_ref[head] = first + second


def chip_kernel(keep_ref, beside_ref, first_ref, second_ref, out_ref, tail_ref):
    out_ref[...] = keep_ref[...] + beside_ref[...]
    rows, width = first_ref.shape
    tail_ref[:, :width] = first_ref[rows - WINDOW :, :]
    tail_ref[:, width:] = second_ref[rows - WINDOW :, :]


def tail_kernel(first_ref, second_ref, _, tail_ref):
    rows, width = first_ref.shape
    tail_ref[:, :width] = first_ref[rows - WINDOW :, :]
    tail_ref[:, width:] = second_ref[rows - WINDOW :, :]


def weights_of(scores):
    biggest = jnp.max(scores, axis=1, keepdims=True)
    weights = jnp.exp2((scores - biggest) * EXP2_SCALE)
    return weights, jnp.sum(weights, axis=1, keepdims=True)


def masked_pair(weights, below, above):
    high, low = halves(weights)
    return side(high * above, high * below), side(low * above, low * below)


def local_kernel(part, gain_ref, q_in_ref, k_ref, v_ref, *refs):
    a_ref, b_ref, sum_ref = refs[1:4]
    square_ref = refs[-2]
    lower = lower_mask()
    below = jnp.where(lower, 1.0, 0.0).astype(BF16)
    above = jnp.where(lower, 0.0, 1.0).astype(BF16)
    rows, width = a_ref.shape
    tiles = rows // WINDOW
    groups = width // (GROUP * HD)
    begin = first_head(part, 2 * width // HD)
    if part == 0:
        q_refs, sems = refs[4:6], refs[-1]
        q_ref = q_refs[0]

        def load(number, group):
            there = pl.ds(pl.multiple_of((first_head(number, 2 * width // HD) + group * GROUP) * HD, HD), GROUP * HD)
            here = head_columns(group, 1, GROUP * HD)
            return pltpu.make_async_copy(
                q_in_ref.at[:, there], q_refs[number].at[:, here], sems.at[number, group]
            )

        for number in range(2):
            for group in range(groups):
                load(number, group).start()
    else:
        q_ref = q_in_ref
        square_ref = refs[-1]
    square_ref[...] = jnp.zeros_like(square_ref)

    def tile(n):
        return slice(n * WINDOW, (n + 1) * WINDOW)

    @pl.loop(0, groups)
    def _(group):
        if part == 0:
            load(0, group).wait()
        scores = []
        for j in range(GROUP):
            columns = head_columns(GROUP * group + j)
            qq = side(*halves(q_ref[:, columns]))
            k_high, k_low = halves(k_ref[:, columns])
            now, before = [], [None]
            for n in range(tiles):
                keys = wide_keys(k_high[tile(n)], k_low[tile(n)])
                found = folded(dot_rows(qq[n * WINDOW : min((n + 2) * WINDOW, rows)], keys))
                now.append(found[:WINDOW])
                before.append(found[WINDOW:])
            scores.append((now, before))
        for j in range(GROUP):
            head = GROUP * group + j
            columns = head_columns(head)
            vv = side(*halves(v_ref[:, columns]))
            now, before = scores[j]
            gain_a = gain_ref[0, begin + head]
            for n in range(tiles):
                inner_high, inner_low = halves(jnp.where(lower, now[n], 0.0))
                if n == 0:
                    wide = dot(stack(inner_high, inner_low), vv[tile(0)])
                    b_ref[tile(0), columns] = folded(wide[:WINDOW]) + wide[WINDOW:, :HD]
                    a_ref[tile(0), columns] = jnp.zeros((WINDOW, HD), F32)
                    continue
                weights, total = weights_of(jnp.where(lower, now[n], before[n]))
                pair_high, pair_low = masked_pair(weights, below, above)
                if n % 2:
                    before_high, before_low = halves(before[n])
                else:
                    before_high = before_low = jnp.zeros((WINDOW, HD), BF16)
                left = jnp.concatenate(
                    [pair_high, pair_low, side(before_high, inner_high), side(before_low, inner_low)], axis=0
                )
                wide = dot(left, vv[(n - 1) * WINDOW : (n + 1) * WINDOW])
                a = (folded(wide[tile(0)]) + wide[tile(1), :HD]) * (gain_a / total)
                a_ref[tile(n), columns] = a
                square_ref[tile(n), :] += a * a
                b_ref[tile(n), columns] = folded(wide[tile(2)]) + wide[tile(3), :HD]

    if part == 0:
        for group in range(groups):
            load(1, group).wait()
    sum_ref[...] = row_sums(square_ref[...])


def message_kernel(first_ref, chip_ref, _, out_ref):
    index = lax.axis_index("ctx")
    core, x, y = index % 2, (index >> 1) % 2, index >> 2
    first = jnp.where((core == 0) | (y == 1), first_ref[...], 0.0)
    out_ref[...] = first + jnp.where((core == 0) | (x == 0), chip_ref[...], 0.0)


def prefix_kernel(first_ref, second_ref, keep_ref, beside_ref, _, mine_ref, other_ref):
    index = lax.axis_index("ctx")
    core, x, y = index % 2, (index >> 1) % 2, index >> 2
    use_first = jnp.where(core == 0, x, y) == 1
    use_second = (core == 1) & ((x == 1) | (y == 1)) | (core == 0) & (y == 1)
    earlier = jnp.where(use_first, first_ref[...], 0.0) + jnp.where(use_second, second_ref[...], 0.0)
    mine_ref[...] = earlier + jnp.where(core == 1, beside_ref[...], 0.0)
    other_ref[...] = earlier + jnp.where(core == 0, keep_ref[...], 0.0)


def earlier_kernel(gain_ref, *refs):
    state_refs, half_refs, q_refs, b_refs, sum_refs, out_refs = (refs[2 * i : 2 * i + 2] for i in range(6))
    sums_ref, square_ref = refs[12:]
    rows, width = b_refs[0].shape
    middle = rows // 2
    square_ref[...] = jnp.zeros_like(square_ref)
    for part in range(2):
        begin = first_head(part, 2 * width // HD)
        for head in range(width // HD):
            columns = slice(head * HD, (head + 1) * HD)
            state = state_refs[part][head]
            gain_b = gain_ref[1, begin + head]
            for span, held in ((slice(0, middle), state), (slice(middle, rows), state + half_refs[part][head])):
                qq = side(*halves(q_refs[part][span, columns]))
                b = gain_b * (b_refs[part][span, columns] + folded(dot(qq, wide_state(held))))
                out_refs[part][span, columns] = b
                square_ref[span, :] += b * b
    sums = row_sums(square_ref[...])
    row = lax.broadcasted_iota(jnp.int32, sums.shape, 0)
    sums_ref[...] = jnp.where(row == 0, sum(ref[...] for ref in sum_refs), sums)


def first_weights_kernel(gain_ref, *refs):
    q_refs, k_refs, v_refs = (refs[2 * i : 2 * i + 2] for i in range(3))
    tail_ref, weights_ref, out_ref = refs[6:]
    lower = lower_mask()
    reachable = jnp.logical_or(lower, lax.axis_index("ctx") > 0)
    top = slice(0, WINDOW)
    width = q_refs[0].shape[1]
    for part in range(2):
        begin = first_head(part, 2 * width // HD)
        scores = []
        for head in range(width // HD):
            columns = slice(head * HD, (head + 1) * HD)
            sent = (1 - part) * width + head * HD
            qq = side(*halves(q_refs[part][top, columns]))
            now = folded(dot_rows(qq, wide_keys(*halves(k_refs[part][top, columns]))))
            before = folded(dot_rows(qq, wide_keys(*halves(tail_ref[:, sent : sent + HD]))))
            scores.append(jnp.where(reachable, jnp.where(lower, now, before), -jnp.inf))
        for head in range(width // HD):
            columns = slice(head * HD, (head + 1) * HD)
            weights, total = weights_of(scores[head])
            weights = weights * (gain_ref[0, begin + head] / total)
            now_high, now_low = halves(jnp.where(lower, weights, 0.0))
            vv = side(*halves(v_refs[part][top, columns]))
            wide = dot(stack(now_high, now_low), vv)
            out_ref[:, part * width + head * HD : part * width + (head + 1) * HD] = (
                folded(wide[:WINDOW]) + wide[WINDOW:, :HD]
            )
            held = slice(2 * (part * width + head * HD), 2 * (part * width + (head + 1) * HD))
            weights_ref[:, held] = side(*halves(jnp.where(lower, 0.0, weights)))


def first_values_kernel(weights_ref, now_ref, tail_ref, _, a_ref, sums_ref):
    square = jnp.zeros((WINDOW, HD), F32)
    heads = now_ref.shape[1] // HD
    for part in range(2):
        for head in range(heads // 2):
            j = part * (heads // 2) + head
            sent = (1 - part) * (heads // 2) + head
            columns = slice(j * HD, (j + 1) * HD)
            high = weights_ref[:, 2 * j * HD : (2 * j + 1) * HD]
            low = weights_ref[:, (2 * j + 1) * HD : 2 * (j + 1) * HD]
            wide = dot(stack(high, low), side(*halves(tail_ref[:, sent * HD : (sent + 1) * HD])))
            a = now_ref[:, columns] + (folded(wide[:WINDOW]) + wide[WINDOW:, :HD])
            a_ref[:, columns] = a
            square = square + a * a
    sums_ref[...] = row_sums(square)


def inverse_norm(total):
    return 1.0 / jnp.sqrt(total / (HEADS * HD) + EPS)


def added(refs):
    total = refs[0][...]
    for ref in refs[1:]:
        total = total + ref[...]
    return total


def write(part, rows, held, out_ref, out_hbm, sem):
    width = out_ref.shape[1] // 2
    begin = first_head(part, 2 * width // HD) * HD
    there = pl.ds(pl.multiple_of(begin, HD), width)
    copy = pltpu.make_async_copy(
        out_ref.at[held, pl.ds(part * width, width)], out_hbm.at[rows, there], sem
    )
    copy.start()
    return copy


def scale_kernel(parts, _, *refs):
    sums, refs = refs[:parts], refs[parts:]
    a_refs, b_refs, (out_hbm, first_ref, out_ref, sems) = refs[:2], refs[2:4], refs[4:]
    inverse = inverse_norm(added(sums)).T
    width = a_refs[0].shape[1]
    top = slice(0, WINDOW)
    copies = []
    for n in range(out_ref.shape[0] // WINDOW):
        held = slice(n * WINDOW, (n + 1) * WINDOW)
        rows = slice((n + 1) * WINDOW, (n + 2) * WINDOW)
        inverse_a, inverse_b = inverse[rows, 0:1], inverse[rows, 1:2]
        for part in range(2):
            columns = slice(part * width, (part + 1) * width)
            out_ref[held, columns] = a_refs[part][rows, :] * inverse_a + b_refs[part][rows, :] * inverse_b
            copies.append(write(part, rows, held, out_ref, out_hbm, sems.at[n, part]))
    for part in range(2):
        first_ref[:, part * width : (part + 1) * width] = b_refs[part][top, :] * inverse[top, 1:2]
    for copy in copies:
        copy.wait()


def first_scale_kernel(parts, a_ref, b_ref, _, *refs):
    sums, (out_hbm, out_ref, sems) = refs[:parts], refs[parts:]
    inverse_a = inverse_norm(added(sums)).T[:, 0:1]
    width = b_ref.shape[1] // 2
    copies = []
    pieces = sems.shape[0]
    for n in range(pieces):
        rows = slice(n * WINDOW // pieces, (n + 1) * WINDOW // pieces)
        for part in range(2):
            columns = slice(part * width, (part + 1) * width)
            out_ref[rows, columns] = a_ref[rows, columns] * inverse_a[rows] + b_ref[rows, columns]
            copies.append(write(part, rows, rows, out_ref, out_hbm, sems.at[n, part]))
    for copy in copies:
        copy.wait()


def swap(block, axis, bit):
    return lax.ppermute(block, axis, [(i, i ^ bit) for i in range(lax.axis_size(axis))])


def everyone(block, axis):
    return [block] + [swap(block, axis, bits) for bits in range(1, lax.axis_size(axis))]


def first_phase(chip):
    return lax.ppermute(chip, "ctx", [(i, i ^ (2 if i % 2 == 0 else 4)) for i in range(8)])


def second_phase(message):
    return lax.ppermute(message, "ctx", [(i, i ^ (4 if i % 2 == 0 else 2)) for i in range(8) if i != 3])


def doubled_prefix(chip):
    index = lax.axis_index("ctx")
    earlier = jnp.zeros_like(chip)
    running = chip
    bit = 2
    while bit < lax.axis_size("ctx"):
        partner = swap(running, "ctx", bit)
        earlier = earlier + jnp.where((index & bit) != 0, partner, 0.0)
        running = running + partner
        bit *= 2
    return earlier


def shards(queries, keys, values, head_gain):
    rows, width = queries.shape
    heads = head_gain.shape[1]
    queries, keys, values = (
        pltpu.with_memory_space_constraint(x, pltpu.HBM) for x in (queries, keys, values)
    )
    smem = pl.BlockSpec(memory_space=pltpu.SMEM)
    anywhere = pl.BlockSpec(memory_space=pl.ANY)
    vmem = pl.BlockSpec()

    def array(*shape, dtype=F32):
        return jax.ShapeDtypeStruct(shape, dtype)

    def call(kernel, name, **kwargs):
        return pl.pallas_call(
            kernel,
            name=name,
            compiler_params=pltpu.CompilerParams(vmem_limit_bytes=VMEM_BYTES),
            cost_estimate=pl.CostEstimate(flops=0, bytes_accessed=0, transcendentals=0),
            **kwargs,
        )

    packed = array(heads // 2, HD, HD)
    half = array(rows, width // 2)
    first_tile = array(WINDOW, width)
    dma = pltpu.SemaphoreType.DMA
    groups = heads // (2 * GROUP)

    def totals(part, after):
        return call(
            functools.partial(totals_kernel, part),
            "totals",
            in_specs=[anywhere] * 3,
            out_shape=[packed, packed, half, half],
            scratch_shapes=[dma((2, groups))],
        )(keys, values, after)

    def local(part, query_source, after):
        return call(
            functools.partial(local_kernel, part),
            "local",
            in_specs=[smem, vmem if part else anywhere, vmem, vmem, anywhere],
            out_shape=[half, half, array(8, rows)] + ([] if part else [half, half]),
            scratch_shapes=[pltpu.VMEM((rows, HD), F32)] + ([] if part else [dma((2, groups))]),
        )(head_gain, query_source, held_k[part], held_v[part], after)

    route = [(i, i + 1) for i in range(lax.axis_size("ctx") - 1)]
    send, *held_0 = totals(0, queries)
    beside = swap(send, "ctx", 1)
    keep, *held_1 = totals(1, send)
    early, held_k, held_v = zip(held_0, held_1)
    chip, tail_k = call(chip_kernel, "chip", out_shape=[packed, first_tile])(keep, beside, *held_k)
    before_k = lax.ppermute(tail_k, "ctx", route)
    *local_0, query_0, query_1 = local(0, queries, chip)
    message = local_0[2]
    if lax.axis_size("ctx") == 8:
        first = first_phase(chip)
        message = call(
            message_kernel,
            "message",
            in_specs=[vmem, vmem, anywhere],
            out_shape=packed,
        )(first, chip, message)
    held_q = query_0, query_1
    window, linear, window_sums = zip(local_0, local(1, query_1, message))
    tail_v = call(
        tail_kernel, "tail", in_specs=[vmem, vmem, anywhere], out_shape=first_tile
    )(*held_v, window_sums[1])
    before_v = lax.ppermute(tail_v, "ctx", route)
    first_weights, first_now = call(
        first_weights_kernel,
        "first_weights",
        in_specs=[smem] + [vmem] * 7,
        out_shape=[array(WINDOW, 2 * width, dtype=BF16), first_tile],
    )(head_gain, *held_q, *held_k, *held_v, before_k)

    if lax.axis_size("ctx") == 8:
        second = second_phase(message)
        mine, other = call(
            prefix_kernel,
            "prefix",
            in_specs=[vmem] * 4 + [anywhere],
            out_shape=[packed, packed],
        )(first, second, keep, beside, first_now)
    else:
        earlier = doubled_prefix(chip)
        core = lax.axis_index("ctx") % 2
        mine = earlier + jnp.where(core == 1, beside, 0.0)
        other = earlier + jnp.where(core == 0, keep, 0.0)
    other = swap(other, "ctx", 1)

    *linear, sums = call(
        earlier_kernel,
        "earlier",
        in_specs=[smem] + [vmem] * 10,
        out_shape=[half, half, array(8, rows)],
        scratch_shapes=[pltpu.VMEM((rows, HD), F32)],
    )(head_gain, other, mine, *early, *held_q, *linear, *window_sums)
    sums = everyone(sums, "head")
    first_a, first_sums = call(
        first_values_kernel,
        "first_values",
        in_specs=[vmem] * 3 + [anywhere],
        out_shape=[first_tile, array(8, WINDOW)],
    )(first_weights, first_now, before_v, sums[0])
    first_sums = everyone(first_sums, "head")
    out, first_b = call(
        functools.partial(scale_kernel, len(sums)),
        "scale",
        in_specs=[anywhere] + [vmem] * (4 + len(sums)),
        out_specs=[anywhere, vmem],
        out_shape=[array(rows, width), first_tile],
        scratch_shapes=[pltpu.VMEM((rows - WINDOW, width), F32), dma((rows // WINDOW - 1, 2))],
    )(first_sums[0], *sums, *window, *linear)
    return call(
        functools.partial(first_scale_kernel, len(sums)),
        "first_scale",
        in_specs=[vmem, vmem, anywhere] + [vmem] * len(sums),
        out_specs=anywhere,
        out_shape=array(rows, width),
        scratch_shapes=[pltpu.VMEM((WINDOW, width), F32), dma((4, 2))],
        input_output_aliases={2: 0},
    )(first_a, first_b, out, *first_sums)


def solution(mesh):
    in_specs = (P("ctx", "head"), P("ctx", "head"), P("ctx", "head"), P(None, "head"))
    out_specs = P("ctx", "head")
    return jax.shard_map(shards, mesh=mesh, in_specs=in_specs, out_specs=out_specs, check_vma=False)
```

```python
import functools
import math

import jax
import jax.numpy as jnp
from jax import lax
from jax.experimental import pallas as pl
from jax.experimental.pallas import tpu as pltpu
from jax.sharding import PartitionSpec as P

HEADS = 64
HD = 128
WINDOW = 128
EPS = 1e-06
F32 = jnp.float32
BF16 = jnp.bfloat16
EXP2_SCALE = math.log2(math.e) / math.sqrt(HD)
VMEM_BYTES = 20 * 1024 * 1024
GROUP = 4


def halves(x):
    high = x.astype(BF16)
    low = (x - high.astype(F32)).astype(BF16)
    return high, low


def dot(a, b):
    return lax.dot_general(a, b, (((1,), (0,)), ((), ())), preferred_element_type=F32)


def dot_rows(a, b):
    return lax.dot_general(a, b, (((1,), (1,)), ((), ())), preferred_element_type=F32)


def dot_columns(a, b):
    return lax.dot_general(a, b, (((0,), (0,)), ((), ())), preferred_element_type=F32)


def side(a, b):
    return jnp.concatenate([a, b], axis=1)


def stack(a, b):
    return jnp.concatenate([a, b], axis=0)


def outer_state(k_high, k_low, v_high, v_low):
    grid = dot_columns(side(k_high, k_low), side(v_high, v_low))
    return grid[:HD, :HD] + (grid[:HD, HD:] + grid[HD:, :HD]) + grid[HD:, HD:]


def lower_mask():
    rows = lax.broadcasted_iota(jnp.int32, (WINDOW, WINDOW), 0)
    columns = lax.broadcasted_iota(jnp.int32, (WINDOW, WINDOW), 1)
    return rows >= columns


def row_sums(square):
    ones = jnp.ones((8, HD), BF16)
    high, low = halves(square)
    return dot_rows(ones, high) + dot_rows(ones, low)


def wide_keys(k_high, k_low):
    return stack(side(k_high, k_high), side(k_low, k_low))


def wide_state(state):
    high, low = halves(state)
    return stack(side(high, low), side(high, low))


def folded(wide):
    half = wide.shape[1] // 2
    return wide[:, :half] + wide[:, half:]


def head_columns(head, count=1, width=HD):
    return pl.ds(pl.multiple_of(head * width, width), count * width)


def first_head(part, heads):
    core = lax.axis_index("ctx") % 2
    return jnp.where(core == part, heads // 2, 0)


def column_copies(part, sources, targets, sems):
    begin = first_head(part, sources[0].shape[1] // HD) * HD
    width = GROUP * HD
    copies = []
    for group in range(targets[0].shape[1] // width):
        there = pl.ds(pl.multiple_of(begin + group * width, HD), width)
        here = pl.ds(group * width, width)
        copies.append(
            [
                pltpu.make_async_copy(source.at[:, there], target.at[:, here], sems.at[i, group])
                for i, (source, target) in enumerate(zip(sources, targets))
            ]
        )
    return copies


def totals_kernel(part, k_hbm, v_hbm, _, total_ref, half_ref, k_ref, v_ref, sems):
    middle = k_ref.shape[0] // 2
    copies = column_copies(part, (k_hbm, v_hbm), (k_ref, v_ref), sems)
    for group in copies:
        for copy in group:
            copy.start()
    for i, group in enumerate(copies):
        for copy in group:
            copy.wait()
        for head in range(i * GROUP, (i + 1) * GROUP):
            columns = slice(head * HD, (head + 1) * HD)
            k_high, k_low = halves(k_ref[:, columns])
            v_high, v_low = halves(v_ref[:, columns])
            first = outer_state(k_high[:middle], k_low[:middle], v_high[:middle], v_low[:middle])
            second = outer_state(k_high[middle:], k_low[middle:], v_high[middle:], v_low[middle:])
            half_ref[head] = first
            total_ref[head] = first + second


def chip_kernel(keep_ref, beside_ref, first_ref, second_ref, out_ref, tail_ref):
    out_ref[...] = keep_ref[...] + beside_ref[...]
    rows, width = first_ref.shape
    tail_ref[:, :width] = first_ref[rows - WINDOW :, :]
    tail_ref[:, width:] = second_ref[rows - WINDOW :, :]


def tail_kernel(first_ref, second_ref, _, tail_ref):
    rows, width = first_ref.shape
    tail_ref[:, :width] = first_ref[rows - WINDOW :, :]
    tail_ref[:, width:] = second_ref[rows - WINDOW :, :]


def weights_of(scores):
    biggest = jnp.max(scores, axis=1, keepdims=True)
    weights = jnp.exp2((scores - biggest) * EXP2_SCALE)
    return weights, jnp.sum(weights, axis=1, keepdims=True)


def masked_pair(weights, below, above):
    high, low = halves(weights)
    return side(high * above, high * below), side(low * above, low * below)


def local_kernel(part, gain_ref, q_in_ref, k_ref, v_ref, *refs):
    a_ref, b_ref, sum_ref = refs[1:4]
    square_ref = refs[-2]
    lower = lower_mask()
    below = jnp.where(lower, 1.0, 0.0).astype(BF16)
    above = jnp.where(lower, 0.0, 1.0).astype(BF16)
    rows, width = a_ref.shape
    tiles = rows // WINDOW
    groups = width // (GROUP * HD)
    begin = first_head(part, 2 * width // HD)
    if part == 0:
        q_refs, sems = refs[4:6], refs[-1]
        q_ref = q_refs[0]

        def load(number, group):
            there = pl.ds(pl.multiple_of((first_head(number, 2 * width // HD) + group * GROUP) * HD, HD), GROUP * HD)
            here = head_columns(group, 1, GROUP * HD)
            return pltpu.make_async_copy(
                q_in_ref.at[:, there], q_refs[number].at[:, here], sems.at[number, group]
            )

        for number in range(2):
            for group in range(groups):
                load(number, group).start()
    else:
        q_ref = q_in_ref
        square_ref = refs[-1]
    square_ref[...] = jnp.zeros_like(square_ref)

    def tile(n):
        return slice(n * WINDOW, (n + 1) * WINDOW)

    @pl.loop(0, groups)
    def _(group):
        if part == 0:
            load(0, group).wait()
        scores = []
        for j in range(GROUP):
            columns = head_columns(GROUP * group + j)
            qq = side(*halves(q_ref[:, columns]))
            k_high, k_low = halves(k_ref[:, columns])
            now, before = [], [None]
            for n in range(tiles):
                keys = wide_keys(k_high[tile(n)], k_low[tile(n)])
                found = folded(dot_rows(qq[n * WINDOW : min((n + 2) * WINDOW, rows)], keys))
                now.append(found[:WINDOW])
                before.append(found[WINDOW:])
            scores.append((now, before))
        for j in range(GROUP):
            head = GROUP * group + j
            columns = head_columns(head)
            vv = side(*halves(v_ref[:, columns]))
            now, before = scores[j]
            gain_a = gain_ref[0, begin + head]
            for n in range(tiles):
                inner_high, inner_low = halves(jnp.where(lower, now[n], 0.0))
                if n == 0:
                    wide = dot(stack(inner_high, inner_low), vv[tile(0)])
                    b_ref[tile(0), columns] = folded(wide[:WINDOW]) + wide[WINDOW:, :HD]
                    a_ref[tile(0), columns] = jnp.zeros((WINDOW, HD), F32)
                    continue
                weights, total = weights_of(jnp.where(lower, now[n], before[n]))
                pair_high, pair_low = masked_pair(weights, below, above)
                if n % 2:
                    before_high, before_low = halves(before[n])
                else:
                    before_high = before_low = jnp.zeros((WINDOW, HD), BF16)
                left = jnp.concatenate(
                    [pair_high, pair_low, side(before_high, inner_high), side(before_low, inner_low)], axis=0
                )
                wide = dot(left, vv[(n - 1) * WINDOW : (n + 1) * WINDOW])
                a = (folded(wide[tile(0)]) + wide[tile(1), :HD]) * (gain_a / total)
                a_ref[tile(n), columns] = a
                square_ref[tile(n), :] += a * a
                b_ref[tile(n), columns] = folded(wide[tile(2)]) + wide[tile(3), :HD]

    if part == 0:
        for group in range(groups):
            load(1, group).wait()
    sum_ref[...] = row_sums(square_ref[...])


def message_kernel(first_ref, chip_ref, _, out_ref):
    index = lax.axis_index("ctx")
    core, x, y = index % 2, (index >> 1) % 2, index >> 2
    first = jnp.where((core == 0) | (y == 1), first_ref[...], 0.0)
    out_ref[...] = first + jnp.where((core == 0) | (x == 0), chip_ref[...], 0.0)


def prefix_kernel(first_ref, second_ref, keep_ref, beside_ref, _, mine_ref, other_ref):
    index = lax.axis_index("ctx")
    core, x, y = index % 2, (index >> 1) % 2, index >> 2
    use_first = jnp.where(core == 0, x, y) == 1
    use_second = (core == 1) & ((x == 1) | (y == 1)) | (core == 0) & (y == 1)
    earlier = jnp.where(use_first, first_ref[...], 0.0) + jnp.where(use_second, second_ref[...], 0.0)
    mine_ref[...] = earlier + jnp.where(core == 1, beside_ref[...], 0.0)
    other_ref[...] = earlier + jnp.where(core == 0, keep_ref[...], 0.0)


def earlier_kernel(gain_ref, *refs):
    state_refs, half_refs, q_refs, b_refs, sum_refs, out_refs = (refs[2 * i : 2 * i + 2] for i in range(6))
    sums_ref, square_ref = refs[12:]
    rows, width = b_refs[0].shape
    middle = rows // 2
    square_ref[...] = jnp.zeros_like(square_ref)
    for part in range(2):
        begin = first_head(part, 2 * width // HD)
        for head in range(width // HD):
            columns = slice(head * HD, (head + 1) * HD)
            state = state_refs[part][head]
            gain_b = gain_ref[1, begin + head]
            for span, held in ((slice(0, middle), state), (slice(middle, rows), state + half_refs[part][head])):
                qq = side(*halves(q_refs[part][span, columns]))
                b = gain_b * (b_refs[part][span, columns] + folded(dot(qq, wide_state(held))))
                out_refs[part][span, columns] = b
                square_ref[span, :] += b * b
    sums = row_sums(square_ref[...])
    row = lax.broadcasted_iota(jnp.int32, sums.shape, 0)
    sums_ref[...] = jnp.where(row == 0, sum(ref[...] for ref in sum_refs), sums)


def first_weights_kernel(gain_ref, *refs):
    q_refs, k_refs, v_refs = (refs[2 * i : 2 * i + 2] for i in range(3))
    tail_ref, weights_ref, out_ref = refs[6:]
    lower = lower_mask()
    reachable = jnp.logical_or(lower, lax.axis_index("ctx") > 0)
    top = slice(0, WINDOW)
    width = q_refs[0].shape[1]
    for part in range(2):
        begin = first_head(part, 2 * width // HD)
        scores = []
        for head in range(width // HD):
            columns = slice(head * HD, (head + 1) * HD)
            sent = (1 - part) * width + head * HD
            qq = side(*halves(q_refs[part][top, columns]))
            now = folded(dot_rows(qq, wide_keys(*halves(k_refs[part][top, columns]))))
            before = folded(dot_rows(qq, wide_keys(*halves(tail_ref[:, sent : sent + HD]))))
            scores.append(jnp.where(reachable, jnp.where(lower, now, before), -jnp.inf))
        for head in range(width // HD):
            columns = slice(head * HD, (head + 1) * HD)
            weights, total = weights_of(scores[head])
            weights = weights * (gain_ref[0, begin + head] / total)
            now_high, now_low = halves(jnp.where(lower, weights, 0.0))
            vv = side(*halves(v_refs[part][top, columns]))
            wide = dot(stack(now_high, now_low), vv)
            out_ref[:, part * width + head * HD : part * width + (head + 1) * HD] = (
                folded(wide[:WINDOW]) + wide[WINDOW:, :HD]
            )
            held = slice(2 * (part * width + head * HD), 2 * (part * width + (head + 1) * HD))
            weights_ref[:, held] = side(*halves(jnp.where(lower, 0.0, weights)))


def first_values_kernel(weights_ref, now_ref, tail_ref, _, a_ref, sums_ref):
    square = jnp.zeros((WINDOW, HD), F32)
    heads = now_ref.shape[1] // HD
    for part in range(2):
        for head in range(heads // 2):
            j = part * (heads // 2) + head
            sent = (1 - part) * (heads // 2) + head
            columns = slice(j * HD, (j + 1) * HD)
            high = weights_ref[:, 2 * j * HD : (2 * j + 1) * HD]
            low = weights_ref[:, (2 * j + 1) * HD : 2 * (j + 1) * HD]
            wide = dot(stack(high, low), side(*halves(tail_ref[:, sent * HD : (sent + 1) * HD])))
            a = now_ref[:, columns] + (folded(wide[:WINDOW]) + wide[WINDOW:, :HD])
            a_ref[:, columns] = a
            square = square + a * a
    sums_ref[...] = row_sums(square)


def inverse_norm(total):
    return 1.0 / jnp.sqrt(total / (HEADS * HD) + EPS)


def added(refs):
    total = refs[0][...]
    for ref in refs[1:]:
        total = total + ref[...]
    return total


def write(part, rows, held, out_ref, out_hbm, sem):
    width = out_ref.shape[1] // 2
    begin = first_head(part, 2 * width // HD) * HD
    there = pl.ds(pl.multiple_of(begin, HD), width)
    copy = pltpu.make_async_copy(
        out_ref.at[held, pl.ds(part * width, width)], out_hbm.at[rows, there], sem
    )
    copy.start()
    return copy


def scale_kernel(parts, _, *refs):
    sums, refs = refs[:parts], refs[parts:]
    a_refs, b_refs, (out_hbm, first_ref, out_ref, sems) = refs[:2], refs[2:4], refs[4:]
    inverse = inverse_norm(added(sums)).T
    width = a_refs[0].shape[1]
    top = slice(0, WINDOW)
    copies = []
    for n in range(out_ref.shape[0] // WINDOW):
        held = slice(n * WINDOW, (n + 1) * WINDOW)
        rows = slice((n + 1) * WINDOW, (n + 2) * WINDOW)
        inverse_a, inverse_b = inverse[rows, 0:1], inverse[rows, 1:2]
        for part in range(2):
            columns = slice(part * width, (part + 1) * width)
            out_ref[held, columns] = a_refs[part][rows, :] * inverse_a + b_refs[part][rows, :] * inverse_b
            copies.append(write(part, rows, held, out_ref, out_hbm, sems.at[n, part]))
    for part in range(2):
        first_ref[:, part * width : (part + 1) * width] = b_refs[part][top, :] * inverse[top, 1:2]
    for copy in copies:
        copy.wait()


def first_scale_kernel(parts, a_ref, b_ref, _, *refs):
    sums, (out_hbm, out_ref, sems) = refs[:parts], refs[parts:]
    inverse_a = inverse_norm(added(sums)).T[:, 0:1]
    width = b_ref.shape[1] // 2
    copies = []
    pieces = sems.shape[0]
    for n in range(pieces):
        rows = slice(n * WINDOW // pieces, (n + 1) * WINDOW // pieces)
        for part in range(2):
            columns = slice(part * width, (part + 1) * width)
            out_ref[rows, columns] = a_ref[rows, columns] * inverse_a[rows] + b_ref[rows, columns]
            copies.append(write(part, rows, rows, out_ref, out_hbm, sems.at[n, part]))
    for copy in copies:
        copy.wait()


def swap(block, axis, bit):
    return lax.ppermute(block, axis, [(i, i ^ bit) for i in range(lax.axis_size(axis))])


def everyone(block, axis):
    return [block] + [swap(block, axis, bits) for bits in range(1, lax.axis_size(axis))]


def first_phase(chip):
    return lax.ppermute(chip, "ctx", [(i, i ^ (2 if i % 2 == 0 else 4)) for i in range(8)])


def second_phase(message):
    return lax.ppermute(message, "ctx", [(i, i ^ (4 if i % 2 == 0 else 2)) for i in range(8)])


def doubled_prefix(chip):
    index = lax.axis_index("ctx")
    earlier = jnp.zeros_like(chip)
    running = chip
    bit = 2
    while bit < lax.axis_size("ctx"):
        partner = swap(running, "ctx", bit)
        earlier = earlier + jnp.where((index & bit) != 0, partner, 0.0)
        running = running + partner
        bit *= 2
    return earlier


def shards(queries, keys, values, head_gain):
    rows, width = queries.shape
    heads = head_gain.shape[1]
    queries, keys, values = (
        pltpu.with_memory_space_constraint(x, pltpu.HBM) for x in (queries, keys, values)
    )
    smem = pl.BlockSpec(memory_space=pltpu.SMEM)
    anywhere = pl.BlockSpec(memory_space=pl.ANY)
    vmem = pl.BlockSpec()

    def array(*shape, dtype=F32):
        return jax.ShapeDtypeStruct(shape, dtype)

    def call(kernel, name, **kwargs):
        return pl.pallas_call(
            kernel,
            name=name,
            compiler_params=pltpu.CompilerParams(vmem_limit_bytes=VMEM_BYTES),
            cost_estimate=pl.CostEstimate(flops=0, bytes_accessed=0, transcendentals=0),
            **kwargs,
        )

    packed = array(heads // 2, HD, HD)
    half = array(rows, width // 2)
    first_tile = array(WINDOW, width)
    dma = pltpu.SemaphoreType.DMA
    groups = heads // (2 * GROUP)

    def totals(part, after):
        return call(
            functools.partial(totals_kernel, part),
            "totals",
            in_specs=[anywhere] * 3,
            out_shape=[packed, packed, half, half],
            scratch_shapes=[dma((2, groups))],
        )(keys, values, after)

    def local(part, query_source, after):
        return call(
            functools.partial(local_kernel, part),
            "local",
            in_specs=[smem, vmem if part else anywhere, vmem, vmem, anywhere],
            out_shape=[half, half, array(8, rows)] + ([] if part else [half, half]),
            scratch_shapes=[pltpu.VMEM((rows, HD), F32)] + ([] if part else [dma((2, groups))]),
        )(head_gain, query_source, held_k[part], held_v[part], after)

    route = [(i, i + 1) for i in range(lax.axis_size("ctx") - 1)]
    send, *held_0 = totals(0, queries)
    beside = swap(send, "ctx", 1)
    keep, *held_1 = totals(1, send)
    early, held_k, held_v = zip(held_0, held_1)
    chip, tail_k = call(chip_kernel, "chip", out_shape=[packed, first_tile])(keep, beside, *held_k)
    before_k = lax.ppermute(tail_k, "ctx", route)
    *local_0, query_0, query_1 = local(0, queries, chip)
    message = local_0[2]
    if lax.axis_size("ctx") == 8:
        first = first_phase(chip)
        message = call(
            message_kernel,
            "message",
            in_specs=[vmem, vmem, anywhere],
            out_shape=packed,
        )(first, chip, message)
    held_q = query_0, query_1
    window, linear, window_sums = zip(local_0, local(1, query_1, message))
    tail_v = call(
        tail_kernel, "tail", in_specs=[vmem, vmem, anywhere], out_shape=first_tile
    )(*held_v, window_sums[1])
    before_v = lax.ppermute(tail_v, "ctx", route)
    first_weights, first_now = call(
        first_weights_kernel,
        "first_weights",
        in_specs=[smem] + [vmem] * 7,
        out_shape=[array(WINDOW, 2 * width, dtype=BF16), first_tile],
    )(head_gain, *held_q, *held_k, *held_v, before_k)

    if lax.axis_size("ctx") == 8:
        second = second_phase(message)
        mine, other = call(
            prefix_kernel,
            "prefix",
            in_specs=[vmem] * 4 + [anywhere],
            out_shape=[packed, packed],
        )(first, second, keep, beside, first_now)
    else:
        earlier = doubled_prefix(chip)
        core = lax.axis_index("ctx") % 2
        mine = earlier + jnp.where(core == 1, beside, 0.0)
        other = earlier + jnp.where(core == 0, keep, 0.0)
    other = swap(other, "ctx", 1)

    *linear, sums = call(
        earlier_kernel,
        "earlier",
        in_specs=[smem] + [vmem] * 10,
        out_shape=[half, half, array(8, rows)],
        scratch_shapes=[pltpu.VMEM((rows, HD), F32)],
    )(head_gain, other, mine, *early, *held_q, *linear, *window_sums)
    sums = everyone(sums, "head")
    first_a, first_sums = call(
        first_values_kernel,
        "first_values",
        in_specs=[vmem] * 3 + [anywhere],
        out_shape=[first_tile, array(8, WINDOW)],
    )(first_weights, first_now, before_v, sums[0])
    first_sums = everyone(first_sums, "head")
    out, first_b = call(
        functools.partial(scale_kernel, len(sums)),
        "scale",
        in_specs=[anywhere] + [vmem] * (4 + len(sums)),
        out_specs=[anywhere, vmem],
        out_shape=[array(rows, width), first_tile],
        scratch_shapes=[pltpu.VMEM((rows - WINDOW, width), F32), dma((rows // WINDOW - 1, 2))],
    )(first_sums[0], *sums, *window, *linear)
    return call(
        functools.partial(first_scale_kernel, len(sums)),
        "first_scale",
        in_specs=[vmem, vmem, anywhere] + [vmem] * len(sums),
        out_specs=anywhere,
        out_shape=array(rows, width),
        scratch_shapes=[pltpu.VMEM((WINDOW, width), F32), dma((4, 2))],
        input_output_aliases={2: 0},
    )(first_a, first_b, out, *first_sums)


def solution(mesh):
    in_specs = (P("ctx", "head"), P("ctx", "head"), P("ctx", "head"), P(None, "head"))
    out_specs = P("ctx", "head")
    return jax.shard_map(shards, mesh=mesh, in_specs=in_specs, out_specs=out_specs, check_vma=False)
```

```python
import functools
import math

import jax
import jax.numpy as jnp
from jax import lax
from jax.experimental import pallas as pl
from jax.experimental.pallas import tpu as pltpu
from jax.sharding import PartitionSpec as P

HEADS = 64
HD = 128
WINDOW = 128
EPS = 1e-06
F32 = jnp.float32
BF16 = jnp.bfloat16
EXP2_SCALE = math.log2(math.e) / math.sqrt(HD)
VMEM_BYTES = 20 * 1024 * 1024
GROUP = 4


def halves(x):
    high = x.astype(BF16)
    low = (x - high.astype(F32)).astype(BF16)
    return high, low


def dot(a, b):
    return lax.dot_general(a, b, (((1,), (0,)), ((), ())), preferred_element_type=F32)


def dot_rows(a, b):
    return lax.dot_general(a, b, (((1,), (1,)), ((), ())), preferred_element_type=F32)


def dot_columns(a, b):
    return lax.dot_general(a, b, (((0,), (0,)), ((), ())), preferred_element_type=F32)


def side(a, b):
    return jnp.concatenate([a, b], axis=1)


def stack(a, b):
    return jnp.concatenate([a, b], axis=0)


def outer_state(k_high, k_low, v_high, v_low):
    grid = dot_columns(side(k_high, k_low), side(v_high, v_low))
    return grid[:HD, :HD] + (grid[:HD, HD:] + grid[HD:, :HD]) + grid[HD:, HD:]


def lower_mask():
    rows = lax.broadcasted_iota(jnp.int32, (WINDOW, WINDOW), 0)
    columns = lax.broadcasted_iota(jnp.int32, (WINDOW, WINDOW), 1)
    return rows >= columns


def row_sums(square):
    ones = jnp.ones((8, HD), BF16)
    high, low = halves(square)
    return dot_rows(ones, high) + dot_rows(ones, low)


def wide_keys(k_high, k_low):
    return stack(side(k_high, k_high), side(k_low, k_low))


def wide_state(state):
    high, low = halves(state)
    return stack(side(high, low), side(high, low))


def folded(wide):
    half = wide.shape[1] // 2
    return wide[:, :half] + wide[:, half:]


def head_columns(head, count=1, width=HD):
    return pl.ds(pl.multiple_of(head * width, width), count * width)


def first_head(part, heads):
    core = lax.axis_index("ctx") % 2
    return jnp.where(core == part, heads // 2, 0)


def column_copies(part, sources, targets, sems):
    begin = first_head(part, sources[0].shape[1] // HD) * HD
    width = GROUP * HD
    copies = []
    for group in range(targets[0].shape[1] // width):
        there = pl.ds(pl.multiple_of(begin + group * width, HD), width)
        here = pl.ds(group * width, width)
        copies.append(
            [
                pltpu.make_async_copy(source.at[:, there], target.at[:, here], sems.at[i, group])
                for i, (source, target) in enumerate(zip(sources, targets))
            ]
        )
    return copies


def totals_kernel(part, k_hbm, v_hbm, _, total_ref, half_ref, k_ref, v_ref, sems):
    middle = k_ref.shape[0] // 2
    copies = column_copies(part, (k_hbm, v_hbm), (k_ref, v_ref), sems)
    for group in copies:
        for copy in group:
            copy.start()
    for i, group in enumerate(copies):
        for copy in group:
            copy.wait()
        for head in range(i * GROUP, (i + 1) * GROUP):
            columns = slice(head * HD, (head + 1) * HD)
            k_high, k_low = halves(k_ref[:, columns])
            v_high, v_low = halves(v_ref[:, columns])
            first = outer_state(k_high[:middle], k_low[:middle], v_high[:middle], v_low[:middle])
            second = outer_state(k_high[middle:], k_low[middle:], v_high[middle:], v_low[middle:])
            half_ref[head] = first
            total_ref[head] = first + second


def chip_kernel(keep_ref, beside_ref, out_ref):
    out_ref[...] = keep_ref[...] + beside_ref[...]


def key_tail_kernel(k_hbm, tail_ref, sems):
    rows, width = k_hbm.shape
    copies = []
    for part in range(2):
        there = pl.ds(pl.multiple_of(first_head(part, width // HD) * HD, HD), width // 2)
        here = pl.ds(part * (width // 2), width // 2)
        copies.append(
            pltpu.make_async_copy(
                k_hbm.at[pl.ds(rows - WINDOW, WINDOW), there], tail_ref.at[:, here], sems.at[part]
            )
        )
    for copy in copies:
        copy.start()
    for copy in copies:
        copy.wait()


def relay_kernel(tail_ref, relayed_ref, _, out_ref):
    out_ref[...] = jnp.where(lax.axis_index("ctx") == 7, relayed_ref[...], tail_ref[...])


def tail_kernel(first_ref, second_ref, _, tail_ref):
    rows, width = first_ref.shape
    tail_ref[:, :width] = first_ref[rows - WINDOW :, :]
    tail_ref[:, width:] = second_ref[rows - WINDOW :, :]


def weights_of(scores):
    biggest = jnp.max(scores, axis=1, keepdims=True)
    weights = jnp.exp2((scores - biggest) * EXP2_SCALE)
    return weights, jnp.sum(weights, axis=1, keepdims=True)


def masked_pair(weights, below, above):
    high, low = halves(weights)
    return side(high * above, high * below), side(low * above, low * below)


def local_kernel(part, gain_ref, q_in_ref, k_ref, v_ref, *refs):
    a_ref, b_ref, sum_ref = refs[1:4]
    square_ref = refs[-2]
    lower = lower_mask()
    below = jnp.where(lower, 1.0, 0.0).astype(BF16)
    above = jnp.where(lower, 0.0, 1.0).astype(BF16)
    rows, width = a_ref.shape
    tiles = rows // WINDOW
    groups = width // (GROUP * HD)
    begin = first_head(part, 2 * width // HD)
    if part == 0:
        q_refs, sems = refs[4:6], refs[-1]
        q_ref = q_refs[0]

        def load(number, group):
            there = pl.ds(pl.multiple_of((first_head(number, 2 * width // HD) + group * GROUP) * HD, HD), GROUP * HD)
            here = head_columns(group, 1, GROUP * HD)
            return pltpu.make_async_copy(
                q_in_ref.at[:, there], q_refs[number].at[:, here], sems.at[number, group]
            )

        for number in range(2):
            for group in range(groups):
                load(number, group).start()
    else:
        q_ref = q_in_ref
        square_ref = refs[-1]
    square_ref[...] = jnp.zeros_like(square_ref)

    def tile(n):
        return slice(n * WINDOW, (n + 1) * WINDOW)

    @pl.loop(0, groups)
    def _(group):
        if part == 0:
            load(0, group).wait()
        scores = []
        for j in range(GROUP):
            columns = head_columns(GROUP * group + j)
            qq = side(*halves(q_ref[:, columns]))
            k_high, k_low = halves(k_ref[:, columns])
            now, before = [], [None]
            for n in range(tiles):
                keys = wide_keys(k_high[tile(n)], k_low[tile(n)])
                found = folded(dot_rows(qq[n * WINDOW : min((n + 2) * WINDOW, rows)], keys))
                now.append(found[:WINDOW])
                before.append(found[WINDOW:])
            scores.append((now, before))
        for j in range(GROUP):
            head = GROUP * group + j
            columns = head_columns(head)
            vv = side(*halves(v_ref[:, columns]))
            now, before = scores[j]
            gain_a = gain_ref[0, begin + head]
            for n in range(tiles):
                inner_high, inner_low = halves(jnp.where(lower, now[n], 0.0))
                if n == 0:
                    wide = dot(stack(inner_high, inner_low), vv[tile(0)])
                    b_ref[tile(0), columns] = folded(wide[:WINDOW]) + wide[WINDOW:, :HD]
                    a_ref[tile(0), columns] = jnp.zeros((WINDOW, HD), F32)
                    continue
                weights, total = weights_of(jnp.where(lower, now[n], before[n]))
                pair_high, pair_low = masked_pair(weights, below, above)
                if n % 2:
                    before_high, before_low = halves(before[n])
                else:
                    before_high = before_low = jnp.zeros((WINDOW, HD), BF16)
                left = jnp.concatenate(
                    [pair_high, pair_low, side(before_high, inner_high), side(before_low, inner_low)], axis=0
                )
                wide = dot(left, vv[(n - 1) * WINDOW : (n + 1) * WINDOW])
                a = (folded(wide[tile(0)]) + wide[tile(1), :HD]) * (gain_a / total)
                a_ref[tile(n), columns] = a
                square_ref[tile(n), :] += a * a
                b_ref[tile(n), columns] = folded(wide[tile(2)]) + wide[tile(3), :HD]

    if part == 0:
        for group in range(groups):
            load(1, group).wait()
    sum_ref[...] = row_sums(square_ref[...])


def message_kernel(first_ref, chip_ref, _, out_ref):
    index = lax.axis_index("ctx")
    core, x, y = index % 2, (index >> 1) % 2, index >> 2
    first = jnp.where((core == 0) | (y == 1), first_ref[...], 0.0)
    out_ref[...] = first + jnp.where((core == 0) | (x == 0), chip_ref[...], 0.0)


def prefix_kernel(first_ref, second_ref, keep_ref, beside_ref, _, mine_ref, other_ref):
    index = lax.axis_index("ctx")
    core, x, y = index % 2, (index >> 1) % 2, index >> 2
    use_first = jnp.where(core == 0, x, y) == 1
    use_second = (core == 1) & ((x == 1) | (y == 1)) | (core == 0) & (y == 1)
    earlier = jnp.where(use_first, first_ref[...], 0.0) + jnp.where(use_second, second_ref[...], 0.0)
    mine_ref[...] = earlier + jnp.where(core == 1, beside_ref[...], 0.0)
    other_ref[...] = earlier + jnp.where(core == 0, keep_ref[...], 0.0)


def earlier_kernel(gain_ref, *refs):
    state_refs, half_refs, q_refs, b_refs, sum_refs, out_refs = (refs[2 * i : 2 * i + 2] for i in range(6))
    sums_ref, square_ref = refs[12:]
    rows, width = b_refs[0].shape
    middle = rows // 2
    square_ref[...] = jnp.zeros_like(square_ref)
    for part in range(2):
        begin = first_head(part, 2 * width // HD)
        for head in range(width // HD):
            columns = slice(head * HD, (head + 1) * HD)
            state = state_refs[part][head]
            gain_b = gain_ref[1, begin + head]
            for span, held in ((slice(0, middle), state), (slice(middle, rows), state + half_refs[part][head])):
                qq = side(*halves(q_refs[part][span, columns]))
                b = gain_b * (b_refs[part][span, columns] + folded(dot(qq, wide_state(held))))
                out_refs[part][span, columns] = b
                square_ref[span, :] += b * b
    sums = row_sums(square_ref[...])
    row = lax.broadcasted_iota(jnp.int32, sums.shape, 0)
    sums_ref[...] = jnp.where(row == 0, sum(ref[...] for ref in sum_refs), sums)


def added_columns(refs, columns):
    total = refs[0][:, columns]
    for ref in refs[1:]:
        total = total + ref[:, columns]
    return total


def first_weights_kernel(gain_ref, *refs):
    q_refs, k_refs, v_refs = (refs[2 * i : 2 * i + 2] for i in range(3))
    *tail_refs, weights_ref, out_ref = refs[6:]
    lower = lower_mask()
    reachable = jnp.logical_or(lower, lax.axis_index("ctx") > 0)
    top = slice(0, WINDOW)
    width = q_refs[0].shape[1]
    for part in range(2):
        begin = first_head(part, 2 * width // HD)
        scores = []
        for head in range(width // HD):
            columns = slice(head * HD, (head + 1) * HD)
            sent = (1 - part) * width + head * HD
            qq = side(*halves(q_refs[part][top, columns]))
            now = folded(dot_rows(qq, wide_keys(*halves(k_refs[part][top, columns]))))
            before = folded(dot_rows(qq, wide_keys(*halves(added_columns(tail_refs, slice(sent, sent + HD))))))
            scores.append(jnp.where(reachable, jnp.where(lower, now, before), -jnp.inf))
        for head in range(width // HD):
            columns = slice(head * HD, (head + 1) * HD)
            weights, total = weights_of(scores[head])
            weights = weights * (gain_ref[0, begin + head] / total)
            now_high, now_low = halves(jnp.where(lower, weights, 0.0))
            vv = side(*halves(v_refs[part][top, columns]))
            wide = dot(stack(now_high, now_low), vv)
            out_ref[:, part * width + head * HD : part * width + (head + 1) * HD] = (
                folded(wide[:WINDOW]) + wide[WINDOW:, :HD]
            )
            held = slice(2 * (part * width + head * HD), 2 * (part * width + (head + 1) * HD))
            weights_ref[:, held] = side(*halves(jnp.where(lower, 0.0, weights)))


def first_values_kernel(weights_ref, now_ref, tail_ref, _, a_ref, sums_ref):
    square = jnp.zeros((WINDOW, HD), F32)
    heads = now_ref.shape[1] // HD
    for part in range(2):
        for head in range(heads // 2):
            j = part * (heads // 2) + head
            sent = (1 - part) * (heads // 2) + head
            columns = slice(j * HD, (j + 1) * HD)
            high = weights_ref[:, 2 * j * HD : (2 * j + 1) * HD]
            low = weights_ref[:, (2 * j + 1) * HD : 2 * (j + 1) * HD]
            wide = dot(stack(high, low), side(*halves(tail_ref[:, sent * HD : (sent + 1) * HD])))
            a = now_ref[:, columns] + (folded(wide[:WINDOW]) + wide[WINDOW:, :HD])
            a_ref[:, columns] = a
            square = square + a * a
    sums_ref[...] = row_sums(square)


def inverse_norm(total):
    return 1.0 / jnp.sqrt(total / (HEADS * HD) + EPS)


def added(refs):
    total = refs[0][...]
    for ref in refs[1:]:
        total = total + ref[...]
    return total


def write(part, rows, held, out_ref, out_hbm, sem):
    width = out_ref.shape[1] // 2
    begin = first_head(part, 2 * width // HD) * HD
    there = pl.ds(pl.multiple_of(begin, HD), width)
    copy = pltpu.make_async_copy(
        out_ref.at[held, pl.ds(part * width, width)], out_hbm.at[rows, there], sem
    )
    copy.start()
    return copy


def scale_kernel(parts, _, *refs):
    sums, refs = refs[:parts], refs[parts:]
    a_refs, b_refs, (out_hbm, first_ref, out_ref, sems) = refs[:2], refs[2:4], refs[4:]
    inverse = inverse_norm(added(sums)).T
    width = a_refs[0].shape[1]
    top = slice(0, WINDOW)
    copies = []
    for n in range(out_ref.shape[0] // WINDOW):
        held = slice(n * WINDOW, (n + 1) * WINDOW)
        rows = slice((n + 1) * WINDOW, (n + 2) * WINDOW)
        inverse_a, inverse_b = inverse[rows, 0:1], inverse[rows, 1:2]
        for part in range(2):
            columns = slice(part * width, (part + 1) * width)
            out_ref[held, columns] = a_refs[part][rows, :] * inverse_a + b_refs[part][rows, :] * inverse_b
            copies.append(write(part, rows, held, out_ref, out_hbm, sems.at[n, part]))
    for part in range(2):
        first_ref[:, part * width : (part + 1) * width] = b_refs[part][top, :] * inverse[top, 1:2]
    for copy in copies:
        copy.wait()


def first_scale_kernel(parts, a_ref, b_ref, _, *refs):
    sums, (out_hbm, out_ref, sems) = refs[:parts], refs[parts:]
    inverse_a = inverse_norm(added(sums)).T[:, 0:1]
    width = b_ref.shape[1] // 2
    copies = []
    pieces = sems.shape[0]
    for n in range(pieces):
        rows = slice(n * WINDOW // pieces, (n + 1) * WINDOW // pieces)
        for part in range(2):
            columns = slice(part * width, (part + 1) * width)
            out_ref[rows, columns] = a_ref[rows, columns] * inverse_a[rows] + b_ref[rows, columns]
            copies.append(write(part, rows, rows, out_ref, out_hbm, sems.at[n, part]))
    for copy in copies:
        copy.wait()


def swap(block, axis, bit):
    return lax.ppermute(block, axis, [(i, i ^ bit) for i in range(lax.axis_size(axis))])


def everyone(block, axis):
    return [block] + [swap(block, axis, bits) for bits in range(1, lax.axis_size(axis))]


def first_phase(chip):
    return lax.ppermute(chip, "ctx", [(i, i ^ (2 if i % 2 == 0 else 4)) for i in range(8)])


def second_phase(message):
    return lax.ppermute(message, "ctx", [(i, i ^ (4 if i % 2 == 0 else 2)) for i in range(8)])


def doubled_prefix(chip):
    index = lax.axis_index("ctx")
    earlier = jnp.zeros_like(chip)
    running = chip
    bit = 2
    while bit < lax.axis_size("ctx"):
        partner = swap(running, "ctx", bit)
        earlier = earlier + jnp.where((index & bit) != 0, partner, 0.0)
        running = running + partner
        bit *= 2
    return earlier


def shards(queries, keys, values, head_gain):
    rows, width = queries.shape
    heads = head_gain.shape[1]
    queries, keys, values = (
        pltpu.with_memory_space_constraint(x, pltpu.HBM) for x in (queries, keys, values)
    )
    smem = pl.BlockSpec(memory_space=pltpu.SMEM)
    anywhere = pl.BlockSpec(memory_space=pl.ANY)
    vmem = pl.BlockSpec()

    def array(*shape, dtype=F32):
        return jax.ShapeDtypeStruct(shape, dtype)

    def call(kernel, name, **kwargs):
        return pl.pallas_call(
            kernel,
            name=name,
            compiler_params=pltpu.CompilerParams(vmem_limit_bytes=VMEM_BYTES),
            cost_estimate=pl.CostEstimate(flops=0, bytes_accessed=0, transcendentals=0),
            **kwargs,
        )

    packed = array(heads // 2, HD, HD)
    half = array(rows, width // 2)
    first_tile = array(WINDOW, width)
    dma = pltpu.SemaphoreType.DMA
    groups = heads // (2 * GROUP)

    def totals(part, after):
        return call(
            functools.partial(totals_kernel, part),
            "totals",
            in_specs=[anywhere] * 3,
            out_shape=[packed, packed, half, half],
            scratch_shapes=[dma((2, groups))],
        )(keys, values, after)

    def local(part, query_source, after):
        return call(
            functools.partial(local_kernel, part),
            "local",
            in_specs=[smem, vmem if part else anywhere, vmem, vmem, anywhere],
            out_shape=[half, half, array(8, rows)] + ([] if part else [half, half]),
            scratch_shapes=[pltpu.VMEM((rows, HD), F32)] + ([] if part else [dma((2, groups))]),
        )(head_gain, query_source, held_k[part], held_v[part], after)

    route = [(i, i + 1) for i in range(lax.axis_size("ctx") - 1)]
    short = lax.axis_size("ctx") == 8
    tail_k = call(
        key_tail_kernel,
        "key_tail",
        in_specs=[anywhere],
        out_shape=first_tile,
        scratch_shapes=[dma((2,))],
    )(keys)
    before_k = [lax.ppermute(tail_k, "ctx", [(1, 2), (5, 6)])] if short else []
    send, *held_0 = totals(0, queries)
    beside = swap(send, "ctx", 1)
    keep, *held_1 = totals(1, send)
    early, held_k, held_v = zip(held_0, held_1)
    chip = call(chip_kernel, "chip", in_specs=[vmem, vmem], out_shape=packed)(keep, beside)
    tail_k, tail_v = (
        call(tail_kernel, "tail", in_specs=[vmem, vmem, anywhere], out_shape=first_tile)(*held, chip)
        for held in (held_k, held_v)
    )
    later = [pair for pair in route if not short or pair not in ((1, 2), (5, 6))]
    before_k.append(lax.ppermute(tail_k, "ctx", later))
    if short:
        relayed = lax.ppermute(tail_v, "ctx", [(3, 7)])
        route = [pair for pair in route if pair != (3, 4)] + [(7, 4)]
    *local_0, query_0, query_1 = local(0, queries, before_k[0])
    message = local_0[2]
    if lax.axis_size("ctx") == 8:
        first = first_phase(chip)
        message = call(
            message_kernel,
            "message",
            in_specs=[vmem, vmem, anywhere],
            out_shape=packed,
        )(first, chip, message)
    held_q = query_0, query_1
    window, linear, window_sums = zip(local_0, local(1, query_1, message))
    if short:
        tail_v = call(
            relay_kernel, "relay", in_specs=[vmem, vmem, anywhere], out_shape=first_tile
        )(tail_v, relayed, window_sums[1])
    before_v = lax.ppermute(tail_v, "ctx", route)
    first_weights, first_now = call(
        first_weights_kernel,
        "first_weights",
        in_specs=[smem] + [vmem] * (6 + len(before_k)),
        out_shape=[array(WINDOW, 2 * width, dtype=BF16), first_tile],
    )(head_gain, *held_q, *held_k, *held_v, *before_k)

    if lax.axis_size("ctx") == 8:
        second = second_phase(message)
        mine, other = call(
            prefix_kernel,
            "prefix",
            in_specs=[vmem] * 4 + [anywhere],
            out_shape=[packed, packed],
        )(first, second, keep, beside, first_now)
    else:
        earlier = doubled_prefix(chip)
        core = lax.axis_index("ctx") % 2
        mine = earlier + jnp.where(core == 1, beside, 0.0)
        other = earlier + jnp.where(core == 0, keep, 0.0)
    other = swap(other, "ctx", 1)

    *linear, sums = call(
        earlier_kernel,
        "earlier",
        in_specs=[smem] + [vmem] * 10,
        out_shape=[half, half, array(8, rows)],
        scratch_shapes=[pltpu.VMEM((rows, HD), F32)],
    )(head_gain, other, mine, *early, *held_q, *linear, *window_sums)
    sums = everyone(sums, "head")
    first_a, first_sums = call(
        first_values_kernel,
        "first_values",
        in_specs=[vmem] * 3 + [anywhere],
        out_shape=[first_tile, array(8, WINDOW)],
    )(first_weights, first_now, before_v, sums[0])
    first_sums = everyone(first_sums, "head")
    out, first_b = call(
        functools.partial(scale_kernel, len(sums)),
        "scale",
        in_specs=[anywhere] + [vmem] * (4 + len(sums)),
        out_specs=[anywhere, vmem],
        out_shape=[array(rows, width), first_tile],
        scratch_shapes=[pltpu.VMEM((rows - WINDOW, width), F32), dma((rows // WINDOW - 1, 2))],
    )(first_sums[0], *sums, *window, *linear)
    return call(
        functools.partial(first_scale_kernel, len(sums)),
        "first_scale",
        in_specs=[vmem, vmem, anywhere] + [vmem] * len(sums),
        out_specs=anywhere,
        out_shape=array(rows, width),
        scratch_shapes=[pltpu.VMEM((WINDOW, width), F32), dma((4, 2))],
        input_output_aliases={2: 0},
    )(first_a, first_b, out, *first_sums)


def solution(mesh):
    in_specs = (P("ctx", "head"), P("ctx", "head"), P("ctx", "head"), P(None, "head"))
    out_specs = P("ctx", "head")
    return jax.shard_map(shards, mesh=mesh, in_specs=in_specs, out_specs=out_specs, check_vma=False)
```

```python
import functools
import math

import jax
import jax.numpy as jnp
from jax import lax
from jax.experimental import pallas as pl
from jax.experimental.pallas import tpu as pltpu
from jax.sharding import PartitionSpec as P

HEADS = 64
HD = 128
WINDOW = 128
EPS = 1e-06
F32 = jnp.float32
BF16 = jnp.bfloat16
EXP2_SCALE = math.log2(math.e) / math.sqrt(HD)
VMEM_BYTES = 20 * 1024 * 1024
GROUP = 4


def halves(x):
    high = x.astype(BF16)
    low = (x - high.astype(F32)).astype(BF16)
    return high, low


def dot(a, b):
    return lax.dot_general(a, b, (((1,), (0,)), ((), ())), preferred_element_type=F32)


def dot_rows(a, b):
    return lax.dot_general(a, b, (((1,), (1,)), ((), ())), preferred_element_type=F32)


def dot_columns(a, b):
    return lax.dot_general(a, b, (((0,), (0,)), ((), ())), preferred_element_type=F32)


def side(a, b):
    return jnp.concatenate([a, b], axis=1)


def stack(a, b):
    return jnp.concatenate([a, b], axis=0)


def outer_state(k_high, k_low, v_high, v_low):
    grid = dot_columns(side(k_high, k_low), side(v_high, v_low))
    return grid[:HD, :HD] + (grid[:HD, HD:] + grid[HD:, :HD]) + grid[HD:, HD:]


def lower_mask():
    rows = lax.broadcasted_iota(jnp.int32, (WINDOW, WINDOW), 0)
    columns = lax.broadcasted_iota(jnp.int32, (WINDOW, WINDOW), 1)
    return rows >= columns


def row_sums(square):
    ones = jnp.ones((8, HD), BF16)
    high, low = halves(square)
    return dot_rows(ones, high) + dot_rows(ones, low)


def wide_keys(k_high, k_low):
    return stack(side(k_high, k_high), side(k_low, jnp.zeros_like(k_low)))


def wide_state(state):
    high, low = halves(state)
    return stack(side(high, low), side(high, jnp.zeros_like(high)))


def folded(wide):
    half = wide.shape[1] // 2
    return wide[:, :half] + wide[:, half:]


def head_columns(head, count=1, width=HD):
    return pl.ds(pl.multiple_of(head * width, width), count * width)


def load_kernel(q_hbm, _, q_ref, sems):
    width = q_ref.shape[1] // sems.shape[0]
    copies = []
    for i in range(sems.shape[0]):
        columns = pl.ds(i * width, width)
        copies.append(pltpu.make_async_copy(q_hbm.at[:, columns], q_ref.at[:, columns], sems.at[i]))
    for copy in copies:
        copy.start()
    for copy in copies:
        copy.wait()


def pass_kernel(*_):
    pass


def chip_kernel(keep_ref, beside_ref, _, out_ref, __):
    out_ref[...] = keep_ref[...] + beside_ref[...]


def totals_kernel(k_hbm, v_hbm, keep_ref, send_ref, half_ref, k_ref, v_ref, tail_k_ref, tail_v_ref, sems):
    core = lax.axis_index("ctx") % 2
    rows, width = k_ref.shape
    middle = rows // 2
    groups = width // (GROUP * HD)

    def copies(group):
        columns = head_columns(group, 1, GROUP * HD)
        return [
            pltpu.make_async_copy(source.at[:, columns], target.at[:, columns], sems.at[i, group])
            for i, (source, target) in enumerate(((k_hbm, k_ref), (v_hbm, v_ref)))
        ]

    for group in range(groups):
        for copy in copies(group):
            copy.start()

    @pl.loop(0, groups)
    def _(group):
        for copy in copies(group):
            copy.wait()
        for i in range(GROUP // 2):
            states = []
            for j in (2 * i, 2 * i + 1):
                head = GROUP * group + j
                columns = head_columns(head)
                k_high, k_low = halves(k_ref[:, columns])
                v_high, v_low = halves(v_ref[:, columns])
                first = outer_state(k_high[:middle], k_low[:middle], v_high[:middle], v_low[:middle])
                second = outer_state(k_high[middle:], k_low[middle:], v_high[middle:], v_low[middle:])
                half_ref[head] = first
                states.append(first + second)
            pair = GROUP // 2 * group + i
            keep_ref[pair] = jnp.where(core == 0, states[0], states[1])
            send_ref[pair] = jnp.where(core == 0, states[1], states[0])
        columns = head_columns(group, 1, GROUP * HD)
        tail_k_ref[:, columns] = k_ref[rows - WINDOW :, columns]
        tail_v_ref[:, columns] = v_ref[rows - WINDOW :, columns]


def weights_of(scores):
    biggest = jnp.max(scores, axis=1, keepdims=True)
    weights = jnp.exp2((scores - biggest) * EXP2_SCALE)
    return weights, jnp.sum(weights, axis=1, keepdims=True)


def masked_pair(weights, below, above):
    high, low = halves(weights)
    return side(high * above, high * below), side(low * above, low * below)


def local_kernel(begin, extra, gain_ref, q_ref, k_ref, v_ref, *refs):
    a_ref, b_ref, sum_ref, square_ref = refs[extra:]
    lower = lower_mask()
    below = jnp.where(lower, 1.0, 0.0).astype(BF16)
    above = jnp.where(lower, 0.0, 1.0).astype(BF16)
    rows, width = a_ref.shape
    tiles = rows // WINDOW
    groups = width // (GROUP * HD)
    square_ref[...] = jnp.zeros_like(square_ref)

    def tile(n):
        return slice(n * WINDOW, (n + 1) * WINDOW)

    @pl.loop(0, groups)
    def _(group):
        scores = []
        for j in range(GROUP):
            columns = head_columns(begin + GROUP * group + j)
            qq = side(*halves(q_ref[:, columns]))
            k_high, k_low = halves(k_ref[:, columns])
            now, before = [], [None]
            for n in range(tiles):
                keys = wide_keys(k_high[tile(n)], k_low[tile(n)])
                found = folded(dot_rows(qq[n * WINDOW : min((n + 2) * WINDOW, rows)], keys))
                now.append(found[:WINDOW])
                before.append(found[WINDOW:])
            scores.append((now, before))
        for j in range(GROUP):
            head = GROUP * group + j
            columns = head_columns(head)
            vv = side(*halves(v_ref[:, head_columns(begin + head)]))
            now, before = scores[j]
            gain_a = gain_ref[0, begin + head]
            for n in range(tiles):
                inner_high, inner_low = halves(jnp.where(lower, now[n], 0.0))
                if n == 0:
                    wide = dot(stack(inner_high, inner_low), vv[tile(0)])
                    b_ref[tile(0), columns] = folded(wide[:WINDOW]) + wide[WINDOW:, :HD]
                    a_ref[tile(0), columns] = jnp.zeros((WINDOW, HD), F32)
                    continue
                weights, total = weights_of(jnp.where(lower, now[n], before[n]))
                pair_high, pair_low = masked_pair(weights, below, above)
                if n % 2:
                    before_high, before_low = halves(before[n])
                else:
                    before_high = before_low = jnp.zeros((WINDOW, HD), BF16)
                left = jnp.concatenate(
                    [pair_high, pair_low, side(before_high, inner_high), side(before_low, inner_low)], axis=0
                )
                wide = dot(left, vv[(n - 1) * WINDOW : (n + 1) * WINDOW])
                a = (folded(wide[tile(0)]) + wide[tile(1), :HD]) * (gain_a / total)
                a_ref[tile(n), columns] = a
                square_ref[tile(n), :] += a * a
                b_ref[tile(n), columns] = folded(wide[tile(2)]) + wide[tile(3), :HD]

    sum_ref[...] = row_sums(square_ref[...])


def message_kernel(first_ref, chip_ref, _, out_ref):
    index = lax.axis_index("ctx")
    core, x, y = index % 2, (index >> 1) % 2, index >> 2
    first = jnp.where((core == 0) | (y == 1), first_ref[...], 0.0)
    out_ref[...] = first + jnp.where((core == 0) | (x == 0), chip_ref[...], 0.0)


def prefix_kernel(first_ref, second_ref, keep_ref, beside_ref, *refs):
    mine_ref, other_ref = refs[-2:]
    index = lax.axis_index("ctx")
    core, x, y = index % 2, (index >> 1) % 2, index >> 2
    use_first = jnp.where(core == 0, x, y) == 1
    use_second = (core == 1) & ((x == 1) | (y == 1)) | (core == 0) & (y == 1)
    earlier = jnp.where(use_first, first_ref[...], 0.0) + jnp.where(use_second, second_ref[...], 0.0)
    mine_ref[...] = earlier + jnp.where(core == 1, beside_ref[...], 0.0)
    other_ref[...] = earlier + jnp.where(core == 0, keep_ref[...], 0.0)


def earlier_kernel(count, gain_ref, half_ref, mine_ref, other_ref, q_ref, *refs):
    b_refs, sum_refs, out_refs = (refs[i * count : (i + 1) * count] for i in range(3))
    sums_ref, square_ref = refs[3 * count :]
    core = lax.axis_index("ctx") % 2
    rows = b_refs[0].shape[0]
    middle = rows // 2
    head = 0
    square_ref[...] = jnp.zeros_like(square_ref)
    for b_ref, out_ref in zip(b_refs, out_refs):
        for j in range(b_ref.shape[1] // HD):
            columns = slice(j * HD, (j + 1) * HD)
            state = jnp.where(core == head % 2, mine_ref[head // 2], other_ref[head // 2])
            gain_b = gain_ref[1, head]
            for part, held in ((slice(0, middle), state), (slice(middle, rows), state + half_ref[head])):
                qq = side(*halves(q_ref[part, head * HD : (head + 1) * HD]))
                b = gain_b * (b_ref[part, columns] + folded(dot(qq, wide_state(held))))
                out_ref[part, columns] = b
                square_ref[part, :] += b * b
            head += 1
    sums = row_sums(square_ref[...])
    row = lax.broadcasted_iota(jnp.int32, sums.shape, 0)
    sums_ref[...] = jnp.where(row == 0, sum(ref[...] for ref in sum_refs), sums)


def first_weights_kernel(gain_ref, q_ref, k_ref, v_ref, tail_ref, weights_ref, out_ref):
    lower = lower_mask()
    reachable = jnp.logical_or(lower, lax.axis_index("ctx") > 0)
    top = slice(0, WINDOW)
    count = tail_ref.shape[1] // (2 * HD)
    for part in range(2):
        scores = []
        for j in range(count):
            columns = slice((part * count + j) * HD, (part * count + j + 1) * HD)
            qq = side(*halves(q_ref[top, columns]))
            now = folded(dot_rows(qq, wide_keys(*halves(k_ref[top, columns]))))
            before = folded(dot_rows(qq, wide_keys(*halves(tail_ref[:, columns]))))
            scores.append(jnp.where(reachable, jnp.where(lower, now, before), -jnp.inf))
        for j in range(count):
            head = part * count + j
            columns = slice(head * HD, (head + 1) * HD)
            weights, total = weights_of(scores[j])
            weights = weights * (gain_ref[0, head] / total)
            now_high, now_low = halves(jnp.where(lower, weights, 0.0))
            vv = side(*halves(v_ref[top, columns]))
            wide = dot(stack(now_high, now_low), vv)
            out_ref[:, columns] = folded(wide[:WINDOW]) + wide[WINDOW:, :HD]
            weights_ref[:, 2 * head * HD : 2 * (head + 1) * HD] = side(*halves(jnp.where(lower, 0.0, weights)))


def first_values_kernel(weights_ref, now_ref, tail_v_ref, _, a_ref, sums_ref):
    square = jnp.zeros((WINDOW, HD), F32)
    for j in range(now_ref.shape[1] // HD):
        columns = slice(j * HD, (j + 1) * HD)
        high = weights_ref[:, 2 * j * HD : (2 * j + 1) * HD]
        low = weights_ref[:, (2 * j + 1) * HD : 2 * (j + 1) * HD]
        wide = dot(stack(high, low), side(*halves(tail_v_ref[:, columns])))
        a = now_ref[:, columns] + (folded(wide[:WINDOW]) + wide[WINDOW:, :HD])
        a_ref[:, columns] = a
        square = square + a * a
    sums_ref[...] = row_sums(square)


def inverse_norm(total):
    return 1.0 / jnp.sqrt(total / (HEADS * HD) + EPS)


def added(refs):
    total = refs[0][...]
    for ref in refs[1:]:
        total = total + ref[...]
    return total


def scale_kernel(count, parts, _, *refs):
    sums, refs = refs[:parts], refs[parts:]
    a_refs, b_refs, (out_hbm, out_ref, sems) = refs[:count], refs[count : 2 * count], refs[2 * count :]
    inverse = inverse_norm(added(sums)).T
    copies = []
    for n in range(out_ref.shape[0] // WINDOW):
        held = slice(n * WINDOW, (n + 1) * WINDOW)
        rows = slice((n + 1) * WINDOW, (n + 2) * WINDOW)
        inverse_a, inverse_b = inverse[rows, 0:1], inverse[rows, 1:2]
        begin = 0
        for a_ref, b_ref in zip(a_refs, b_refs):
            columns = slice(begin, begin + a_ref.shape[1])
            out_ref[held, columns] = a_ref[rows, :] * inverse_a + b_ref[rows, :] * inverse_b
            begin = columns.stop
        copy = pltpu.make_async_copy(out_ref.at[held, :], out_hbm.at[rows, :], sems.at[n])
        copy.start()
        copies.append(copy)
    for copy in copies:
        copy.wait()


def first_scale_kernel(count, parts, a_ref, _, *refs):
    b_refs, refs = refs[:count], refs[count:]
    sums, first_sums, (out_hbm, out_ref, sems) = refs[:parts], refs[parts : 2 * parts], refs[2 * parts :]
    inverse_a = inverse_norm(added(first_sums)).T[:, 0:1]
    inverse_b = inverse_norm(added(sums)[:, :WINDOW]).T[:, 1:2]
    copies = []
    for n in range(sems.shape[0]):
        rows = slice(n * WINDOW // sems.shape[0], (n + 1) * WINDOW // sems.shape[0])
        begin = 0
        for b_ref in b_refs:
            columns = slice(begin, begin + b_ref.shape[1])
            out_ref[rows, columns] = a_ref[rows, columns] * inverse_a[rows] + b_ref[rows, :] * inverse_b[rows]
            begin = columns.stop
        copy = pltpu.make_async_copy(out_ref.at[rows, :], out_hbm.at[rows, :], sems.at[n])
        copy.start()
        copies.append(copy)
    for copy in copies:
        copy.wait()


def swap(block, axis, bit):
    return lax.ppermute(block, axis, [(i, i ^ bit) for i in range(lax.axis_size(axis))])


def everyone(block, axis):
    return [block] + [swap(block, axis, bits) for bits in range(1, lax.axis_size(axis))]


def first_phase(chip):
    return lax.ppermute(chip, "ctx", [(i, i ^ (2 if i % 2 == 0 else 4)) for i in range(8)])


def second_phase(message):
    return lax.ppermute(message, "ctx", [(i, i ^ (4 if i % 2 == 0 else 2)) for i in range(8)])


def doubled_prefix(chip):
    index = lax.axis_index("ctx")
    earlier = jnp.zeros_like(chip)
    running = chip
    bit = 2
    while bit < lax.axis_size("ctx"):
        partner = swap(running, "ctx", bit)
        earlier = earlier + jnp.where((index & bit) != 0, partner, 0.0)
        running = running + partner
        bit *= 2
    return earlier


def shards(queries, keys, values, head_gain):
    rows, width = queries.shape
    heads = head_gain.shape[1]
    queries, keys, values = (
        pltpu.with_memory_space_constraint(x, pltpu.HBM) for x in (queries, keys, values)
    )
    smem = pl.BlockSpec(memory_space=pltpu.SMEM)
    anywhere = pl.BlockSpec(memory_space=pl.ANY)
    vmem = pl.BlockSpec()

    def array(*shape, dtype=F32):
        return jax.ShapeDtypeStruct(shape, dtype)

    def call(kernel, name, **kwargs):
        return pl.pallas_call(
            kernel,
            name=name,
            compiler_params=pltpu.CompilerParams(vmem_limit_bytes=VMEM_BYTES),
            cost_estimate=pl.CostEstimate(flops=0, bytes_accessed=0, transcendentals=0),
            **kwargs,
        )

    packed = array(heads // 2, HD, HD)
    first_tile = array(WINDOW, width)
    dma = pltpu.SemaphoreType.DMA
    keep, send, half, held_k, held_v, tail_k, tail_v = call(
        totals_kernel,
        "totals",
        in_specs=[anywhere, anywhere],
        out_shape=[
            packed,
            packed,
            array(heads, HD, HD),
            array(rows, width),
            array(rows, width),
            first_tile,
            first_tile,
        ],
        scratch_shapes=[dma((2, heads // GROUP))],
    )(keys, values)
    beside = swap(send, "ctx", 1)
    chip, tail_k = call(
        chip_kernel,
        "chip",
        in_specs=[vmem, vmem, anywhere],
        out_specs=[vmem, anywhere],
        out_shape=[packed, first_tile],
        input_output_aliases={2: 1},
    )(keep, beside, tail_k)
    held_q = call(
        load_kernel,
        "load",
        in_specs=[anywhere, anywhere],
        out_shape=array(rows, width),
        scratch_shapes=[dma((4,))],
    )(queries, chip)
    def local(begin, count, after):
        taken = count * HD
        after = [] if after is None else [after]
        return call(
            functools.partial(local_kernel, begin, len(after)),
            "local",
            in_specs=[smem, vmem, vmem, vmem] + [anywhere] * len(after),
            out_shape=[array(rows, taken), array(rows, taken), array(8, rows)],
            scratch_shapes=[pltpu.VMEM((rows, HD), F32)],
        )(head_gain, held_q, held_k, held_v, *after)

    def pass_on(array_now, after):
        return call(
            pass_kernel,
            "pass",
            in_specs=[anywhere, anywhere],
            out_specs=anywhere,
            out_shape=array(*array_now.shape),
            input_output_aliases={0: 0},
        )(array_now, after)

    begin = heads * 3 // 4 // GROUP * GROUP
    parts = [local(0, GROUP, None)]
    route = [(i, i + 1) for i in range(lax.axis_size("ctx") - 1)]
    before_k = lax.ppermute(pass_on(tail_k, parts[0][2]), "ctx", route)
    if begin > GROUP:
        parts.append(local(GROUP, begin - GROUP, parts[0][2]))
    message = None
    if lax.axis_size("ctx") == 8:
        first = first_phase(chip)
        message = call(
            message_kernel,
            "message",
            in_specs=[vmem, vmem, anywhere],
            out_shape=packed,
        )(first, chip, parts[-1][2])
    parts.append(local(begin, heads - begin, parts[-1][2] if message is None else message))
    window, linear, window_sums = zip(*parts)
    before_v = lax.ppermute(pass_on(tail_v, window_sums[-1]), "ctx", route)
    first_weights, first_now = call(
        first_weights_kernel,
        "first_weights",
        in_specs=[smem] + [vmem] * 4,
        out_shape=[array(WINDOW, 2 * width, dtype=BF16), first_tile],
    )(head_gain, held_q, held_k, held_v, before_k)

    if message is not None:
        second = second_phase(message)
        mine, other = call(
            prefix_kernel,
            "prefix",
            in_specs=[vmem] * 4 + [anywhere],
            out_shape=[packed, packed],
        )(first, second, keep, beside, first_now)
    else:
        earlier = doubled_prefix(chip)
        core = lax.axis_index("ctx") % 2
        mine = earlier + jnp.where(core == 1, beside, 0.0)
        other = earlier + jnp.where(core == 0, keep, 0.0)
    other = swap(other, "ctx", 1)

    *linear, sums = call(
        functools.partial(earlier_kernel, len(parts)),
        "earlier",
        in_specs=[smem] + [vmem] * (4 + 2 * len(parts)),
        out_shape=[array(*x.shape) for x in linear] + [array(8, rows)],
        scratch_shapes=[pltpu.VMEM((rows, HD), F32)],
    )(head_gain, half, mine, other, held_q, *linear, *window_sums)
    sums = everyone(sums, "head")
    first_a, first_sums = call(
        first_values_kernel,
        "first_values",
        in_specs=[vmem] * 3 + [anywhere],
        out_shape=[first_tile, array(8, WINDOW)],
    )(first_weights, first_now, before_v, sums[0])
    first_sums = everyone(first_sums, "head")
    out = call(
        functools.partial(scale_kernel, len(parts), len(sums)),
        "scale",
        in_specs=[anywhere] + [vmem] * (2 * len(parts) + len(sums)),
        out_specs=anywhere,
        out_shape=array(rows, width),
        scratch_shapes=[pltpu.VMEM((rows - WINDOW, width), F32), dma((rows // WINDOW - 1,))],
    )(first_sums[0], *sums, *window, *linear)
    return call(
        functools.partial(first_scale_kernel, len(parts), len(sums)),
        "first_scale",
        in_specs=[vmem, anywhere] + [vmem] * (len(parts) + 2 * len(sums)),
        out_specs=anywhere,
        out_shape=array(rows, width),
        scratch_shapes=[pltpu.VMEM((WINDOW, width), F32), dma((4,))],
        input_output_aliases={1: 0},
    )(first_a, out, *linear, *sums, *first_sums)


def solution(mesh):
    in_specs = (P("ctx", "head"), P("ctx", "head"), P("ctx", "head"), P(None, "head"))
    out_specs = P("ctx", "head")
    return jax.shard_map(shards, mesh=mesh, in_specs=in_specs, out_specs=out_specs, check_vma=False)
```

```python
import functools
import math

import jax
import jax.numpy as jnp
from jax import lax
from jax.experimental import pallas as pl
from jax.experimental.pallas import tpu as pltpu
from jax.sharding import PartitionSpec as P

HEADS = 64
HD = 128
WINDOW = 128
EPS = 1e-06
F32 = jnp.float32
BF16 = jnp.bfloat16
EXP2_SCALE = math.log2(math.e) / math.sqrt(HD)
VMEM_BYTES = 20 * 1024 * 1024
GROUP = 4


def halves(x):
    high = x.astype(BF16)
    low = (x - high.astype(F32)).astype(BF16)
    return high, low


def dot(a, b):
    return lax.dot_general(a, b, (((1,), (0,)), ((), ())), preferred_element_type=F32)


def dot_rows(a, b):
    return lax.dot_general(a, b, (((1,), (1,)), ((), ())), preferred_element_type=F32)


def dot_columns(a, b):
    return lax.dot_general(a, b, (((0,), (0,)), ((), ())), preferred_element_type=F32)


def side(a, b):
    return jnp.concatenate([a, b], axis=1)


def stack(a, b):
    return jnp.concatenate([a, b], axis=0)


def outer_state(k_high, k_low, v_high, v_low):
    grid = dot_columns(side(k_high, k_low), side(v_high, v_low))
    return grid[:HD, :HD] + (grid[:HD, HD:] + grid[HD:, :HD]) + grid[HD:, HD:]


def lower_mask():
    rows = lax.broadcasted_iota(jnp.int32, (WINDOW, WINDOW), 0)
    columns = lax.broadcasted_iota(jnp.int32, (WINDOW, WINDOW), 1)
    return rows >= columns


def row_sums(square):
    ones = jnp.ones((8, HD), BF16)
    high, low = halves(square)
    return dot_rows(ones, high) + dot_rows(ones, low)


def wide_keys(k_high, k_low):
    return stack(side(k_high, k_high), side(k_low, k_low))


def wide_state(state):
    high, low = halves(state)
    return stack(side(high, low), side(high, low))


def folded(wide):
    half = wide.shape[1] // 2
    return wide[:, :half] + wide[:, half:]


def head_columns(head, count=1, width=HD):
    return pl.ds(pl.multiple_of(head * width, width), count * width)


def load_kernel(q_hbm, _, q_ref, sems):
    width = q_ref.shape[1] // sems.shape[0]
    copies = []
    for i in range(sems.shape[0]):
        columns = pl.ds(i * width, width)
        copies.append(pltpu.make_async_copy(q_hbm.at[:, columns], q_ref.at[:, columns], sems.at[i]))
    for copy in copies:
        copy.start()
    for copy in copies:
        copy.wait()


def pass_kernel(*_):
    pass


def chip_kernel(keep_ref, beside_ref, _, __, out_ref, ___):
    out_ref[...] = keep_ref[...] + beside_ref[...]


def totals_kernel(k_hbm, v_hbm, keep_ref, send_ref, half_ref, k_ref, v_ref, tail_k_ref, tail_v_ref, sems):
    core = lax.axis_index("ctx") % 2
    rows, width = k_ref.shape
    middle = rows // 2
    groups = width // (GROUP * HD)

    def copies(group):
        columns = head_columns(group, 1, GROUP * HD)
        return [
            pltpu.make_async_copy(source.at[:, columns], target.at[:, columns], sems.at[i, group])
            for i, (source, target) in enumerate(((k_hbm, k_ref), (v_hbm, v_ref)))
        ]

    for group in range(groups):
        for copy in copies(group):
            copy.start()

    @pl.loop(0, groups)
    def _(group):
        for copy in copies(group):
            copy.wait()
        for i in range(GROUP // 2):
            states = []
            for j in (2 * i, 2 * i + 1):
                head = GROUP * group + j
                columns = head_columns(head)
                k_high, k_low = halves(k_ref[:, columns])
                v_high, v_low = halves(v_ref[:, columns])
                first = outer_state(k_high[:middle], k_low[:middle], v_high[:middle], v_low[:middle])
                second = outer_state(k_high[middle:], k_low[middle:], v_high[middle:], v_low[middle:])
                half_ref[head] = first
                states.append(first + second)
            pair = GROUP // 2 * group + i
            keep_ref[pair] = jnp.where(core == 0, states[0], states[1])
            send_ref[pair] = jnp.where(core == 0, states[1], states[0])
        columns = head_columns(group, 1, GROUP * HD)
        tail_k_ref[:, columns] = k_ref[rows - WINDOW :, columns]
        tail_v_ref[:, columns] = v_ref[rows - WINDOW :, columns]


def weights_of(scores):
    biggest = jnp.max(scores, axis=1, keepdims=True)
    weights = jnp.exp2((scores - biggest) * EXP2_SCALE)
    return weights, jnp.sum(weights, axis=1, keepdims=True)


def masked_pair(weights, below, above):
    high, low = halves(weights)
    return side(high * above, high * below), side(low * above, low * below)


def local_kernel(begin, extra, gain_ref, q_ref, k_ref, v_ref, *refs):
    a_ref, b_ref, sum_ref, square_ref = refs[extra:]
    lower = lower_mask()
    below = jnp.where(lower, 1.0, 0.0).astype(BF16)
    above = jnp.where(lower, 0.0, 1.0).astype(BF16)
    rows, width = a_ref.shape
    tiles = rows // WINDOW
    groups = width // (GROUP * HD)
    square_ref[...] = jnp.zeros_like(square_ref)

    def tile(n):
        return slice(n * WINDOW, (n + 1) * WINDOW)

    @pl.loop(0, groups)
    def _(group):
        scores = []
        for j in range(GROUP):
            columns = head_columns(begin + GROUP * group + j)
            qq = side(*halves(q_ref[:, columns]))
            k_high, k_low = halves(k_ref[:, columns])
            now, before = [], [None]
            for n in range(tiles):
                keys = wide_keys(k_high[tile(n)], k_low[tile(n)])
                found = folded(dot_rows(qq[n * WINDOW : min((n + 2) * WINDOW, rows)], keys))
                now.append(found[:WINDOW])
                before.append(found[WINDOW:])
            scores.append((now, before))
        for j in range(GROUP):
            head = GROUP * group + j
            columns = head_columns(head)
            vv = side(*halves(v_ref[:, head_columns(begin + head)]))
            now, before = scores[j]
            gain_a = gain_ref[0, begin + head]
            for n in range(tiles):
                inner_high, inner_low = halves(jnp.where(lower, now[n], 0.0))
                if n == 0:
                    wide = dot(stack(inner_high, inner_low), vv[tile(0)])
                    b_ref[tile(0), columns] = folded(wide[:WINDOW]) + wide[WINDOW:, :HD]
                    a_ref[tile(0), columns] = jnp.zeros((WINDOW, HD), F32)
                    continue
                weights, total = weights_of(jnp.where(lower, now[n], before[n]))
                pair_high, pair_low = masked_pair(weights, below, above)
                if n % 2:
                    before_high, before_low = halves(before[n])
                else:
                    before_high = before_low = jnp.zeros((WINDOW, HD), BF16)
                left = jnp.concatenate(
                    [pair_high, pair_low, side(before_high, inner_high), side(before_low, inner_low)], axis=0
                )
                wide = dot(left, vv[(n - 1) * WINDOW : (n + 1) * WINDOW])
                a = (folded(wide[tile(0)]) + wide[tile(1), :HD]) * (gain_a / total)
                a_ref[tile(n), columns] = a
                square_ref[tile(n), :] += a * a
                b_ref[tile(n), columns] = folded(wide[tile(2)]) + wide[tile(3), :HD]

    sum_ref[...] = row_sums(square_ref[...])


def message_kernel(first_ref, chip_ref, _, out_ref):
    index = lax.axis_index("ctx")
    core, x, y = index % 2, (index >> 1) % 2, index >> 2
    first = jnp.where((core == 0) | (y == 1), first_ref[...], 0.0)
    out_ref[...] = first + jnp.where((core == 0) | (x == 0), chip_ref[...], 0.0)


def prefix_kernel(first_ref, second_ref, keep_ref, beside_ref, *refs):
    mine_ref, other_ref = refs[-2:]
    index = lax.axis_index("ctx")
    core, x, y = index % 2, (index >> 1) % 2, index >> 2
    use_first = jnp.where(core == 0, x, y) == 1
    use_second = (core == 1) & ((x == 1) | (y == 1)) | (core == 0) & (y == 1)
    earlier = jnp.where(use_first, first_ref[...], 0.0) + jnp.where(use_second, second_ref[...], 0.0)
    mine_ref[...] = earlier + jnp.where(core == 1, beside_ref[...], 0.0)
    other_ref[...] = earlier + jnp.where(core == 0, keep_ref[...], 0.0)


def earlier_kernel(count, gain_ref, half_ref, mine_ref, other_ref, q_ref, *refs):
    b_refs, sum_refs, out_refs = (refs[i * count : (i + 1) * count] for i in range(3))
    sums_ref, square_ref = refs[3 * count :]
    core = lax.axis_index("ctx") % 2
    rows = b_refs[0].shape[0]
    middle = rows // 2
    head = 0
    square_ref[...] = jnp.zeros_like(square_ref)
    for b_ref, out_ref in zip(b_refs, out_refs):
        for j in range(b_ref.shape[1] // HD):
            columns = slice(j * HD, (j + 1) * HD)
            state = jnp.where(core == head % 2, mine_ref[head // 2], other_ref[head // 2])
            gain_b = gain_ref[1, head]
            for part, held in ((slice(0, middle), state), (slice(middle, rows), state + half_ref[head])):
                qq = side(*halves(q_ref[part, head * HD : (head + 1) * HD]))
                b = gain_b * (b_ref[part, columns] + folded(dot(qq, wide_state(held))))
                out_ref[part, columns] = b
                square_ref[part, :] += b * b
            head += 1
    sums = row_sums(square_ref[...])
    row = lax.broadcasted_iota(jnp.int32, sums.shape, 0)
    sums_ref[...] = jnp.where(row == 0, sum(ref[...] for ref in sum_refs), sums)


def first_weights_kernel(gain_ref, q_ref, k_ref, v_ref, tail_ref, weights_ref, out_ref):
    lower = lower_mask()
    reachable = jnp.logical_or(lower, lax.axis_index("ctx") > 0)
    top = slice(0, WINDOW)
    count = tail_ref.shape[1] // (2 * HD)
    for part in range(2):
        scores = []
        for j in range(count):
            columns = slice((part * count + j) * HD, (part * count + j + 1) * HD)
            qq = side(*halves(q_ref[top, columns]))
            now = folded(dot_rows(qq, wide_keys(*halves(k_ref[top, columns]))))
            before = folded(dot_rows(qq, wide_keys(*halves(tail_ref[:, columns]))))
            scores.append(jnp.where(reachable, jnp.where(lower, now, before), -jnp.inf))
        for j in range(count):
            head = part * count + j
            columns = slice(head * HD, (head + 1) * HD)
            weights, total = weights_of(scores[j])
            weights = weights * (gain_ref[0, head] / total)
            now_high, now_low = halves(jnp.where(lower, weights, 0.0))
            vv = side(*halves(v_ref[top, columns]))
            wide = dot(stack(now_high, now_low), vv)
            out_ref[:, columns] = folded(wide[:WINDOW]) + wide[WINDOW:, :HD]
            weights_ref[:, 2 * head * HD : 2 * (head + 1) * HD] = side(*halves(jnp.where(lower, 0.0, weights)))


def first_values_kernel(weights_ref, now_ref, tail_v_ref, _, a_ref, sums_ref):
    square = jnp.zeros((WINDOW, HD), F32)
    for j in range(now_ref.shape[1] // HD):
        columns = slice(j * HD, (j + 1) * HD)
        high = weights_ref[:, 2 * j * HD : (2 * j + 1) * HD]
        low = weights_ref[:, (2 * j + 1) * HD : 2 * (j + 1) * HD]
        wide = dot(stack(high, low), side(*halves(tail_v_ref[:, columns])))
        a = now_ref[:, columns] + (folded(wide[:WINDOW]) + wide[WINDOW:, :HD])
        a_ref[:, columns] = a
        square = square + a * a
    sums_ref[...] = row_sums(square)


def inverse_norm(total):
    return 1.0 / jnp.sqrt(total / (HEADS * HD) + EPS)


def added(refs):
    total = refs[0][...]
    for ref in refs[1:]:
        total = total + ref[...]
    return total


def scale_kernel(count, parts, _, *refs):
    sums, refs = refs[:parts], refs[parts:]
    a_refs, b_refs, (out_hbm, out_ref, sems) = refs[:count], refs[count : 2 * count], refs[2 * count :]
    inverse = inverse_norm(added(sums)).T
    copies = []
    for n in range(out_ref.shape[0] // WINDOW):
        held = slice(n * WINDOW, (n + 1) * WINDOW)
        rows = slice((n + 1) * WINDOW, (n + 2) * WINDOW)
        inverse_a, inverse_b = inverse[rows, 0:1], inverse[rows, 1:2]
        begin = 0
        for a_ref, b_ref in zip(a_refs, b_refs):
            columns = slice(begin, begin + a_ref.shape[1])
            out_ref[held, columns] = a_ref[rows, :] * inverse_a + b_ref[rows, :] * inverse_b
            begin = columns.stop
        copy = pltpu.make_async_copy(out_ref.at[held, :], out_hbm.at[rows, :], sems.at[n])
        copy.start()
        copies.append(copy)
    for copy in copies:
        copy.wait()


def first_scale_kernel(count, parts, a_ref, _, *refs):
    b_refs, refs = refs[:count], refs[count:]
    sums, first_sums, (out_hbm, out_ref, sems) = refs[:parts], refs[parts : 2 * parts], refs[2 * parts :]
    inverse_a = inverse_norm(added(first_sums)).T[:, 0:1]
    inverse_b = inverse_norm(added(sums)[:, :WINDOW]).T[:, 1:2]
    copies = []
    for n in range(sems.shape[0]):
        rows = slice(n * WINDOW // sems.shape[0], (n + 1) * WINDOW // sems.shape[0])
        begin = 0
        for b_ref in b_refs:
            columns = slice(begin, begin + b_ref.shape[1])
            out_ref[rows, columns] = a_ref[rows, columns] * inverse_a[rows] + b_ref[rows, :] * inverse_b[rows]
            begin = columns.stop
        copy = pltpu.make_async_copy(out_ref.at[rows, :], out_hbm.at[rows, :], sems.at[n])
        copy.start()
        copies.append(copy)
    for copy in copies:
        copy.wait()


def swap(block, axis, bit):
    return lax.ppermute(block, axis, [(i, i ^ bit) for i in range(lax.axis_size(axis))])


def everyone(block, axis):
    return [block] + [swap(block, axis, bits) for bits in range(1, lax.axis_size(axis))]


def first_phase(chip):
    return lax.ppermute(chip, "ctx", [(i, i ^ (2 if i % 2 == 0 else 4)) for i in range(8)])


def second_phase(message):
    return lax.ppermute(message, "ctx", [(i, i ^ (4 if i % 2 == 0 else 2)) for i in range(8)])


def doubled_prefix(chip):
    index = lax.axis_index("ctx")
    earlier = jnp.zeros_like(chip)
    running = chip
    bit = 2
    while bit < lax.axis_size("ctx"):
        partner = swap(running, "ctx", bit)
        earlier = earlier + jnp.where((index & bit) != 0, partner, 0.0)
        running = running + partner
        bit *= 2
    return earlier


def shards(queries, keys, values, head_gain):
    rows, width = queries.shape
    heads = head_gain.shape[1]
    queries, keys, values = (
        pltpu.with_memory_space_constraint(x, pltpu.HBM) for x in (queries, keys, values)
    )
    smem = pl.BlockSpec(memory_space=pltpu.SMEM)
    anywhere = pl.BlockSpec(memory_space=pl.ANY)
    vmem = pl.BlockSpec()

    def array(*shape, dtype=F32):
        return jax.ShapeDtypeStruct(shape, dtype)

    def call(kernel, name, **kwargs):
        return pl.pallas_call(
            kernel,
            name=name,
            compiler_params=pltpu.CompilerParams(vmem_limit_bytes=VMEM_BYTES),
            cost_estimate=pl.CostEstimate(flops=0, bytes_accessed=0, transcendentals=0),
            **kwargs,
        )

    packed = array(heads // 2, HD, HD)
    first_tile = array(WINDOW, width)
    dma = pltpu.SemaphoreType.DMA
    keep, send, half, held_k, held_v, tail_k, tail_v = call(
        totals_kernel,
        "totals",
        in_specs=[anywhere, anywhere],
        out_shape=[
            packed,
            packed,
            array(heads, HD, HD),
            array(rows, width),
            array(rows, width),
            first_tile,
            first_tile,
        ],
        scratch_shapes=[dma((2, heads // GROUP))],
    )(keys, values)
    beside = swap(send, "ctx", 1)
    held_q = call(
        load_kernel,
        "load",
        in_specs=[anywhere, anywhere],
        out_shape=array(rows, width),
        scratch_shapes=[dma((4,))],
    )(queries, send)
    chip, tail_k = call(
        chip_kernel,
        "chip",
        in_specs=[vmem, vmem, anywhere, anywhere],
        out_specs=[vmem, anywhere],
        out_shape=[packed, first_tile],
        input_output_aliases={3: 1},
    )(keep, beside, held_q, tail_k)
    route = [(i, i + 1) for i in range(lax.axis_size("ctx") - 1)]
    before_k = lax.ppermute(tail_k, "ctx", route)

    def local(begin, count, after):
        taken = count * HD
        after = [] if after is None else [after]
        return call(
            functools.partial(local_kernel, begin, len(after)),
            "local",
            in_specs=[smem, vmem, vmem, vmem] + [anywhere] * len(after),
            out_shape=[array(rows, taken), array(rows, taken), array(8, rows)],
            scratch_shapes=[pltpu.VMEM((rows, HD), F32)],
        )(head_gain, held_q, held_k, held_v, *after)

    def pass_on(array_now, after):
        return call(
            pass_kernel,
            "pass",
            in_specs=[anywhere, anywhere],
            out_specs=anywhere,
            out_shape=array(*array_now.shape),
            input_output_aliases={0: 0},
        )(array_now, after)

    begin = heads * 3 // 4 // GROUP * GROUP
    parts = [local(0, begin, None)]
    message = None
    if lax.axis_size("ctx") == 8:
        first = first_phase(chip)
        message = call(
            message_kernel,
            "message",
            in_specs=[vmem, vmem, anywhere],
            out_shape=packed,
        )(first, chip, parts[0][2])
    parts.append(local(begin, heads - begin, message))
    window, linear, window_sums = zip(*parts)
    before_v = lax.ppermute(pass_on(tail_v, window_sums[1]), "ctx", route)
    first_weights, first_now = call(
        first_weights_kernel,
        "first_weights",
        in_specs=[smem] + [vmem] * 4,
        out_shape=[array(WINDOW, 2 * width, dtype=BF16), first_tile],
    )(head_gain, held_q, held_k, held_v, before_k)

    if message is not None:
        second = second_phase(message)
        mine, other = call(
            prefix_kernel,
            "prefix",
            in_specs=[vmem] * 4 + [anywhere],
            out_shape=[packed, packed],
        )(first, second, keep, beside, first_now)
    else:
        earlier = doubled_prefix(chip)
        core = lax.axis_index("ctx") % 2
        mine = earlier + jnp.where(core == 1, beside, 0.0)
        other = earlier + jnp.where(core == 0, keep, 0.0)
    other = swap(other, "ctx", 1)

    *linear, sums = call(
        functools.partial(earlier_kernel, len(parts)),
        "earlier",
        in_specs=[smem] + [vmem] * (4 + 2 * len(parts)),
        out_shape=[array(*x.shape) for x in linear] + [array(8, rows)],
        scratch_shapes=[pltpu.VMEM((rows, HD), F32)],
    )(head_gain, half, mine, other, held_q, *linear, *window_sums)
    sums = everyone(sums, "head")
    first_a, first_sums = call(
        first_values_kernel,
        "first_values",
        in_specs=[vmem] * 3 + [anywhere],
        out_shape=[first_tile, array(8, WINDOW)],
    )(first_weights, first_now, before_v, sums[0])
    first_sums = everyone(first_sums, "head")
    out = call(
        functools.partial(scale_kernel, len(parts), len(sums)),
        "scale",
        in_specs=[anywhere] + [vmem] * (2 * len(parts) + len(sums)),
        out_specs=anywhere,
        out_shape=array(rows, width),
        scratch_shapes=[pltpu.VMEM((rows - WINDOW, width), F32), dma((rows // WINDOW - 1,))],
    )(first_sums[0], *sums, *window, *linear)
    return call(
        functools.partial(first_scale_kernel, len(parts), len(sums)),
        "first_scale",
        in_specs=[vmem, anywhere] + [vmem] * (len(parts) + 2 * len(sums)),
        out_specs=anywhere,
        out_shape=array(rows, width),
        scratch_shapes=[pltpu.VMEM((WINDOW, width), F32), dma((4,))],
        input_output_aliases={1: 0},
    )(first_a, out, *linear, *sums, *first_sums)


def solution(mesh):
    in_specs = (P("ctx", "head"), P("ctx", "head"), P("ctx", "head"), P(None, "head"))
    out_specs = P("ctx", "head")
    return jax.shard_map(shards, mesh=mesh, in_specs=in_specs, out_specs=out_specs, check_vma=False)
```
